32 devices in a mesh: wide: 8 (over z, x), narrow: 4 (over y, core).
Axes of the slice: x: 2, y: 2, z: 4, core: 2. Of those that a mesh axis runs over, the one named last changes fastest.
Arguments:
- tokens: bfloat16 [2, 12288, 960], P(None, ('wide', 'narrow')), may hold values from -6 to 6
- lengths: int32 [2, 32, 8], P(None, ('wide', 'narrow')), may hold values from 0 to 384, as said below
- cotangent: bfloat16 [2, 12288, 960], P(None, ('wide', 'narrow')), may hold values from -6 to 6
- query_weight: bfloat16 [960, 960], P('wide', 'narrow'), may hold values from -0.25 to 0.25
- key_matrix: bfloat16 [960, 320], P('wide', 'narrow'), may hold values from -0.25 to 0.25
- value_matrix: bfloat16 [960, 320], P('wide', 'narrow'), may hold values from -0.1875 to 0.1875
- output_weight: bfloat16 [960, 960], P('wide', 'narrow'), may hold values from -0.5 to 0.5
- gate_weight: bfloat16 [960, 2560], P('narrow', 'wide'), may hold values from -0.1875 to 0.1875
- up_weight: bfloat16 [960, 2560], P('narrow', 'wide'), may hold values from -0.1875 to 0.1875
- down_weight: bfloat16 [2560, 960], P('wide', 'narrow'), may hold values from -0.25 to 0.25
- attention_gain: bfloat16 [960], P('narrow'), may hold values from 0.25 to 1.75
- feedforward_gain: bfloat16 [960], P('narrow'), may hold values from 0.25 to 1.75
Outputs:
- mixed: bfloat16 [2, 12288, 960], P(None, ('wide', 'narrow'))
- tokens_grad: bfloat16 [2, 12288, 960], P(None, ('wide', 'narrow'))
- query_grad: float32 [960, 960], P('wide', 'narrow')
- key_grad: float32 [960, 320], P('wide', 'narrow')
- value_grad: float32 [960, 320], P('wide', 'narrow')
- output_grad: float32 [960, 960], P('wide', 'narrow')
- gate_grad: float32 [960, 2560], P('narrow', 'wide')
- up_grad: float32 [960, 2560], P('narrow', 'wide')
- down_grad: float32 [2560, 960], P('wide', 'narrow')
- attention_gain_grad: float32 [960], P('narrow')
- feedforward_gain_grad: float32 [960], P('narrow')
The draws below stay inside these ranges and needn't reach their ends.
Inputs may be any that keep to these rules, and one draw needn't show every extreme that they name: lengths[m, b] lists, in order, the documents packed into bucket b of micro-batch m; a bucket's lengths sum to at most 384, the rest of its rows are padding, zeros are empty slots, and in every draw some bucket holds a single document of 384 rows.
All inputs are finite; a program needn't handle non-finite values.
Results may differ from the reference program's by a relative error of at most 0.02.
Values may be sent and summed in bfloat16 or wider, within the bound.
No kernel may reach another device: no remote copies, remote signals or barrier semaphores. Data moves between devices by JAX's collectives and lax.ppermute only.
A program may use at most 256 MiB of HBM per device.

```python
import jax
import jax.numpy as jnp
from jax import lax

MODEL_WIDTH = 960
QUERY_HEADS = 15
KEY_VALUE_HEADS = 5
HEAD_WIDTH = 64
FF = 2560
ROWS = 384
MB = 2
SLOTS = 8
BUCKETS = 32
TOKENS = 12288


def draw_lengths(key, part):
    key = jax.random.fold_in(key, 17)
    cut_key, pad_key, count_key, pick_key = jax.random.split(key, 4)
    bucket_total = MB * BUCKETS
    cuts = jax.random.randint(cut_key, (bucket_total, SLOTS - 1), 1, ROWS)
    padding = jax.random.randint(pad_key, (bucket_total, 1), 0, ROWS // 4 + 1)
    filled = ROWS - padding
    active = jnp.left_shift(1, jax.random.randint(count_key, (bucket_total, 1), 0, 4)) - 1
    slot_ids = jnp.arange(SLOTS - 1)
    cuts = jnp.where(slot_ids[None, :] < active, jnp.minimum(cuts, filled), filled)
    cuts = jnp.sort(cuts, axis=1)
    bounds = jnp.concatenate([jnp.zeros((bucket_total, 1), jnp.int32), cuts, filled], axis=1)
    doc_lengths = bounds[:, 1:] - bounds[:, :-1]
    chosen = jax.random.randint(pick_key, (), 0, bucket_total)
    single = jnp.zeros((SLOTS,), jnp.int32).at[0].set(ROWS)
    bucket_ids = jnp.arange(bucket_total)
    doc_lengths = jnp.where((bucket_ids == chosen)[:, None], single[None, :], doc_lengths)
    return doc_lengths.reshape(MB, BUCKETS, SLOTS).astype(jnp.int32)


def levels(own_key, extent, cuts, smallest, largest):
    gain, own = 1.0, jax.random.fold_in(own_key, 6)
    for axis_at, shards_of in cuts:
        heights = jnp.exp(jax.random.uniform(jax.random.fold_in(own, axis_at), (shards_of,), jnp.float32, smallest / len(cuts), largest / len(cuts)))
        gain = gain * jnp.repeat(heights, extent[axis_at] // shards_of).reshape([-1 if axis == axis_at else 1 for axis in range(len(extent))])
    return gain


def noise(stream_key, extent, deviation, reach, shards=(), held_as=jnp.bfloat16):
    array = jax.random.normal(stream_key, extent, jnp.float32) * deviation
    if len(shards) > 0:
        array = levels(stream_key, extent, shards, -0.22, 0.18) * array
    return jnp.clip(array, min=-reach, max=reach).astype(held_as)


def setup_inputs(seed: int = 0) -> dict:
    splits = jax.random.split(jax.random.key(seed), 13)
    return {
        "tokens": noise(splits[0], (MB, TOKENS, MODEL_WIDTH), 1.0, 6.0, ((1, 32),)),
        "lengths": draw_lengths(jax.random.fold_in(splits[12], 71), 0),
        "cotangent": noise(splits[2], (MB, TOKENS, MODEL_WIDTH), 1.0, 6.0, ((1, 32),)),
        "query_weight": noise(splits[3], (MODEL_WIDTH, MODEL_WIDTH), (MODEL_WIDTH // 2) ** -0.5, 0.25, ((0, 8), (1, 4))),
        "key_matrix": noise(splits[4], (MODEL_WIDTH, KEY_VALUE_HEADS * HEAD_WIDTH), (MODEL_WIDTH // 2) ** -0.5, 0.25, ((0, 8), (1, 4))),
        "value_matrix": noise(splits[5], (MODEL_WIDTH, KEY_VALUE_HEADS * HEAD_WIDTH), MODEL_WIDTH ** -0.5, 0.1875, ((0, 8), (1, 4))),
        "output_weight": noise(splits[6], (MODEL_WIDTH, MODEL_WIDTH), (MODEL_WIDTH // 8) ** -0.5, 0.5, ((0, 8), (1, 4))),
        "gate_weight": noise(splits[7], (MODEL_WIDTH, FF), MODEL_WIDTH ** -0.5, 0.1875, ((0, 4), (1, 8))),
        "up_weight": noise(splits[8], (MODEL_WIDTH, FF), MODEL_WIDTH ** -0.5, 0.1875, ((0, 4), (1, 8))),
        "down_weight": noise(splits[9], (FF, MODEL_WIDTH), (FF // 4) ** -0.5, 0.25, ((0, 8), (1, 4))),
        "attention_gain": jnp.clip(1.0 + 0.15 * jax.random.normal(splits[10], (MODEL_WIDTH,), jnp.float32), 0.25, 1.75).astype(jnp.bfloat16),
        "feedforward_gain": jnp.clip(1.0 + 0.15 * jax.random.normal(splits[11], (MODEL_WIDTH,), jnp.float32), 0.25, 1.75).astype(jnp.bfloat16),
    }


@jax.custom_vjp
def low(v):
    return lax.optimization_barrier(v.astype(jnp.bfloat16)).astype(jnp.float32)

@jax.custom_vjp
def low_back(v):
    return v

def low_keep(v):
    return (low(v), None)

def low_pass(kept, grad):
    return (grad,)

def back_keep(v):
    return (v, None)

def back_low(kept, grad):
    return (low(grad),)
low.defvjp(low_keep, low_pass)
low_back.defvjp(back_keep, back_low)
EPS = 1e-05
THETA = 10000.0

def segments_of(lengths_row, count_of_rows):
    ends = jnp.cumsum(lengths_row, dtype=jnp.int32)
    starts = ends - lengths_row
    places = jnp.arange(count_of_rows, dtype=jnp.int32)
    segment = lax.optimization_barrier(jnp.sum((places[:, None] >= ends[None, :]).astype(jnp.int32), axis=1, dtype=jnp.int32))
    slot_ids = jnp.arange(lengths_row.shape[0], dtype=jnp.int32)
    opening = lax.optimization_barrier(jnp.sum(jnp.where(segment[:, None] == slot_ids[None, :], starts[None, :], 0), axis=1, dtype=jnp.int32))
    opening = jnp.where(segment == lengths_row.shape[0], ends[-1], opening)
    return (segment, places - opening)

def rotation_tables(position, head_size):
    half = head_size // 2
    freqs = THETA ** (-jnp.arange(half, dtype=jnp.float32) * 2.0 / head_size)
    angles = position.astype(jnp.float32)[:, None] * freqs[None, :]
    return (jnp.cos(angles)[:, None, :], jnp.sin(angles)[:, None, :])

def rotate(field, cosine_table, sine_table, head_size):
    count_of_rows = field.shape[0]
    pieces = field.reshape(count_of_rows, -1, head_size)
    half = head_size // 2
    left_half = pieces[..., :half]
    right_half = pieces[..., half:]
    turned = jnp.concatenate([left_half * cosine_table - right_half * sine_table, right_half * cosine_table + left_half * sine_table], axis=-1)
    return turned.reshape(count_of_rows, -1)

def bucket_layer(params, token_rows, lengths_row):
    query_weight, key_matrix, value_matrix, output_weight, gate_weight, up_weight, down_weight, attention_gain, feedforward_gain = params
    count_of_rows = token_rows.shape[0]
    highest = lax.Precision.HIGHEST
    segment, position = segments_of(lengths_row, count_of_rows)
    valid_rows = (segment < lengths_row.shape[0]).astype(jnp.float32)[:, None]
    row_order = jnp.arange(count_of_rows, dtype=jnp.int32)
    allowed = (segment[:, None] == segment[None, :]) & (row_order[None, :] <= row_order[:, None])
    cosine_table, sine_table = rotation_tables(position, HEAD_WIDTH)
    attention_scale = lax.rsqrt(lax.optimization_barrier(jnp.mean(token_rows * token_rows, axis=1, keepdims=True)) + EPS)
    attention_in = low(token_rows * attention_scale * attention_gain)
    query_value = low_back(jnp.dot(attention_in, query_weight, precision=highest))
    key_value = low_back(jnp.dot(attention_in, key_matrix, precision=highest))
    projected_values = low(low_back(jnp.dot(attention_in, value_matrix, precision=highest)))
    rotated_queries = low(rotate(query_value, cosine_table, sine_table, HEAD_WIDTH))
    rotated_keys = low(rotate(key_value, cosine_table, sine_table, HEAD_WIDTH))
    heads_per_group = QUERY_HEADS // KEY_VALUE_HEADS
    query_head_rows = rotated_queries.reshape(count_of_rows, KEY_VALUE_HEADS, heads_per_group, HEAD_WIDTH)
    key_head_rows = rotated_keys.reshape(count_of_rows, KEY_VALUE_HEADS, HEAD_WIDTH)
    value_head_rows = projected_values.reshape(count_of_rows, KEY_VALUE_HEADS, HEAD_WIDTH)
    logits = low_back(HEAD_WIDTH ** (-0.5) * jnp.einsum('qgcd,kgd->gcqk', query_head_rows, key_head_rows, precision=highest))
    logits = jnp.where(allowed[None, None], logits, -1000000000.0)
    soft_probs = low(jax.nn.softmax(logits, axis=-1))
    attended = jnp.einsum('gcqk,kgd->qgcd', soft_probs, value_head_rows, precision=highest).reshape(count_of_rows, QUERY_HEADS * HEAD_WIDTH)
    attended = low(low_back(attended))
    residual = token_rows + low_back(jnp.dot(attended, output_weight, precision=highest))
    feed_scale = lax.rsqrt(lax.optimization_barrier(jnp.mean(residual * residual, axis=1, keepdims=True)) + EPS)
    feed_in = low(residual * feed_scale * feedforward_gain)
    gate_value = low_back(jnp.dot(feed_in, gate_weight, precision=highest))
    up_value = low_back(jnp.dot(feed_in, up_weight, precision=highest))
    hidden = low(jax.nn.silu(gate_value) * up_value)
    return valid_rows * (residual + low_back(jnp.dot(hidden, down_weight, precision=highest)))

def reference(tokens, lengths, cotangent, query_weight, key_matrix, value_matrix, output_weight, gate_weight, up_weight, down_weight, attention_gain, feedforward_gain):
    params = tuple((weight_item.astype(jnp.float32) for weight_item in (query_weight, key_matrix, value_matrix, output_weight, gate_weight, up_weight, down_weight, attention_gain, feedforward_gain)))
    bucket_count = MB * BUCKETS
    token_blocks = tokens.astype(jnp.float32).reshape(bucket_count, ROWS, MODEL_WIDTH)
    length_blocks = lengths.reshape(bucket_count, SLOTS)

    def forward(params_in, blocks_in):

        def one_bucket(item):
            return bucket_layer(params_in, item[0], item[1])
        return lax.map(jax.checkpoint(one_bucket), (blocks_in, length_blocks))
    mixed, pullback = jax.vjp(forward, params, token_blocks)
    param_grads, token_grads = pullback(cotangent.astype(jnp.float32).reshape(bucket_count, ROWS, MODEL_WIDTH))
    return (mixed.reshape(MB, TOKENS, MODEL_WIDTH).astype(jnp.bfloat16), token_grads.reshape(MB, TOKENS, MODEL_WIDTH).astype(jnp.bfloat16), param_grads[0], param_grads[1], param_grads[2], param_grads[3], param_grads[4], param_grads[5], param_grads[6], param_grads[7], param_grads[8])
```

```python
import functools

import jax
import jax.numpy as jnp
from jax import lax
from jax.experimental import pallas as pl
from jax.experimental.pallas import tpu as pltpu
from jax.sharding import PartitionSpec as P

QUERY_HEADS = 15
KEY_VALUE_HEADS = 5
HEAD_WIDTH = 64


EPS = 1e-05
THETA = 10000.0


def segments_of(lengths_row, count_of_rows):
    ends = jnp.cumsum(lengths_row, dtype=jnp.int32)
    starts = ends - lengths_row
    places = jnp.arange(count_of_rows, dtype=jnp.int32)
    segment = jnp.sum((places[:, None] >= ends[None, :]).astype(jnp.int32), axis=1, dtype=jnp.int32)
    slot_ids = jnp.arange(lengths_row.shape[0], dtype=jnp.int32)
    opening = jnp.sum(
        jnp.where(segment[:, None] == slot_ids[None, :], starts[None, :], 0),
        axis=1,
        dtype=jnp.int32,
    )
    opening = jnp.where(segment == lengths_row.shape[0], ends[-1], opening)
    return (segment, places - opening)


def rotation_tables(position, head_size):
    half = head_size // 2
    freqs = THETA ** (-jnp.arange(half, dtype=jnp.float32) * 2.0 / head_size)
    angles = position.astype(jnp.float32)[:, None] * freqs[None, :]
    return (jnp.cos(angles)[:, None, :], jnp.sin(angles)[:, None, :])


def rotate(field, cosine_table, sine_table, head_size, inverse):
    count_of_rows = field.shape[0]
    pieces = field.reshape(count_of_rows, -1, head_size)
    half = head_size // 2
    left_half = pieces[..., :half]
    right_half = pieces[..., half:]
    sine_used = -sine_table if inverse else sine_table
    turned = jnp.concatenate(
        [
            left_half * cosine_table - right_half * sine_used,
            right_half * cosine_table + left_half * sine_used,
        ],
        axis=-1,
    )
    return turned.reshape(count_of_rows, -1)


def rms_scale(field):
    return lax.rsqrt(jnp.mean(field * field, axis=1, keepdims=True) + EPS)


def rms_back(field, scale, gain, upstream):
    normed = field * scale
    gain_grad = jnp.sum(upstream * normed, axis=0)
    normed_grad = upstream * gain
    field_grad = scale * (
        normed_grad - normed * jnp.mean(normed_grad * normed, axis=1, keepdims=True)
    )
    return (field_grad, gain_grad)


def head_block(matrix, member, width):
    return matrix[:, member * width : (member + 1) * width]


def masked_logits(queries, key_block, allowed, head_size):
    logits = jnp.einsum(
        "qcd,kd->cqk", queries, key_block, preferred_element_type=jnp.float32
    ) * head_size ** (-0.5)
    return jnp.where(allowed[None], logits, -1000000000.0)


def attention_forward(
    rotated_queries, rotated_keys, projected_values, allowed, head_size, heads_per_group
):
    count_of_rows = rotated_queries.shape[0]
    outputs = []
    log_sums = []
    for member in range(rotated_keys.shape[1] // head_size):
        queries = head_block(rotated_queries, member, heads_per_group * head_size).reshape(
            count_of_rows, heads_per_group, head_size
        )
        key_block = head_block(rotated_keys, member, head_size)
        value_block = head_block(projected_values, member, head_size)
        logits = masked_logits(queries, key_block, allowed, head_size)
        row_peak = jnp.max(logits, axis=-1, keepdims=True)
        shifted = jnp.exp(logits - row_peak)
        denominator = jnp.sum(shifted, axis=-1, keepdims=True)
        soft_probs = (shifted / denominator).astype(jnp.bfloat16)
        attended = jnp.einsum(
            "cqk,kd->qcd", soft_probs, value_block, preferred_element_type=jnp.float32
        )
        outputs.append(attended.reshape(count_of_rows, heads_per_group * head_size))
        log_sums.append(row_peak + jnp.log(denominator))
    return (jnp.concatenate(outputs, axis=1), log_sums)


def attention_backward(
    rotated_queries,
    rotated_keys,
    projected_values,
    allowed,
    log_sums,
    attended_grad,
    head_size,
    heads_per_group,
):
    count_of_rows = rotated_queries.shape[0]
    factor = head_size ** (-0.5)
    query_parts, key_parts, value_parts = ([], [], [])
    for member in range(len(log_sums)):
        queries = head_block(rotated_queries, member, heads_per_group * head_size).reshape(
            count_of_rows, heads_per_group, head_size
        )
        key_block = head_block(rotated_keys, member, head_size)
        value_block = head_block(projected_values, member, head_size)
        head_grads = head_block(attended_grad, member, heads_per_group * head_size).reshape(
            count_of_rows, heads_per_group, head_size
        )
        soft_probs = jnp.exp(
            masked_logits(queries, key_block, allowed, head_size) - log_sums[member]
        )
        prob_grad = jnp.einsum(
            "qcd,kd->cqk", head_grads, value_block, preferred_element_type=jnp.float32
        )
        logit_grad = (
            soft_probs * (prob_grad - jnp.sum(soft_probs * prob_grad, axis=-1, keepdims=True))
        ).astype(jnp.bfloat16)
        query_part = (
            jnp.einsum("cqk,kd->qcd", logit_grad, key_block, preferred_element_type=jnp.float32)
            * factor
        )
        query_parts.append(query_part.reshape(count_of_rows, heads_per_group * head_size))
        key_parts.append(
            jnp.einsum("cqk,qcd->kd", logit_grad, queries, preferred_element_type=jnp.float32)
            * factor
        )
        value_parts.append(
            jnp.einsum(
                "cqk,qcd->kd",
                soft_probs.astype(jnp.bfloat16),
                head_grads,
                preferred_element_type=jnp.float32,
            )
        )
    return (
        jnp.concatenate(query_parts, axis=1),
        jnp.concatenate(key_parts, axis=1),
        jnp.concatenate(value_parts, axis=1),
    )


F32=jnp.float32; BF=jnp.bfloat16
NT=(((1,),(1,)),((),()))
TN=(((0,),(0,)),((),()))
NN=(((1,),(0,)),((),()))
def dot(a,b,dn): return lax.dot_general(a,b,dn,preferred_element_type=F32)

def ffn_kernel(tile, bf_ref, gf_ref, own_ref, other_ref, own_grad, other_grad, mix_ref, gbf_ref, mix_acc, gbf_acc):
    step = pl.program_id(0)
    pair, wide, _, sub, lanes = own_ref.shape

    def weight(kind):
        parts = [
            ref[at, :, kind].reshape(tile, lanes) for ref in (own_ref, other_ref) for at in range(pair)
        ]
        return jnp.concatenate(parts, axis=1)

    gate, up, down = weight(0), weight(1), weight(2)
    rows_in = bf_ref[...]
    grad_in = gf_ref[...]
    gate_value = dot(rows_in, gate, NT)
    up_value = dot(rows_in, up, NT)
    hidden_grad = dot(grad_in, down, NT)
    sigmoid_gate = 1.0 / (1.0 + jnp.exp(-gate_value))
    silu = gate_value * sigmoid_gate
    hidden = (silu * up_value).astype(BF)
    gate_part = (hidden_grad * up_value * (sigmoid_gate * (1.0 + gate_value * (1.0 - sigmoid_gate)))).astype(BF)
    up_part = (hidden_grad * silu).astype(BF)
    mix = dot(hidden, down, NN)
    back = dot(gate_part, gate, NN) + dot(up_part, up, NN)

    @pl.when(step == 0)
    def _():
        mix_acc[...] = mix
        gbf_acc[...] = back

    @pl.when(step > 0)
    def _():
        mix_acc[...] += mix
        gbf_acc[...] += back

    for kind, (left, right) in enumerate(((gate_part, rows_in), (up_part, rows_in), (hidden, grad_in))):
        term = dot(left, right, TN).astype(BF)
        for index in range(2 * pair):
            ref = (own_grad, other_grad)[index // pair]
            ref[index % pair, :, kind] = term[:, index * lanes : (index + 1) * lanes].reshape(wide, sub, lanes)

    @pl.when(step == pl.num_programs(0) - 1)
    def _():
        mix_ref[...] = mix_acc[...]
        gbf_ref[...] = gbf_acc[...]


def ffn_call(rows_in, grad_in, own, other):
    pair, wide, _, units, lanes = own.shape
    rows, width = rows_in.shape
    tile = 256
    sub = tile // wide
    steps = units // sub
    weight_spec = pl.BlockSpec((pair, wide, 3, sub, lanes), lambda t: (0, 0, 0, t, 0))
    whole = pl.BlockSpec((rows, width), lambda t: (0, 0))
    own_terms, other_terms, mix, back = pl.pallas_call(
        functools.partial(ffn_kernel, tile),
        grid=(steps,),
        in_specs=[whole, whole, weight_spec, weight_spec],
        out_specs=[weight_spec, weight_spec, whole, whole],
        out_shape=[jax.ShapeDtypeStruct(own.shape, BF)] * 2 + [jax.ShapeDtypeStruct((rows, width), F32)] * 2,
        scratch_shapes=[pltpu.VMEM((rows, width), F32)] * 2,
        compiler_params=pltpu.CompilerParams(vmem_limit_bytes=56 * 1024 * 1024),
        cost_estimate=pl.CostEstimate(
            flops=18 * rows * width * units * wide,
            bytes_accessed=rows * width * 12 + 4 * own.size * 2,
            transcendentals=rows * units * wide,
        ),
        name="feed_forward",
    )(rows_in, grad_in, own, other)
    return mix, back, own_terms, other_terms


AXES = ("wide", "narrow")


class Grid:
    def __init__(self):
        self.wide = lax.axis_size("wide")
        self.narrow = lax.axis_size("narrow")
        self.outer = 4
        self.inner = self.wide // 4
        self.pair = self.narrow // 2
        self.size = {"outer": 4, "inner": self.inner, "pair": self.pair, "core": 2}
        self.stride = {"outer": self.inner * self.narrow, "inner": self.narrow, "pair": 2, "core": 1}
        linear = lax.axis_index("wide") * self.narrow + lax.axis_index("narrow")
        self.at = {name: (linear // self.stride[name]) % self.size[name] for name in self.size}

    def shift(self, value, name):
        size, stride = self.size[name], self.stride[name]
        pairs = []
        for source in range(self.wide * self.narrow):
            digit = (source // stride) % size
            pairs.append((source, source + ((digit + 1) % size - digit) * stride))
        return lax.ppermute(value, AXES, pairs)

    def gather(self, block, name):
        blocks = [block]
        for _ in range(self.size[name] - 1):
            blocks.append(self.shift(blocks[-1], name))
        return blocks

    def in_order(self, blocks, name):
        size = self.size[name]
        doubled = jnp.stack(blocks[::-1] + blocks[:0:-1])
        return lax.dynamic_slice_in_dim(doubled, size - 1 - self.at[name], size, 0)

    def scatter(self, pick, name):
        size = self.size[name]
        total = pick(1)
        for step in range(1, size):
            total = self.shift(total, name) + pick((step + 1) % size)
        return total

    def behind(self, name, steps):
        return (self.at[name] + (self.size[name] - steps)) % self.size[name]


def chosen(array, index):
    return lax.dynamic_index_in_dim(array, index, 0, keepdims=False)


def gather_chunk(grid, shard, cut):
    ring = grid.gather(shard, "outer")
    first = jnp.stack([part[:, :cut] for part in ring])
    second = jnp.stack([part[:, cut:] for part in ring])
    first_wide = jnp.concatenate(grid.gather(first, "inner"))
    second_pair = jnp.stack(grid.gather(second, "pair"))
    first_all = jnp.stack(grid.gather(first_wide, "pair"))
    second_all = jnp.concatenate(grid.gather(second_pair, "inner"), axis=1)
    own = jnp.concatenate([first_all, second_all], axis=3)
    return own, grid.shift(own, "core")


def scatter_chunk(grid, own, other, cut):
    outer = grid.outer
    both = grid.shift(other, "core") + own
    first = grid.scatter(lambda r: both[r, :, :, :cut], "pair")
    first = grid.scatter(lambda r: first[r * outer : (r + 1) * outer], "inner")
    second_wide = grid.scatter(lambda r: both[:, r * outer : (r + 1) * outer, :, cut:], "inner")
    second = grid.scatter(lambda r: second_wide[r], "pair")
    merged = jnp.concatenate([first, second], axis=2)
    return grid.scatter(lambda r: merged[r], "outer")


def gather_attention(grid, shard):
    cut = shard.shape[0] // 2
    ring = grid.in_order(grid.gather(shard, "outer"), "outer")
    first = grid.in_order(grid.gather(ring[:, :cut], "inner"), "inner")
    second = grid.in_order(grid.gather(ring[:, cut:], "pair"), "pair")
    first = grid.in_order(grid.gather(first, "pair"), "pair")
    second = grid.in_order(grid.gather(second, "inner"), "inner")
    own = jnp.concatenate([first, jnp.swapaxes(second, 0, 1)], axis=3)
    return grid.in_order(grid.gather(own, "core"), "core")


def scatter_attention(grid, terms):
    cut = terms.shape[4] // 2
    both = grid.scatter(lambda r: chosen(terms, grid.behind("core", r)), "core")
    first_terms = both[:, :, :, :cut]
    first_inner = grid.scatter(lambda r: chosen(first_terms, grid.behind("pair", r)), "pair")
    first = grid.scatter(lambda r: chosen(first_inner, grid.behind("inner", r)), "inner")
    second_terms = jnp.swapaxes(both[:, :, :, cut:], 0, 1)
    second_pair = grid.scatter(lambda r: chosen(second_terms, grid.behind("inner", r)), "inner")
    second = grid.scatter(lambda r: chosen(second_pair, grid.behind("pair", r)), "pair")
    merged = jnp.concatenate([first, second], axis=1)
    return grid.scatter(lambda r: chosen(merged, grid.behind("outer", r)), "outer")


def rounded_up(count, step):
    return -(-count // step) * step


def body(
    tokens,
    lengths,
    cotangent,
    query_weight,
    key_matrix,
    value_matrix,
    output_weight,
    gate_weight,
    up_weight,
    down_weight,
    attention_gain,
    feedforward_gain,
):
    grid = Grid()
    head_size = HEAD_WIDTH
    heads_per_group = QUERY_HEADS // KEY_VALUE_HEADS
    batches, bucket_rows, width = tokens.shape
    rows = batches * bucket_rows
    wide, narrow, pair = grid.wide, grid.narrow, grid.pair
    d_w, d_n = query_weight.shape
    kv_n = key_matrix.shape[1]
    f_w = down_weight.shape[0]
    d_pad = rounded_up(d_n, 128)
    a_rows = rounded_up(d_w + 2, 32)

    packed = jnp.concatenate([query_weight, output_weight, key_matrix, value_matrix], axis=1)
    lanes = packed.shape[1]
    gains = jnp.concatenate([attention_gain, feedforward_gain, jnp.zeros((2 * kv_n,), BF)])
    a_shard = jnp.concatenate([packed, jnp.zeros((a_rows - d_w, lanes), BF).at[0].set(gains)], axis=0)
    f_shard = jnp.pad(
        jnp.stack([gate_weight.T, up_weight.T, down_weight]), ((0, 0), (0, 0), (0, d_pad - d_n))
    )
    sub = 256 // wide
    half = f_w // 2
    cut = (half // sub + 1) // 2 * sub

    a_all = gather_attention(grid, a_shard)
    chunks = [gather_chunk(grid, f_shard[:, i * half : (i + 1) * half], cut) for i in range(2)]

    def natural(lo, count):
        block = a_all[:, :, :, :, :d_w, lo : lo + count]
        return block.transpose(3, 2, 4, 1, 0, 5).reshape(wide * d_w, narrow * count)

    query_full = natural(0, d_n)
    key_full = natural(2 * d_n, kv_n)
    value_full = natural(2 * d_n + kv_n, kv_n)
    order = [
        (grid.behind("core", dc), grid.behind("pair", dy)) for dc in range(2) for dy in range(pair)
    ]
    by_narrow = a_all.reshape(2 * pair, *a_all.shape[2:])
    relative = [c_at * pair + y_at for c_at, y_at in order]

    def padded(block):
        return jnp.pad(block, ((0, 0), (0, d_pad - d_n)))

    output_parts = []
    gain_first_parts = []
    gain_second_parts = []
    for index in range(narrow):
        gain_first_parts.append(by_narrow[(index % 2) * pair + index // 2, 0, 0, d_w, :d_n])
    for index in relative:
        block = chosen(by_narrow, index)
        output_parts.append(
            padded(
                block[:, :, :d_w, d_n : 2 * d_n].transpose(1, 0, 2, 3).reshape(wide * d_w, d_n)
            )
        )
        gain_second_parts.append(jnp.pad(block[0, 0, d_w, d_n : 2 * d_n], (0, d_pad - d_n)))
    output_full = jnp.concatenate(output_parts, axis=1)
    gain_first = jnp.concatenate(gain_first_parts).astype(F32)
    gain_second = jnp.concatenate(gain_second_parts).astype(F32)

    def to_relative(field):
        stacked = jnp.stack([padded(field[:, i * d_n : (i + 1) * d_n]) for i in range(narrow)])
        return jnp.concatenate([chosen(stacked, y_at * 2 + c_at) for c_at, y_at in order], axis=1)

    def to_natural(field):
        stacked = jnp.stack([field[:, i * d_pad : i * d_pad + d_n] for i in range(narrow)])
        blocks = []
        for index in range(narrow):
            dc = (grid.at["core"] + index % 2) % 2
            dy = (grid.at["pair"] - index // 2 + pair) % pair
            blocks.append(chosen(stacked, dc * pair + dy))
        return jnp.concatenate(blocks, axis=1)

    token_low = tokens.reshape(rows, width)
    token_rows = token_low.astype(F32)
    token_relative = to_relative(token_low).astype(F32)
    tables = [segments_of(lengths[m, 0], bucket_rows) for m in range(batches)]
    row_order = jnp.arange(bucket_rows, dtype=jnp.int32)
    allowed = [
        (segment[:, None] == segment[None, :]) & (row_order[None, :] <= row_order[:, None])
        for segment, _ in tables
    ]
    valid_rows = jnp.concatenate(
        [(segment < lengths.shape[2]).astype(F32)[:, None] for segment, _ in tables]
    )
    cosine_table, sine_table = rotation_tables(
        jnp.concatenate([position for _, position in tables]), head_size
    )
    attention_scale = rms_scale(token_rows)
    attention_in = (token_rows * attention_scale * gain_first).astype(BF)
    query_value = jnp.dot(attention_in, query_full, preferred_element_type=F32)
    key_value = jnp.dot(attention_in, key_full, preferred_element_type=F32)
    projected_values = jnp.dot(attention_in, value_full, preferred_element_type=F32).astype(BF)
    rotated_queries = rotate(query_value, cosine_table, sine_table, head_size, False).astype(BF)
    rotated_keys = rotate(key_value, cosine_table, sine_table, head_size, False).astype(BF)

    def bucket(field, m):
        return field[m * bucket_rows : (m + 1) * bucket_rows]

    attended_parts = []
    log_sums = []
    for m in range(batches):
        attended, sums = attention_forward(
            bucket(rotated_queries, m),
            bucket(rotated_keys, m),
            bucket(projected_values, m),
            allowed[m],
            head_size,
            heads_per_group,
        )
        attended_parts.append(attended)
        log_sums.append(sums)
    attended_low = jnp.concatenate(attended_parts).astype(BF)

    def mean(field):
        return jnp.sum(field, axis=1, keepdims=True) / width

    residual = token_relative + jnp.dot(attended_low, output_full, preferred_element_type=F32)
    feed_scale = lax.rsqrt(mean(residual * residual) + EPS)
    feed_normed = residual * feed_scale
    feed_in = (feed_normed * gain_second).astype(BF)
    out_grad = to_relative(cotangent.reshape(rows, width)).astype(F32) * valid_rows
    branch_grad = out_grad.astype(BF)

    branch, feed_in_grad = 0.0, 0.0
    feed_shards = []
    for own, other in chunks:
        mix, grad_in, own_terms, other_terms = ffn_call(feed_in, branch_grad, own, other)
        branch = branch + mix
        feed_in_grad = feed_in_grad + grad_in
        feed_shards.append(scatter_chunk(grid, own_terms, other_terms, cut))
    mixed = to_natural((valid_rows * (residual + branch)).astype(BF))

    feed_gain_part = jnp.sum(feed_in_grad * feed_normed, axis=0)
    normed_grad = feed_in_grad * gain_second
    residual_grad = out_grad + feed_scale * (
        normed_grad - feed_normed * mean(normed_grad * feed_normed)
    )
    attention_branch_grad = residual_grad.astype(BF)
    attended_grad = dot(attention_branch_grad, output_full, NT).astype(BF)
    output_wgrad = dot(attended_low, attention_branch_grad, TN).astype(BF)
    backward = [
        attention_backward(
            bucket(rotated_queries, m),
            bucket(rotated_keys, m),
            bucket(projected_values, m),
            allowed[m],
            log_sums[m],
            bucket(attended_grad, m),
            head_size,
            heads_per_group,
        )
        for m in range(batches)
    ]
    query_rot_grad, key_rot_grad, value_part = [
        jnp.concatenate([parts[i] for parts in backward]) for i in range(3)
    ]
    query_part = rotate(query_rot_grad, cosine_table, sine_table, head_size, True).astype(BF)
    key_part = rotate(key_rot_grad, cosine_table, sine_table, head_size, True).astype(BF)
    value_low = value_part.astype(BF)
    attention_in_grad = (
        dot(query_part, query_full, NT)
        + dot(key_part, key_full, NT)
        + dot(value_low, value_full, NT)
    )
    query_wgrad = dot(attention_in, query_part, TN).astype(BF)
    key_wgrad = dot(attention_in, key_part, TN).astype(BF)
    value_wgrad = dot(attention_in, value_low, TN).astype(BF)
    token_extra, attention_gain_part = rms_back(
        token_rows, attention_scale, gain_first, attention_in_grad
    )
    tokens_grad = (to_natural(residual_grad) + token_extra).astype(BF)

    def blocked(field, count):
        return field.reshape(grid.outer, grid.inner, d_w, pair, 2, count).transpose(4, 3, 1, 0, 2, 5)

    stacked = jnp.stack([output_wgrad[:, i * d_pad : i * d_pad + d_n] for i in range(narrow)])
    output_natural = []
    for index in range(narrow):
        dc = (grid.at["core"] + index % 2) % 2
        dy = (grid.at["pair"] - index // 2 + pair) % pair
        output_natural.append(chosen(stacked, dc * pair + dy))
    terms = jnp.concatenate(
        [
            blocked(query_wgrad, d_n),
            blocked(jnp.concatenate(output_natural, axis=1), d_n),
            blocked(key_wgrad, kv_n),
            blocked(value_wgrad, kv_n),
        ],
        axis=5,
    )
    feed_gain_natural = to_natural(feed_gain_part[None])[0]
    gain_terms = jnp.concatenate(
        [
            attention_gain_part.reshape(pair, 2, d_n).transpose(1, 0, 2),
            feed_gain_natural.reshape(pair, 2, d_n).transpose(1, 0, 2),
            jnp.zeros((2, pair, 2 * kv_n), F32),
        ],
        axis=2,
    ).astype(BF)
    gain_terms = jnp.broadcast_to(
        gain_terms[:, :, None, None, None, :], (2, pair, grid.inner, grid.outer, 1, lanes)
    )
    spare = jnp.zeros((2, pair, grid.inner, grid.outer, a_rows - d_w - 1, lanes), BF)
    a_sum = scatter_attention(grid, jnp.concatenate([terms, gain_terms, spare], axis=4)).astype(F32)
    feed_sum = jnp.concatenate(feed_shards, axis=1).astype(F32)[:, :, :d_n]
    return (
        mixed.reshape(tokens.shape),
        tokens_grad.reshape(tokens.shape),
        a_sum[:d_w, :d_n],
        a_sum[:d_w, 2 * d_n : 2 * d_n + kv_n],
        a_sum[:d_w, 2 * d_n + kv_n :],
        a_sum[:d_w, d_n : 2 * d_n],
        feed_sum[0].T,
        feed_sum[1].T,
        feed_sum[2],
        a_sum[d_w, :d_n],
        a_sum[d_w, d_n : 2 * d_n],
    )


def solution(mesh):
    in_specs = (
        P(None, ("wide", "narrow"), None),
        P(None, ("wide", "narrow"), None),
        P(None, ("wide", "narrow"), None),
        P("wide", "narrow"),
        P("wide", "narrow"),
        P("wide", "narrow"),
        P("wide", "narrow"),
        P("narrow", "wide"),
        P("narrow", "wide"),
        P("wide", "narrow"),
        P("narrow"),
        P("narrow"),
    )
    out_specs = (
        P(None, ("wide", "narrow"), None),
        P(None, ("wide", "narrow"), None),
        P("wide", "narrow"),
        P("wide", "narrow"),
        P("wide", "narrow"),
        P("wide", "narrow"),
        P("narrow", "wide"),
        P("narrow", "wide"),
        P("wide", "narrow"),
        P("narrow"),
        P("narrow"),
    )
    return jax.shard_map(body, mesh=mesh, in_specs=in_specs, out_specs=out_specs, check_vma=False)
```

```python
import functools

import jax
import jax.numpy as jnp
from jax import lax
from jax.experimental import pallas as pl
from jax.experimental.pallas import tpu as pltpu
from jax.sharding import PartitionSpec as P

QUERY_HEADS = 15
KEY_VALUE_HEADS = 5
HEAD_WIDTH = 64


EPS = 1e-05
THETA = 10000.0


def segments_of(lengths_row, count_of_rows):
    ends = jnp.cumsum(lengths_row, dtype=jnp.int32)
    starts = ends - lengths_row
    places = jnp.arange(count_of_rows, dtype=jnp.int32)
    segment = jnp.sum((places[:, None] >= ends[None, :]).astype(jnp.int32), axis=1, dtype=jnp.int32)
    slot_ids = jnp.arange(lengths_row.shape[0], dtype=jnp.int32)
    opening = jnp.sum(
        jnp.where(segment[:, None] == slot_ids[None, :], starts[None, :], 0),
        axis=1,
        dtype=jnp.int32,
    )
    opening = jnp.where(segment == lengths_row.shape[0], ends[-1], opening)
    return (segment, places - opening)


F32 = jnp.float32
BF = jnp.bfloat16
NT = (((1,), (1,)), ((), ()))
TN = (((0,), (0,)), ((), ()))
NN = (((1,), (0,)), ((), ()))
VMEM_BYTES = 36 * 1024 * 1024


def dot(left, right, dims):
    return lax.dot_general(left, right, dims, preferred_element_type=F32)


def side(parts):
    return parts[0] if len(parts) == 1 else jnp.concatenate(parts, axis=1)


def mean_of(field, width):
    return jnp.sum(field, axis=1, keepdims=True) * (1.0 / width)


def row_of(block, row):
    at = lax.broadcasted_iota(jnp.int32, (block.shape[0], 1), 0)
    return jnp.sum(jnp.where(at == row, block.astype(F32), 0.0), axis=0, keepdims=True)


def zeros_beside(field, lanes, before):
    pad = jnp.zeros((field.shape[0], lanes - field.shape[1]), field.dtype)
    return side([pad, field] if before else [field, pad])


def turn(field, cosine, sine):
    lane = lax.broadcasted_iota(jnp.int32, (1, 128), 1)
    low = (lane % 64) < 32
    tiles = []
    for start in range(0, field.shape[1], 128):
        piece = field[:, start : start + 128]
        count = piece.shape[1]
        if count < 128:
            piece = zeros_beside(piece, 128, False)
        other = jnp.where(low, pltpu.roll(piece, 96, 1), pltpu.roll(piece, 32, 1))
        tiles.append((piece * cosine + other * sine)[:, :count])
    return side(tiles)


def places(lengths, bucket, slots, shape, axis):
    at = lax.broadcasted_iota(jnp.int32, shape, axis)
    end = jnp.int32(0)
    segment = jnp.zeros(shape, jnp.int32)
    opening = jnp.zeros(shape, jnp.int32)
    for slot in range(slots):
        length = lengths[bucket * slots + slot]
        end = end + length
        over = at >= end
        segment += jnp.where(over, 1, 0)
        opening += jnp.where(over, length, 0)
    return segment, at - opening, segment < slots


def prepare_narrow_kernel(sizes, batches, slots, w_order, n_order, lengths, tok_ref, cot_ref, tn_ref, gf_ref, n_blocks, c_blocks):
    wide, d_w, r_w, d_n, kv_n, pair, d_pad = sizes
    narrow = 2 * pair
    rows = tok_ref.shape[0] // batches
    for b in range(batches):
        part = slice(b * rows, (b + 1) * rows)
        _, _, inside = places(lengths, b, slots, (rows, 1), 0)
        field = tok_ref[part].astype(F32)
        upstream = jnp.where(inside, cot_ref[part].astype(F32), 0.0)
        for n in range(narrow):
            n_blocks[n, part] = zeros_beside(field[:, n * d_n : (n + 1) * d_n], d_pad, True).astype(BF)
            c_blocks[n, part] = zeros_beside(upstream[:, n * d_n : (n + 1) * d_n], d_pad, True).astype(BF)
    tn_ref[...] = side([n_blocks[n_order[index]] for index in range(narrow)])
    gf_ref[...] = side([c_blocks[n_order[index]] for index in range(narrow)])


def prepare_wide_kernel(sizes, batches, slots, w_order, n_order, lengths, tok_ref, freq_ref, tw_ref, cos_ref, sin_ref, w_blocks):
    wide, d_w, r_w, d_n, kv_n, pair, d_pad = sizes
    rows = tok_ref.shape[0] // batches
    field = tok_ref[...].astype(F32)
    for w in range(wide):
        w_blocks[w] = zeros_beside(field[:, w * d_w : (w + 1) * d_w], r_w, False).astype(BF)
    tw_ref[...] = side([w_blocks[w_order[p]] for p in range(wide)])
    sign = jnp.where(lax.broadcasted_iota(jnp.int32, (1, 128), 1) % 64 < 32, -1.0, 1.0)
    for b in range(batches):
        part = slice(b * rows, (b + 1) * rows)
        _, position, _ = places(lengths, b, slots, (rows, 1), 0)
        angle = position.astype(F32) * freq_ref[...]
        cos_ref[part] = jnp.cos(angle)
        sin_ref[part] = jnp.sin(angle) * sign


def beside(ref, at):
    return side([ref[at, p] for p in range(ref.shape[1])])


def gain_rows(sizes, own_ref, other_ref, n_order, gain_blocks):
    wide, d_w, r_w, d_n, kv_n, pair, d_pad = sizes
    lane = lax.broadcasted_iota(jnp.int32, (16, r_w), 1)
    chosen = jnp.where(lane == d_w, 1.0, 0.0).astype(BF)
    for index in range(2 * pair):
        block = (own_ref, other_ref)[index // pair][index % pair, 0]
        gain_blocks[n_order[index]] = dot(chosen, block, NT)[:1]
    return side([gain_blocks[n][:, :d_n] for n in range(2 * pair)])


def project_kernel(
    sizes, w_order, n_order, lengths, tw_ref, cos_ref, sin_ref, own_ref, other_ref,
    a_ref, q_ref, k_ref, v_ref, projected, gain_blocks, gain_wide,
):
    wide, d_w, r_w, d_n, kv_n, pair, d_pad = sizes
    narrow = 2 * pair
    width = wide * d_w
    gain = gain_rows(sizes, own_ref, other_ref, n_order, gain_blocks)
    for w in range(wide):
        gain_wide[w] = zeros_beside(gain[:, w * d_w : (w + 1) * d_w], r_w, False)
    field = tw_ref[...].astype(F32)
    scale = lax.rsqrt(mean_of(field * field, width) + EPS)
    a_wide = (field * scale * side([gain_wide[w_order[p]] for p in range(wide)])).astype(BF)
    a_ref[...] = a_wide
    for index in range(narrow):
        block = beside((own_ref, other_ref)[index // pair], index % pair)
        projected[n_order[index]] = dot(a_wide, block, NT)
    cosine, sine = cos_ref[...], sin_ref[...]

    def taken(start, count):
        return side([projected[n][:, start : start + count] for n in range(narrow)])

    q_ref[...] = (turn(taken(0, d_n), cosine, sine) * HEAD_WIDTH**-0.5).astype(BF)
    k_ref[...] = turn(taken(d_n, kv_n), cosine, sine).astype(BF)
    v_ref[...] = taken(d_n + kv_n, kv_n).astype(BF)


def attend_kernel(slots, w_order, n_order, lengths, q_ref, k_ref, v_ref, ob_ref, p_ref):
    rows = q_ref.shape[1]
    bucket = pl.program_id(0)
    seg_row, _, _ = places(lengths, bucket, slots, (1, rows), 1)
    seg_col, _, _ = places(lengths, bucket, slots, (rows, 1), 0)
    step = 128
    group = QUERY_HEADS // KEY_VALUE_HEADS
    head = HEAD_WIDTH
    offset = 0
    for i in range(rows // step):
        upto = (i + 1) * step
        query_at = i * step + lax.broadcasted_iota(jnp.int32, (step, upto), 0)
        key_at = lax.broadcasted_iota(jnp.int32, (step, upto), 1)
        same = seg_col[i * step : upto] == seg_row[:, :upto]
        bias = jnp.where(same & (key_at <= query_at), 0.0, -1000000000.0)
        for g in range(KEY_VALUE_HEADS):
            queries = jnp.concatenate(
                [
                    q_ref[0, i * step : upto, (g * group + j) * head : (g * group + j + 1) * head]
                    for j in range(group)
                ],
                axis=0,
            )
            keys = k_ref[0, :upto, g * head : (g + 1) * head]
            values = v_ref[0, :upto, g * head : (g + 1) * head]
            logits = dot(queries, keys, NT).reshape(group, step, upto) + bias[None]
            peak = jnp.max(logits, axis=-1, keepdims=True)
            shifted = jnp.exp(logits - peak)
            total = jnp.sum(shifted, axis=-1, keepdims=True)
            probs = (shifted * (1.0 / total)).astype(BF).reshape(group * step, upto)
            p_ref[0, g, :, offset : offset + upto] = probs
            out = dot(probs, values, NN).astype(BF)
            ob_ref[0, i * step : upto, g * group * head : (g + 1) * group * head] = side(
                [out[j * step : (j + 1) * step] for j in range(group)]
            )
        offset += upto


def residual_kernel(
    sizes, w_order, n_order, lengths, ob_ref, tn_ref, own_ref, other_ref, ob_wide_ref, hr_ref, bf_ref, e_blocks
):
    wide, d_w, r_w, d_n, kv_n, pair, d_pad = sizes
    narrow = 2 * pair
    spare = d_w // 16 * 16
    width = wide * d_w
    attended = ob_ref[...].astype(F32)
    for w in range(wide):
        e_blocks[w] = zeros_beside(attended[:, w * d_w : (w + 1) * d_w], r_w, False).astype(BF)
    ob_wide = side([e_blocks[w_order[p]] for p in range(wide)])
    ob_wide_ref[...] = ob_wide
    blocks = []
    gains = []
    for index in range(narrow):
        block = (own_ref, other_ref)[index // pair][index % pair].reshape(wide * r_w, d_pad)
        gains.append(row_of(block[spare : spare + 16], d_w - spare))
        rows_in = tn_ref[:, index * d_pad : (index + 1) * d_pad].astype(F32)
        blocks.append(rows_in + dot(ob_wide, block, NN))
    residual = side(blocks)
    hr_ref[...] = residual
    scale = lax.rsqrt(mean_of(residual * residual, width) + EPS)
    bf_ref[...] = (residual * scale * side(gains)).astype(BF)


def middle_kernel(
    sizes, w_order, n_order, lengths, hr_ref, back_ref, gf_ref, ob_ref, own_ref, other_ref,
    gh_ref, go_ref, own_terms, other_terms, e_blocks,
):
    wide, d_w, r_w, d_n, kv_n, pair, d_pad = sizes
    narrow = 2 * pair
    spare = d_w // 16 * 16
    width = wide * d_w
    residual = hr_ref[...]
    blocks = [
        (own_ref, other_ref)[index // pair][index % pair].reshape(wide * r_w, d_pad)
        for index in range(narrow)
    ]
    gain = side([row_of(block[spare : spare + 16], d_w - spare) for block in blocks])
    back = back_ref[...]
    scale = lax.rsqrt(mean_of(residual * residual, width) + EPS)
    normed = residual * scale
    gain_term = jnp.sum(back * normed, axis=0, keepdims=True)
    here = lax.broadcasted_iota(jnp.int32, (r_w, 1), 0) == d_w
    normed_grad = back * gain
    grad = gf_ref[...].astype(F32) + scale * (
        normed_grad - normed * mean_of(normed_grad * normed, width)
    )
    gh_ref[...] = grad
    low = grad.astype(BF)
    total = None
    ob_wide = ob_ref[...]
    for index in range(narrow):
        piece = low[:, index * d_pad : (index + 1) * d_pad]
        part = dot(piece, blocks[index], NT)
        total = part if total is None else total + part
        term = dot(ob_wide, piece, TN).reshape(wide, r_w, d_pad)
        row = gain_term[:, index * d_pad : (index + 1) * d_pad]
        ref = (own_terms, other_terms)[index // pair]
        ref[index % pair] = (term + jnp.where(here, row, 0.0)[None]).astype(BF)
    for p in range(wide):
        e_blocks[w_order[p]] = total[:, p * r_w : (p + 1) * r_w]
    go_ref[...] = side([e_blocks[w][:, :d_w] for w in range(wide)]).astype(BF)


def attend_back_kernel(
    q_ref, k_ref, v_ref, ob_ref, go_ref, p_ref, cos_ref, sin_ref, gq_ref, gk_ref, gv_ref, gq_sum, gk_sum, gv_sum
):
    rows = q_ref.shape[1]
    step = 128
    group = QUERY_HEADS // KEY_VALUE_HEADS
    head = HEAD_WIDTH
    for g in range(KEY_VALUE_HEADS):
        offset = 0
        lanes = slice(g * head, (g + 1) * head)
        gk_total, gv_total = [], []
        for i in range(rows // step):
            upto = (i + 1) * step

            def stacked(ref):
                return jnp.concatenate(
                    [
                        ref[0, i * step : upto, (g * group + j) * head : (g * group + j + 1) * head]
                        for j in range(group)
                    ],
                    axis=0,
                )

            queries, out_grads, outs = stacked(q_ref), stacked(go_ref), stacked(ob_ref)
            keys = k_ref[0, :upto, lanes]
            values = v_ref[0, :upto, lanes]
            probs = p_ref[0, g, :, offset : offset + upto]
            delta = jnp.sum(out_grads.astype(F32) * outs.astype(F32), axis=1, keepdims=True)
            prob_grad = dot(out_grads, values, NT)
            logit_grad = (probs.astype(F32) * (prob_grad - delta)).astype(BF)
            query_part = dot(logit_grad, keys, NN) * head**-0.5
            gq_sum[i * step : upto, g * group * head : (g + 1) * group * head] = side(
                [query_part[j * step : (j + 1) * step] for j in range(group)]
            )
            key_part = dot(logit_grad, queries, TN)
            value_part = dot(probs, out_grads, TN)
            for j in range(i + 1):
                if j == i:
                    gk_total.append(key_part[j * step : (j + 1) * step])
                    gv_total.append(value_part[j * step : (j + 1) * step])
                else:
                    gk_total[j] += key_part[j * step : (j + 1) * step]
                    gv_total[j] += value_part[j * step : (j + 1) * step]
            offset += upto
        gk_sum[:, lanes] = jnp.concatenate(gk_total, axis=0)
        gv_sum[:, lanes] = jnp.concatenate(gv_total, axis=0)
    cosine, sine = cos_ref[0], sin_ref[0]
    gq_ref[0] = turn(gq_sum[...], cosine, -sine).astype(BF)
    gk_ref[0] = turn(gk_sum[...], cosine, -sine).astype(BF)
    gv_ref[0] = gv_sum[...].astype(BF)


def weights_kernel(
    sizes, batches, w_order, n_order, lengths, tw_ref, a_ref, own_ref, other_ref, *refs
):
    wide, d_w, r_w, d_n, kv_n, pair, d_pad = sizes
    narrow = 2 * pair
    width = wide * d_w
    back_ref, own_terms, other_terms, g_blocks, gain_blocks, gain_wide = refs[3 * batches :]
    count = own_ref.shape[2]
    for b in range(batches):
        gq, gk, gv = [refs[kind * batches + b][...].astype(F32) for kind in range(3)]
        bucket = slice(b * gq.shape[0], (b + 1) * gq.shape[0])
        for n in range(narrow):
            piece = side(
                [
                    gq[:, n * d_n : (n + 1) * d_n],
                    gk[:, n * kv_n : (n + 1) * kv_n],
                    gv[:, n * kv_n : (n + 1) * kv_n],
                ]
            )
            if piece.shape[1] < count:
                piece = zeros_beside(piece, count, False)
            g_blocks[n, bucket] = piece.astype(BF)
    total = None
    for index in range(narrow):
        block = beside((own_ref, other_ref)[index // pair], index % pair)
        part = dot(g_blocks[n_order[index]], block, NN)
        total = part if total is None else total + part
    back_ref[...] = total
    field = tw_ref[...].astype(F32)
    scale = lax.rsqrt(mean_of(field * field, width) + EPS)
    gain_term = jnp.sum(total * (field * scale), axis=0, keepdims=True)
    for p in range(wide):
        gain_wide[w_order[p]] = gain_term[:, p * r_w : (p + 1) * r_w]
    gain_term = side([gain_wide[w][:, :d_w] for w in range(wide)])
    for n in range(narrow):
        gain_blocks[n] = zeros_beside(gain_term[:, n * d_n : (n + 1) * d_n], count, False)
    first = lax.broadcasted_iota(jnp.int32, (8, 1), 0) == 0
    lane = lax.broadcasted_iota(jnp.int32, (8, r_w), 1)
    chosen = jnp.where(first & (lane == d_w), 1.0, 0.0)
    a_wide = a_ref[...]
    for index in range(narrow):
        ref = (own_terms, other_terms)[index // pair]
        column = dot(jnp.broadcast_to(gain_blocks[n_order[index]], (8, count)), chosen, TN)
        term = dot(g_blocks[n_order[index]], a_wide, TN)
        for p in range(wide):
            ref[index % pair, p] = (term[:, p * r_w : (p + 1) * r_w] + column).astype(BF)


def outputs_kernel(
    sizes, batches, slots, w_order, n_order, lengths, hr_ref, mix_ref, gh_ref, tw_ref, back_ref, own_ref, other_ref,
    mixed_ref, grad_ref, n_blocks, d_blocks, gain_blocks, gain_wide,
):
    wide, d_w, r_w, d_n, kv_n, pair, d_pad = sizes
    narrow = 2 * pair
    width = wide * d_w
    rows = hr_ref.shape[0] // batches

    def natural(field):
        for index in range(narrow):
            n_blocks[n_order[index]] = field[:, index * d_pad : (index + 1) * d_pad]
        return side([n_blocks[n][:, d_pad - d_n :] for n in range(narrow)])

    inside = jnp.concatenate([places(lengths, b, slots, (rows, 1), 0)[2] for b in range(batches)], axis=0)
    mixed_ref[...] = natural(jnp.where(inside, hr_ref[...] + mix_ref[...], 0.0)).astype(BF)
    gain = gain_rows(sizes, own_ref, other_ref, n_order, gain_blocks)
    for w in range(wide):
        gain_wide[w] = zeros_beside(gain[:, w * d_w : (w + 1) * d_w], r_w, False)
    gain = side([gain_wide[w_order[p]] for p in range(wide)])
    field = tw_ref[...].astype(F32)
    scale = lax.rsqrt(mean_of(field * field, width) + EPS)
    normed = field * scale
    normed_grad = back_ref[...] * gain
    grad = scale * (normed_grad - normed * mean_of(normed_grad * normed, width))
    for p in range(wide):
        d_blocks[w_order[p]] = grad[:, p * r_w : (p + 1) * r_w]
    grad = side([d_blocks[w][:, :d_w] for w in range(wide)])
    grad_ref[...] = (natural(gh_ref[...]) + grad).astype(BF)


def params():
    return pltpu.CompilerParams(vmem_limit_bytes=VMEM_BYTES)


def cost(multiply_adds, arrays, transcendentals=0):
    return pl.CostEstimate(
        flops=2 * multiply_adds,
        bytes_accessed=sum(a.size * a.dtype.itemsize for a in arrays),
        transcendentals=transcendentals,
    )


def shaped(shape, dtype):
    return jax.ShapeDtypeStruct(shape, dtype)


def call(name, kernel, operands, out_shapes, scratch, multiply_adds, specs=None, orders=(), out_specs=None, grid=(1,), transcendentals=0):
    def whole(array):
        return pl.BlockSpec(array.shape, lambda *_: (0,) * len(array.shape))

    in_specs = [spec or whole(array) for array, spec in zip(operands, specs or [None] * len(operands))]
    return pl.pallas_call(
        kernel,
        grid_spec=pltpu.PrefetchScalarGridSpec(
            num_scalar_prefetch=len(orders),
            grid=grid,
            in_specs=in_specs,
            out_specs=out_specs or [whole(o) for o in out_shapes],
            scratch_shapes=scratch,
        ),
        out_shape=out_shapes,
        compiler_params=params(),
        cost_estimate=cost(multiply_adds, list(operands) + list(out_shapes), transcendentals),
        name=name,
    )(*orders, *operands)


FEED_VMEM = 44 * 1024 * 1024


def ffn_kernel(
    chained, bf_hbm, gf_hbm, own_hbm, other_hbm, *refs
):
    before = refs[:2] if chained else ()
    (
        own_out, other_out, mix_out, back_out,
        bf_ref, gf_ref, weights, terms, hidden, gate_part, up_part, mix_ref, back_ref,
        in_sems, out_sems, before_sems,
    ) = refs[len(before) :]
    pair, wide, _, units, lanes = own_hbm.shape
    narrow = 2 * pair
    total = wide * units

    def copy(source, target, sem):
        made = pltpu.make_async_copy(source, target, sem)
        made.start()
        return made

    rows_copy = copy(bf_hbm, bf_ref, in_sems.at[6])
    grads_copy = copy(gf_hbm, gf_ref, in_sems.at[7])
    loads = [
        [
            copy(ref.at[:, :, kind], weights.at[kind, side_at * pair : (side_at + 1) * pair], in_sems.at[2 * kind + side_at])
            for side_at, ref in enumerate((own_hbm, other_hbm))
        ]
        for kind in range(3)
    ]

    def weight(kind, lo=0, count=None):
        blocks = [weights[kind, index].reshape(total, lanes) for index in range(narrow)]
        if count is not None:
            blocks = [block[lo : lo + count] for block in blocks]
        return side(blocks)

    rows_copy.wait()
    for made in loads[0] + loads[1]:
        made.wait()
    grads_copy.wait()
    for made in loads[2]:
        made.wait()
    befores = [
        copy(ref, target, before_sems.at[at])
        for at, (ref, target) in enumerate(zip(before, (mix_ref, back_ref)))
    ]
    rows_in = bf_ref[...]
    grad_in = gf_ref[...]
    step = 256
    for lo in range(0, total, step):
        gate_value = dot(rows_in, weight(0, lo, step), NT)
        up_value = dot(rows_in, weight(1, lo, step), NT)
        hidden_grad = dot(grad_in, weight(2, lo, step), NT)
        sigmoid_gate = 1.0 / (1.0 + jnp.exp(-gate_value))
        silu = gate_value * sigmoid_gate
        hidden[:, lo : lo + step] = (silu * up_value).astype(BF)
        gate_part[:, lo : lo + step] = (
            hidden_grad * up_value * (sigmoid_gate * (1.0 + gate_value * (1.0 - sigmoid_gate)))
        ).astype(BF)
        up_part[:, lo : lo + step] = (hidden_grad * silu).astype(BF)
    stores = []
    for made in befores:
        made.wait()
    mix = dot(hidden[...], weight(2), NN)
    mix_ref[...] = mix_ref[...] + mix if chained else mix
    stores.append(copy(mix_ref, mix_out, out_sems.at[0]))
    back = dot(gate_part[...], weight(0), NN) + dot(up_part[...], weight(1), NN)
    back_ref[...] = back_ref[...] + back if chained else back
    stores.append(copy(back_ref, back_out, out_sems.at[1]))
    for kind, (left, right) in enumerate(((gate_part, rows_in), (up_part, rows_in), (hidden, grad_in))):
        term = dot(left[...], right, TN).astype(BF)
        for index in range(narrow):
            terms[kind, index] = term[:, index * lanes : (index + 1) * lanes].reshape(wide, units, lanes)
        for side_at, ref in enumerate((own_out, other_out)):
            stores.append(
                copy(
                    terms.at[kind, side_at * pair : (side_at + 1) * pair],
                    ref.at[:, :, kind],
                    out_sems.at[2 + 2 * kind + side_at],
                )
            )
    for made in stores:
        made.wait()


def ffn_call(rows_in, grad_in, own, other, before=()):
    pair, wide, _, units, lanes = own.shape
    rows, width = rows_in.shape
    total = wide * units
    anywhere = pl.BlockSpec(memory_space=pl.ANY)
    operands = (rows_in, grad_in, own, other, *before)

    def scratch(*shape, dtype=BF):
        return pltpu.VMEM(shape, dtype)

    own_terms, other_terms, mix, back = pl.pallas_call(
        functools.partial(ffn_kernel, bool(before)),
        in_specs=[anywhere] * len(operands),
        out_specs=[anywhere] * 4,
        out_shape=[shaped((pair, wide, 3, units, lanes), BF)] * 2 + [shaped((rows, width), F32)] * 2,
        scratch_shapes=[
            scratch(rows, width),
            scratch(rows, width),
            scratch(3, 2 * pair, wide, units, lanes),
            scratch(3, 2 * pair, wide, units, lanes),
            scratch(rows, total),
            scratch(rows, total),
            scratch(rows, total),
            scratch(rows, width, dtype=F32),
            scratch(rows, width, dtype=F32),
            pltpu.SemaphoreType.DMA((8,)),
            pltpu.SemaphoreType.DMA((8,)),
            pltpu.SemaphoreType.DMA((2,)),
        ],
        compiler_params=pltpu.CompilerParams(vmem_limit_bytes=FEED_VMEM),
        cost_estimate=cost(9 * rows * width * total, operands),
        name="feed_forward",
    )(*operands)
    return mix, back, own_terms, other_terms


AXES = ("wide", "narrow")


class Grid:
    def __init__(self):
        self.wide = lax.axis_size("wide")
        self.narrow = lax.axis_size("narrow")
        self.outer = 4
        self.inner = self.wide // 4
        self.pair = self.narrow // 2
        self.size = {"outer": 4, "inner": self.inner, "pair": self.pair, "core": 2}
        self.stride = {"outer": self.inner * self.narrow, "inner": self.narrow, "pair": 2, "core": 1}
        linear = lax.axis_index("wide") * self.narrow + lax.axis_index("narrow")
        self.at = {name: (linear // self.stride[name]) % self.size[name] for name in self.size}

    def shift(self, value, name, count=1):
        size, stride = self.size[name], self.stride[name]
        pairs = []
        for source in range(self.wide * self.narrow):
            digit = (source // stride) % size
            pairs.append((source, source + ((digit + count) % size - digit) * stride))
        return lax.ppermute(value, AXES, pairs)

    def behind(self, name, steps):
        return (self.at[name] + (self.size[name] - steps)) % self.size[name]


def after(value, others):
    if not others:
        return value
    return lax.optimization_barrier((value, *others))[0]


class Flow:
    def __init__(self, make, grid, *args):
        self.grid = grid
        self.gates = ()
        self.last = ()
        self.result = None
        self.run = make(self, *args)

    def step(self, *others):
        self.gates = others
        try:
            self.last = next(self.run)
        except StopIteration as stop:
            self.result = stop.value
            return self.result
        return None

    def finish(self):
        while self.result is None:
            self.step()
        return self.result

    def shift(self, value, name, count=1):
        return self.grid.shift(after(value, self.gates), name, count)

    def settle(self, value):
        return after(value, self.gates)


class Clock:
    def __init__(self):
        self.held = ()

    def now(self, value):
        return after(value, self.held)

    def phase(self, *starts, done=(), wait=(), leave=()):
        gates = self.held + tuple(done)
        for flow, steps in starts:
            for _ in range(steps):
                flow.step(*gates)
        flows = [flow for flow, _ in starts if flow not in leave] + list(wait)
        held = sum([tuple(flow.last) for flow in flows], tuple(done))
        if not starts:
            held = self.held + held
        self.held = held if held else self.held


def both_rings(flow, first, first_name, second, second_name):
    one, two = [first], [second]
    for at in range(max(flow.grid.size[first_name], flow.grid.size[second_name]) - 1):
        if at < flow.grid.size[first_name] - 1:
            one.append(flow.shift(one[-1], first_name))
        if at < flow.grid.size[second_name] - 1:
            two.append(flow.shift(two[-1], second_name))
        yield (one[-1], two[-1])
        if at < flow.grid.size[first_name] - 1:
            one[-1] = flow.settle(one[-1])
        if at < flow.grid.size[second_name] - 1:
            two[-1] = flow.settle(two[-1])
    return one, two


def gather_outer(flow, shard):
    moved = [flow.shift(shard, "outer", count) for count in range(1, flow.grid.outer)]
    yield tuple(moved)
    return [shard] + [flow.settle(block) for block in moved]


def gather_ring(flow, shard):
    blocks = [shard]
    for _ in range(flow.grid.outer - 1):
        blocks.append(flow.shift(blocks[-1], "outer"))
        yield (blocks[-1],)
        blocks[-1] = flow.settle(blocks[-1])
    return blocks


def gather_direct(flow, shard, cut):
    blocks = yield from gather_outer(flow, shard)
    return (yield from gather_plane(flow, blocks, cut))


def gather_plane(flow, blocks, cut):
    first = jnp.stack([part[:, :cut] for part in blocks])
    second = jnp.stack([part[:, cut:] for part in blocks])
    one, two = yield from both_rings(flow, first, "inner", second, "pair")
    one, two = yield from both_rings(flow, jnp.concatenate(one), "pair", jnp.stack(two), "inner")
    own = jnp.concatenate([jnp.stack(one), jnp.concatenate(two, axis=1)], axis=3)
    other = flow.shift(own, "core")
    yield (other,)
    return own, other


def gather_outer_last(flow, shard, cut):
    first, second = shard[:, :cut], shard[:, cut:]
    one, two = yield from both_rings(flow, first, "inner", second, "pair")
    one, two = yield from both_rings(flow, jnp.stack(one), "pair", jnp.stack(two), "inner")
    block = jnp.concatenate([jnp.stack(one), jnp.stack(two, axis=1)], axis=3)
    blocks = [block]
    for _ in range(flow.grid.outer - 1):
        blocks.append(flow.shift(blocks[-1], "outer"))
        yield (blocks[-1],)
        blocks[-1] = flow.settle(blocks[-1])
    own = jnp.concatenate(blocks, axis=1)
    other = flow.shift(own, "core")
    yield (other,)
    return own, other


def both_sums(flow, first, first_name, second, second_name):
    sizes = flow.grid.size
    one, two = first(1), second(1)
    for step in range(1, max(sizes[first_name], sizes[second_name])):
        moved = []
        if step < sizes[first_name]:
            one = flow.shift(one, first_name)
            moved.append(one)
        if step < sizes[second_name]:
            two = flow.shift(two, second_name)
            moved.append(two)
        yield tuple(moved)
        if step < sizes[first_name]:
            one = flow.settle(one)
        if step < sizes[second_name]:
            two = flow.settle(two)
        if step < sizes[first_name]:
            one = one + first((step + 1) % sizes[first_name])
        if step < sizes[second_name]:
            two = two + second((step + 1) % sizes[second_name])
    return one, two


def scatter_plane(flow, own, other, cut, outer_major=False):
    outer, inner, pair = flow.grid.outer, flow.grid.inner, flow.grid.pair
    moved = flow.shift(other, "core")
    yield (moved,)
    both = flow.settle(moved) + own
    split = (outer, inner) if outer_major else (inner, outer)
    both = both.reshape(pair, *split, *both.shape[2:])
    at = 1 if outer_major else 0

    def chosen(array, r, axis):
        return lax.index_in_dim(array, r, axis, keepdims=False)

    one, two = yield from both_sums(
        flow,
        lambda r: both[r, :, :, :, :cut],
        "pair",
        lambda r: chosen(both, r, at + 1)[:, :, :, cut:],
        "inner",
    )
    one, two = yield from both_sums(
        flow, lambda r: chosen(one, r, at), "inner", lambda r: two[r], "pair"
    )
    return jnp.concatenate([one, two], axis=2)


def scatter_outer(flow, sums):
    outer = flow.grid.outer
    moved = [flow.shift(sums[r], "outer", outer - r) for r in range(1, outer)]
    yield tuple(moved)
    return sum([flow.settle(block).astype(F32) for block in moved], sums[0].astype(F32))


def rounded_up(count, step):
    return -(-count // step) * step
def body(
    tokens,
    lengths,
    cotangent,
    query_weight,
    key_matrix,
    value_matrix,
    output_weight,
    gate_weight,
    up_weight,
    down_weight,
    attention_gain,
    feedforward_gain,
):
    grid = Grid()
    batches, bucket_rows, width = tokens.shape
    rows = batches * bucket_rows
    wide, narrow, pair, inner, outer = grid.wide, grid.narrow, grid.pair, grid.inner, grid.outer
    d_w, d_n = query_weight.shape
    kv_n = key_matrix.shape[1]
    f_w = down_weight.shape[0]
    d_pad = rounded_up(d_n, 128)
    r_w = rounded_up(d_w + 1, 64)
    taken = d_n + 2 * kv_n
    t_rows = rounded_up(taken, 16)
    sizes = (wide, d_w, r_w, d_n, kv_n, pair, d_pad)

    packed = jnp.concatenate([query_weight.T, key_matrix.T, value_matrix.T], axis=0)
    gain_column = jnp.concatenate([attention_gain, jnp.zeros((2 * kv_n,), BF)])[:, None]
    packed = jnp.concatenate([packed, gain_column, jnp.zeros((taken, r_w - d_w - 1), BF)], axis=1)
    a_shard = jnp.pad(packed, ((0, t_rows - taken), (0, 0)))[None]
    a_cut = rounded_up(t_rows // 2, 16)
    o_shard = jnp.concatenate([output_weight, feedforward_gain[None], jnp.zeros((r_w - d_w - 1, d_n), BF)])
    f_shard = jnp.stack([gate_weight.T, up_weight.T, down_weight])
    sub = 256 // wide
    tiles_in = f_w // sub
    counts = [tiles_in - 2 * (3 * tiles_in // 10), 3 * tiles_in // 10, 3 * tiles_in // 10]
    bounds = [sub * sum(counts[:i]) for i in range(4)]
    shards = [f_shard[:, lo:hi] for lo, hi in zip(bounds, bounds[1:])]
    shards[0] = jnp.concatenate([shards[0], o_shard[None]])
    shards = [jnp.pad(shard, ((0, 0), (0, 0), (d_pad - d_n, 0))) for shard in shards]
    kinds = [shard.shape[0] for shard in shards]
    heights = [shard.shape[1] for shard in shards]
    cuts = [height // 2 for height in heights]
    z_shard = jnp.concatenate([shard.reshape(1, -1, d_pad) for shard in shards[:2]], axis=1)
    z_split = kinds[0] * heights[0]

    place = jnp.arange(wide, dtype=jnp.int32)
    w_order = (grid.at["outer"] - place % outer) % outer * inner
    w_order = (w_order + (grid.at["inner"] - place // outer) % inner).astype(jnp.int32)
    place = jnp.arange(narrow, dtype=jnp.int32)
    n_order = (grid.at["pair"] - place % pair) % pair * 2
    n_order = (n_order + (grid.at["core"] - place // pair) % 2).astype(jnp.int32)
    slots = lengths.shape[2]
    orders = (w_order, n_order, lengths.reshape(-1))
    freqs = THETA ** (-jnp.arange(HEAD_WIDTH // 2, dtype=F32) * 2.0 / HEAD_WIDTH)
    freqs = jnp.concatenate([freqs] * 4)[None]

    def scratch(*shape, dtype=F32):
        return pltpu.VMEM(shape, dtype)

    flow_a = Flow(gather_direct, grid, a_shard, a_cut)
    flow_3 = Flow(gather_outer_last, grid, shards[2], cuts[2])
    flow_z = Flow(gather_ring, grid, z_shard)
    plane = max(inner, pair) - 1
    clock = Clock()
    clock.phase((flow_a, 1), (flow_3, plane), leave=(flow_a,))
    clock.phase((flow_3, plane), leave=(flow_a, flow_3))
    token_rows = tokens.reshape(rows, width)
    cotangent_rows = cotangent.reshape(rows, width)
    token_narrow, branch_grad = call(
        "prepare_narrow",
        functools.partial(prepare_narrow_kernel, sizes, batches, slots),
        (token_rows, cotangent_rows),
        [shaped((rows, narrow * d_pad), BF)] * 2,
        [scratch(narrow, rows, d_pad, dtype=BF)] * 2,
        0,
        orders=orders,
    )
    clock.phase(done=(token_narrow,), wait=(flow_a, flow_3))
    clock.phase((flow_a, plane), (flow_z, 1), leave=(flow_a, flow_z))
    token_wide, cosine, sine = call(
        "prepare_wide",
        functools.partial(prepare_wide_kernel, sizes, batches, slots),
        (clock.now(token_rows), freqs),
        [shaped((rows, wide * r_w), BF), shaped((rows, 128), F32), shaped((rows, 128), F32)],
        [scratch(wide, rows, r_w, dtype=BF)],
        0,
        orders=orders,
    )
    clock.phase(done=(token_wide,), wait=(flow_a, flow_z))
    clock.phase((flow_a, plane), (flow_z, 1))
    clock.phase((flow_a, 1), (flow_z, 1))
    z_blocks = flow_z.finish()
    starts = (0, z_split, z_shard.shape[1])
    flow_1, flow_2 = [
        Flow(
            gather_plane,
            grid,
            [block[0, lo:hi].reshape(kinds[i], heights[i], d_pad) for block in z_blocks],
            cuts[i],
        )
        for i, (lo, hi) in enumerate(zip(starts, starts[1:]))
    ]
    clock.phase((flow_1, plane), (flow_3, 1), leave=(flow_1, flow_3))
    a_own, a_other = flow_a.finish()
    a_own, a_other = [x.reshape(pair, wide, t_rows, r_w) for x in (a_own, a_other)]
    a_in, query, key, value = call(
        "project",
        functools.partial(project_kernel, sizes),
        (clock.now(token_wide), cosine, sine, a_own, a_other),
        [
            shaped((rows, wide * r_w), BF),
            shaped((rows, QUERY_HEADS * HEAD_WIDTH), BF),
            shaped((rows, KEY_VALUE_HEADS * HEAD_WIDTH), BF),
            shaped((rows, KEY_VALUE_HEADS * HEAD_WIDTH), BF),
        ],
        [scratch(narrow, rows, t_rows), scratch(narrow, 1, t_rows), scratch(wide, 1, r_w)],
        rows * wide * r_w * narrow * t_rows,
        orders=orders,
    )

    clock.phase(done=(query,), wait=(flow_1, flow_3))
    clock.phase((flow_1, plane), (flow_3, 1), leave=(flow_1, flow_3))

    def by_bucket(field):
        return field.reshape(batches, bucket_rows, field.shape[-1])

    def bucket_spec(*shape):
        return pl.BlockSpec((1, *shape), lambda b, *_: (b,) + (0,) * len(shape))

    group = QUERY_HEADS // KEY_VALUE_HEADS
    steps = bucket_rows // 128
    p_shape = (batches, KEY_VALUE_HEADS, group * 128, 128 * steps * (steps + 1) // 2)
    query, key, value = by_bucket(query), by_bucket(key), by_bucket(value)
    operands = (clock.now(query), key, value)
    pair_work = batches * QUERY_HEADS * bucket_rows * bucket_rows * HEAD_WIDTH
    out_shapes = [shaped(query.shape, BF), shaped(p_shape, BF)]
    attended, probs = call(
        "attend",
        functools.partial(attend_kernel, slots),
        operands,
        out_shapes,
        [],
        6 * pair_work,
        specs=[bucket_spec(*x.shape[1:]) for x in operands],
        out_specs=[bucket_spec(*x.shape[1:]) for x in out_shapes],
        grid=(batches,),
        orders=orders,
        transcendentals=batches * QUERY_HEADS * bucket_rows * bucket_rows,
    )
    attended_rows = attended.reshape(rows, width)
    clock.phase(done=(attended,), wait=(flow_1, flow_3))
    clock.phase((flow_1, 1), (flow_2, plane), (flow_3, 1), leave=(flow_2, flow_3))
    attended_rows = attended.reshape(rows, width)
    first_own, first_other = flow_1.finish()
    o_spec = pl.BlockSpec((pair, wide, None, r_w, d_pad), lambda *_: (0, 0, 3, 0, 0))
    o_operands = (first_own, first_other)
    o_specs = [o_spec] * 2
    d_lanes = narrow * d_pad
    attended_wide, residual, feed_in = call(
        "residual",
        functools.partial(residual_kernel, sizes),
        (clock.now(attended_rows), token_narrow) + o_operands,
        [
            shaped((rows, wide * r_w), BF),
            shaped((rows, d_lanes), F32),
            shaped((rows, d_lanes), BF),
        ],
        [scratch(wide, rows, r_w, dtype=BF)],
        rows * wide * r_w * d_lanes,
        specs=[None] * 2 + o_specs,
        orders=orders,
    )

    sums_so_far = ()

    def feed(flow):
        nonlocal sums_so_far
        own, other = flow.finish()
        *sums_so_far, own_terms, other_terms = ffn_call(
            clock.now(feed_in), branch_grad, own, other, tuple(sums_so_far)
        )
        clock.phase(done=(own_terms,))
        return own_terms, other_terms

    clock.phase(done=(feed_in,), wait=(flow_2,))
    clock.phase((flow_2, plane), leave=(flow_2,))
    terms = feed(flow_1)
    back_1 = Flow(scatter_plane, grid, *terms, cuts[0])
    clock.phase(wait=(flow_2, flow_3))
    clock.phase((flow_2, 1))
    clock.phase((back_1, 1), (flow_3, 1), leave=(back_1, flow_3))
    terms = feed(flow_2)
    back_2 = Flow(scatter_plane, grid, *terms, cuts[1])
    clock.phase(wait=(back_1, flow_3))
    clock.phase((back_2, 1), (back_1, plane), leave=(back_1, back_2))
    terms = feed(flow_3)
    back_3 = Flow(scatter_plane, grid, *terms, cuts[2], True)
    clock.phase(wait=(back_1, back_2))
    clock.phase((back_3, 1), (back_1, plane), (back_2, plane), leave=(back_1, back_2, back_3))

    mix, back = sums_so_far
    grad, attended_grad, own_o, other_o = call(
        "middle",
        functools.partial(middle_kernel, sizes),
        (clock.now(residual), back, branch_grad, attended_wide) + o_operands,
        [
            shaped((rows, d_lanes), F32),
            shaped((rows, width), BF),
            shaped((pair, wide, r_w, d_pad), BF),
            shaped((pair, wide, r_w, d_pad), BF),
        ],
        [scratch(wide, rows, r_w)],
        2 * rows * wide * r_w * d_lanes,
        specs=[None] * 4 + o_specs,
        orders=orders,
    )

    clock.phase(done=(attended_grad,), wait=(back_1, back_2, back_3))
    back_z1 = Flow(scatter_outer, grid, back_1.finish())
    clock.phase((back_2, plane), (back_z1, 1), leave=(back_2, back_z1))
    operands = (key, value, attended, by_bucket(attended_grad), probs, by_bucket(cosine), by_bucket(sine))
    shapes = [(1, *x.shape[1:]) for x in (query, key, value)]
    grads = []
    for b in range(batches):

        def at_bucket(x):
            return pl.BlockSpec((1, *x.shape[1:]), lambda _, b=b: (b,) + (0,) * (x.ndim - 1))

        grads.append(
            call(
                "attend_back",
                attend_back_kernel,
                (clock.now(query),) + operands,
                [shaped(shape, BF) for shape in shapes],
                [scratch(*shape[1:]) for shape in shapes],
                12 * pair_work // batches,
                specs=[at_bucket(x) for x in (query,) + operands],
            )
        )
        if b == 0:
            clock.phase(done=(grads[0][0],), wait=(back_2, back_z1))
            back_z2 = Flow(scatter_outer, grid, back_2.finish())
            clock.phase((back_3, plane), (back_z2, 1), leave=(back_3, back_z2))
    clock.phase(done=tuple(x[0] for x in grads), wait=(back_3, back_z2))
    back_o = Flow(scatter_plane, grid, own_o[:, :, None], other_o[:, :, None], r_w // 2)
    clock.phase((back_o, 1), (back_3, plane), leave=(back_3, back_o))
    operands = tuple(x.reshape(bucket_rows, -1) for parts in zip(*grads) for x in parts)
    wide_back, own_terms, other_terms = call(
        "weights",
        functools.partial(weights_kernel, sizes, batches),
        (clock.now(token_wide), a_in, a_own, a_other) + operands,
        [shaped((rows, wide * r_w), F32)] + [shaped(a_own.shape, BF)] * 2,
        [scratch(narrow, rows, t_rows, dtype=BF), scratch(narrow, 1, t_rows), scratch(wide, 1, r_w)],
        2 * rows * wide * r_w * narrow * t_rows,
        orders=orders,
    )
    back_a = Flow(scatter_plane, grid, own_terms[:, :, None], other_terms[:, :, None], a_cut)
    clock.phase(done=(own_terms,), wait=(back_o, back_3))
    clock.phase((back_a, 1), (back_o, plane))
    back_z3 = Flow(scatter_outer, grid, back_3.finish())
    clock.phase((back_a, plane), (back_z3, 1), leave=(back_a, back_z3))
    mixed, tokens_grad = call(
        "outputs",
        functools.partial(outputs_kernel, sizes, batches, slots),
        (clock.now(residual), mix, grad, token_wide, wide_back, a_own, a_other),
        [shaped((rows, width), BF)] * 2,
        [
            scratch(narrow, rows, d_pad),
            scratch(wide, rows, r_w),
            scratch(narrow, 1, t_rows),
            scratch(wide, 1, r_w),
        ],
        0,
        orders=orders,
    )
    clock.phase(done=(mixed,), wait=(back_a, back_z3))
    clock.phase((back_a, plane), (back_o, plane))
    o_last = back_o.finish()
    o_last = jnp.concatenate([o_last[..., at : at + r_w] for at in range(0, d_pad, r_w)], axis=2)
    back_za = Flow(scatter_outer, grid, jnp.concatenate([back_a.finish(), o_last], axis=2))
    clock.phase((back_za, 1), leave=(back_za,))
    mixed, tokens_grad = after(mixed, back_za.last), after(tokens_grad, back_za.last)
    ao_sum = back_za.finish()[0]
    a_sum = ao_sum[:t_rows]
    o_sum = jnp.concatenate(
        [ao_sum[at : at + r_w] for at in range(t_rows, ao_sum.shape[0], r_w)], axis=1
    )
    feed_shards = [back_z1.finish(), back_z2.finish(), back_z3.finish()]
    feed_sum = jnp.concatenate(feed_shards, axis=1)[:, :, d_pad - d_n :]
    return (
        mixed.reshape(tokens.shape),
        tokens_grad.reshape(tokens.shape),
        a_sum[:d_n, :d_w].T,
        a_sum[d_n : d_n + kv_n, :d_w].T,
        a_sum[d_n + kv_n : taken, :d_w].T,
        o_sum[:d_w, d_pad - d_n :],
        feed_sum[0].T,
        feed_sum[1].T,
        feed_sum[2],
        a_sum[:d_n, d_w],
        o_sum[d_w, d_pad - d_n :],
    )


def solution(mesh):
    in_specs = (
        P(None, ("wide", "narrow"), None),
        P(None, ("wide", "narrow"), None),
        P(None, ("wide", "narrow"), None),
        P("wide", "narrow"),
        P("wide", "narrow"),
        P("wide", "narrow"),
        P("wide", "narrow"),
        P("narrow", "wide"),
        P("narrow", "wide"),
        P("wide", "narrow"),
        P("narrow"),
        P("narrow"),
    )
    out_specs = (
        P(None, ("wide", "narrow"), None),
        P(None, ("wide", "narrow"), None),
        P("wide", "narrow"),
        P("wide", "narrow"),
        P("wide", "narrow"),
        P("wide", "narrow"),
        P("narrow", "wide"),
        P("narrow", "wide"),
        P("wide", "narrow"),
        P("narrow"),
        P("narrow"),
    )
    return jax.shard_map(body, mesh=mesh, in_specs=in_specs, out_specs=out_specs, check_vma=False)
```

```python
import functools

import jax
import jax.numpy as jnp
from jax import lax
from jax.experimental import pallas as pl
from jax.experimental.pallas import tpu as pltpu
from jax.sharding import PartitionSpec as P

QUERY_HEADS = 15
KEY_VALUE_HEADS = 5
HEAD_WIDTH = 64


EPS = 1e-05
THETA = 10000.0


def segments_of(lengths_row, count_of_rows):
    ends = jnp.cumsum(lengths_row, dtype=jnp.int32)
    starts = ends - lengths_row
    places = jnp.arange(count_of_rows, dtype=jnp.int32)
    segment = jnp.sum((places[:, None] >= ends[None, :]).astype(jnp.int32), axis=1, dtype=jnp.int32)
    slot_ids = jnp.arange(lengths_row.shape[0], dtype=jnp.int32)
    opening = jnp.sum(
        jnp.where(segment[:, None] == slot_ids[None, :], starts[None, :], 0),
        axis=1,
        dtype=jnp.int32,
    )
    opening = jnp.where(segment == lengths_row.shape[0], ends[-1], opening)
    return (segment, places - opening)


F32 = jnp.float32
BF = jnp.bfloat16
NT = (((1,), (1,)), ((), ()))
TN = (((0,), (0,)), ((), ()))
NN = (((1,), (0,)), ((), ()))


def dot(left, right, dims):
    return lax.dot_general(left, right, dims, preferred_element_type=F32)


def side(parts):
    return parts[0] if len(parts) == 1 else jnp.concatenate(parts, axis=1)


def mean_of(field, width):
    return jnp.sum(field, axis=1, keepdims=True) * (1.0 / width)


def row_of(block, row):
    at = lax.broadcasted_iota(jnp.int32, (block.shape[0], 1), 0)
    return jnp.sum(jnp.where(at == row, block.astype(F32), 0.0), axis=0, keepdims=True)


def zeros_beside(field, lanes, before):
    pad = jnp.zeros((field.shape[0], lanes - field.shape[1]), field.dtype)
    return side([pad, field] if before else [field, pad])


def turn(field, cosine, sine):
    lane = lax.broadcasted_iota(jnp.int32, (1, 128), 1)
    low = (lane % 64) < 32
    tiles = []
    for start in range(0, field.shape[1], 128):
        piece = field[:, start : start + 128]
        count = piece.shape[1]
        if count < 128:
            piece = zeros_beside(piece, 128, False)
        other = jnp.where(low, pltpu.roll(piece, 96, 1), pltpu.roll(piece, 32, 1))
        tiles.append((piece * cosine + other * sine)[:, :count])
    return side(tiles)


def places(lengths, bucket, slots, shape, axis):
    at = lax.broadcasted_iota(jnp.int32, shape, axis)
    end = jnp.int32(0)
    segment = jnp.zeros(shape, jnp.int32)
    opening = jnp.zeros(shape, jnp.int32)
    for slot in range(slots):
        length = lengths[bucket * slots + slot]
        end = end + length
        over = at >= end
        segment += jnp.where(over, 1, 0)
        opening += jnp.where(over, length, 0)
    return segment, at - opening, segment < slots


def prepare_narrow_kernel(sizes, batches, slots, w_order, n_order, lengths, tok_ref, cot_ref, tn_ref, gf_ref, n_blocks, c_blocks):
    wide, d_w, r_w, d_n, kv_n, pair, d_pad = sizes
    narrow = 2 * pair
    rows = tok_ref.shape[0] // batches
    for b in range(batches):
        part = slice(b * rows, (b + 1) * rows)
        _, _, inside = places(lengths, b, slots, (rows, 1), 0)
        field = tok_ref[part].astype(F32)
        upstream = jnp.where(inside, cot_ref[part].astype(F32), 0.0)
        for n in range(narrow):
            n_blocks[n, part] = zeros_beside(field[:, n * d_n : (n + 1) * d_n], d_pad, True).astype(BF)
            c_blocks[n, part] = zeros_beside(upstream[:, n * d_n : (n + 1) * d_n], d_pad, True).astype(BF)
    tn_ref[...] = side([n_blocks[n_order[index]] for index in range(narrow)])
    gf_ref[...] = side([c_blocks[n_order[index]] for index in range(narrow)])


def prepare_wide_kernel(sizes, batches, slots, w_order, n_order, lengths, tok_ref, freq_ref, tw_ref, cos_ref, sin_ref, w_blocks):
    wide, d_w, r_w, d_n, kv_n, pair, d_pad = sizes
    rows = tok_ref.shape[0] // batches
    field = tok_ref[...].astype(F32)
    for w in range(wide):
        w_blocks[w] = zeros_beside(field[:, w * d_w : (w + 1) * d_w], r_w, False).astype(BF)
    tw_ref[...] = side([w_blocks[w_order[p]] for p in range(wide)])
    sign = jnp.where(lax.broadcasted_iota(jnp.int32, (1, 128), 1) % 64 < 32, -1.0, 1.0)
    for b in range(batches):
        part = slice(b * rows, (b + 1) * rows)
        _, position, _ = places(lengths, b, slots, (rows, 1), 0)
        angle = position.astype(F32) * freq_ref[...]
        cos_ref[part] = jnp.cos(angle)
        sin_ref[part] = jnp.sin(angle) * sign


def beside(ref, at):
    return side([ref[at, p] for p in range(ref.shape[1])])


def gain_rows(sizes, own_ref, other_ref, n_order, gain_blocks):
    wide, d_w, r_w, d_n, kv_n, pair, d_pad = sizes
    lane = lax.broadcasted_iota(jnp.int32, (16, r_w), 1)
    chosen = jnp.where(lane == d_w, 1.0, 0.0).astype(BF)
    for index in range(2 * pair):
        block = (own_ref, other_ref)[index // pair][index % pair, 0]
        gain_blocks[n_order[index]] = dot(chosen, block, NT)[:1]
    return side([gain_blocks[n][:, :d_n] for n in range(2 * pair)])


def project_kernel(
    sizes, w_order, n_order, lengths, tw_ref, cos_ref, sin_ref, own_ref, other_ref,
    a_ref, q_ref, k_ref, v_ref, projected, gain_blocks, gain_wide,
):
    wide, d_w, r_w, d_n, kv_n, pair, d_pad = sizes
    narrow = 2 * pair
    width = wide * d_w
    gain = gain_rows(sizes, own_ref, other_ref, n_order, gain_blocks)
    for w in range(wide):
        gain_wide[w] = zeros_beside(gain[:, w * d_w : (w + 1) * d_w], r_w, False)
    field = tw_ref[...].astype(F32)
    scale = lax.rsqrt(mean_of(field * field, width) + EPS)
    a_wide = (field * scale * side([gain_wide[w_order[p]] for p in range(wide)])).astype(BF)
    a_ref[...] = a_wide
    for index in range(narrow):
        block = beside((own_ref, other_ref)[index // pair], index % pair)
        projected[n_order[index]] = dot(a_wide, block, NT)
    cosine, sine = cos_ref[...], sin_ref[...]

    def taken(start, count):
        return side([projected[n][:, start : start + count] for n in range(narrow)])

    q_ref[...] = (turn(taken(0, d_n), cosine, sine) * HEAD_WIDTH**-0.5).astype(BF)
    k_ref[...] = turn(taken(d_n, kv_n), cosine, sine).astype(BF)
    v_ref[...] = taken(d_n + kv_n, kv_n).astype(BF)


def attend_kernel(slots, bucket, w_order, n_order, lengths, q_ref, k_ref, v_ref, ob_ref, p_ref):
    rows = q_ref.shape[1]
    seg_row, _, _ = places(lengths, bucket, slots, (1, rows), 1)
    seg_col, _, _ = places(lengths, bucket, slots, (rows, 1), 0)
    step = 128
    group = QUERY_HEADS // KEY_VALUE_HEADS
    head = HEAD_WIDTH
    offset = 0
    for i in range(rows // step):
        upto = (i + 1) * step
        query_at = i * step + lax.broadcasted_iota(jnp.int32, (step, upto), 0)
        key_at = lax.broadcasted_iota(jnp.int32, (step, upto), 1)
        same = seg_col[i * step : upto] == seg_row[:, :upto]
        bias = jnp.where(same & (key_at <= query_at), 0.0, -1000000000.0)
        for g in range(KEY_VALUE_HEADS):
            queries = jnp.concatenate(
                [
                    q_ref[bucket, i * step : upto, (g * group + j) * head : (g * group + j + 1) * head]
                    for j in range(group)
                ],
                axis=0,
            )
            keys = k_ref[bucket, :upto, g * head : (g + 1) * head]
            values = v_ref[bucket, :upto, g * head : (g + 1) * head]
            logits = dot(queries, keys, NT).reshape(group, step, upto) + bias[None]
            peak = jnp.max(logits, axis=-1, keepdims=True)
            shifted = jnp.exp(logits - peak)
            total = jnp.sum(shifted, axis=-1, keepdims=True)
            probs = (shifted * (1.0 / total)).astype(BF).reshape(group * step, upto)
            p_ref[g, :, offset : offset + upto] = probs
            out = dot(probs, values, NN).astype(BF)
            ob_ref[i * step : upto, g * group * head : (g + 1) * group * head] = side(
                [out[j * step : (j + 1) * step] for j in range(group)]
            )
        offset += upto


def residual_kernel(
    sizes, batches, w_order, n_order, lengths, tn_ref, own_ref, other_ref, *refs
):
    ob_wide_ref, hr_ref, bf_ref, e_blocks = refs[batches:]
    wide, d_w, r_w, d_n, kv_n, pair, d_pad = sizes
    narrow = 2 * pair
    spare = d_w // 16 * 16
    width = wide * d_w
    attended = jnp.concatenate([ref[...].astype(F32) for ref in refs[:batches]], axis=0)
    for w in range(wide):
        e_blocks[w] = zeros_beside(attended[:, w * d_w : (w + 1) * d_w], r_w, False).astype(BF)
    ob_wide = side([e_blocks[w_order[p]] for p in range(wide)])
    ob_wide_ref[...] = ob_wide
    blocks = []
    gains = []
    for index in range(narrow):
        block = (own_ref, other_ref)[index // pair][index % pair].reshape(wide * r_w, d_pad)
        gains.append(row_of(block[spare : spare + 16], d_w - spare))
        rows_in = tn_ref[:, index * d_pad : (index + 1) * d_pad].astype(F32)
        blocks.append(rows_in + dot(ob_wide, block, NN))
    residual = side(blocks)
    hr_ref[...] = residual
    scale = lax.rsqrt(mean_of(residual * residual, width) + EPS)
    bf_ref[...] = (residual * scale * side(gains)).astype(BF)


def middle_kernel(
    sizes, w_order, n_order, lengths, hr_ref, back_ref, gf_ref, ob_ref, own_ref, other_ref,
    gh_ref, go_ref, own_terms, other_terms, e_blocks,
):
    wide, d_w, r_w, d_n, kv_n, pair, d_pad = sizes
    narrow = 2 * pair
    spare = d_w // 16 * 16
    width = wide * d_w
    residual = hr_ref[...]
    blocks = [
        (own_ref, other_ref)[index // pair][index % pair].reshape(wide * r_w, d_pad)
        for index in range(narrow)
    ]
    gain = side([row_of(block[spare : spare + 16], d_w - spare) for block in blocks])
    back = back_ref[...]
    scale = lax.rsqrt(mean_of(residual * residual, width) + EPS)
    normed = residual * scale
    gain_term = jnp.sum(back * normed, axis=0, keepdims=True)
    here = lax.broadcasted_iota(jnp.int32, (r_w, 1), 0) == d_w
    normed_grad = back * gain
    grad = gf_ref[...].astype(F32) + scale * (
        normed_grad - normed * mean_of(normed_grad * normed, width)
    )
    gh_ref[...] = grad
    low = grad.astype(BF)
    total = None
    ob_wide = ob_ref[...]
    for index in range(narrow):
        piece = low[:, index * d_pad : (index + 1) * d_pad]
        part = dot(piece, blocks[index], NT)
        total = part if total is None else total + part
        term = dot(ob_wide, piece, TN).reshape(wide, r_w, d_pad)
        row = gain_term[:, index * d_pad : (index + 1) * d_pad]
        ref = (own_terms, other_terms)[index // pair]
        ref[index % pair] = (term + jnp.where(here, row, 0.0)[None]).astype(BF)
    for p in range(wide):
        e_blocks[w_order[p]] = total[:, p * r_w : (p + 1) * r_w]
    go_ref[...] = side([e_blocks[w][:, :d_w] for w in range(wide)]).astype(BF)


def attend_back_kernel(
    bucket, w_order, n_order, lengths, q_ref, k_ref, v_ref, ob_ref, go_ref, p_ref, cos_ref, sin_ref, gq_ref, gk_ref, gv_ref, gq_sum, gk_sum, gv_sum
):
    rows = q_ref.shape[1]
    step = 128
    group = QUERY_HEADS // KEY_VALUE_HEADS
    head = HEAD_WIDTH
    for g in range(KEY_VALUE_HEADS):
        offset = 0
        lanes = slice(g * head, (g + 1) * head)
        gk_total, gv_total = [], []
        for i in range(rows // step):
            upto = (i + 1) * step

            def stacked(ref, *at):
                return jnp.concatenate(
                    [
                        ref[(*at, slice(i * step, upto), slice((g * group + j) * head, (g * group + j + 1) * head))]
                        for j in range(group)
                    ],
                    axis=0,
                )

            queries, out_grads, outs = stacked(q_ref, bucket), stacked(go_ref, bucket), stacked(ob_ref)
            keys = k_ref[bucket, :upto, lanes]
            values = v_ref[bucket, :upto, lanes]
            probs = p_ref[g, :, offset : offset + upto]
            delta = jnp.sum(out_grads.astype(F32) * outs.astype(F32), axis=1, keepdims=True)
            prob_grad = dot(out_grads, values, NT)
            logit_grad = (probs.astype(F32) * (prob_grad - delta)).astype(BF)
            query_part = dot(logit_grad, keys, NN) * head**-0.5
            gq_sum[i * step : upto, g * group * head : (g + 1) * group * head] = side(
                [query_part[j * step : (j + 1) * step] for j in range(group)]
            )
            key_part = dot(logit_grad, queries, TN)
            value_part = dot(probs, out_grads, TN)
            for j in range(i + 1):
                if j == i:
                    gk_total.append(key_part[j * step : (j + 1) * step])
                    gv_total.append(value_part[j * step : (j + 1) * step])
                else:
                    gk_total[j] += key_part[j * step : (j + 1) * step]
                    gv_total[j] += value_part[j * step : (j + 1) * step]
            offset += upto
        gk_sum[:, lanes] = jnp.concatenate(gk_total, axis=0)
        gv_sum[:, lanes] = jnp.concatenate(gv_total, axis=0)
    cosine, sine = cos_ref[bucket], sin_ref[bucket]
    gq_ref[...] = turn(gq_sum[...], cosine, -sine).astype(BF)
    gk_ref[...] = turn(gk_sum[...], cosine, -sine).astype(BF)
    gv_ref[...] = gv_sum[...].astype(BF)


def weights_kernel(
    sizes, batches, w_order, n_order, lengths, tw_ref, a_ref, own_ref, other_ref, *refs
):
    wide, d_w, r_w, d_n, kv_n, pair, d_pad = sizes
    narrow = 2 * pair
    width = wide * d_w
    back_ref, own_terms, other_terms, g_blocks, gain_blocks, gain_wide = refs[3 * batches :]
    count = own_ref.shape[2]
    for b in range(batches):
        gq, gk, gv = [refs[kind * batches + b][...].astype(F32) for kind in range(3)]
        bucket = slice(b * gq.shape[0], (b + 1) * gq.shape[0])
        for n in range(narrow):
            piece = side(
                [
                    gq[:, n * d_n : (n + 1) * d_n],
                    gk[:, n * kv_n : (n + 1) * kv_n],
                    gv[:, n * kv_n : (n + 1) * kv_n],
                ]
            )
            if piece.shape[1] < count:
                piece = zeros_beside(piece, count, False)
            g_blocks[n, bucket] = piece.astype(BF)
    total = None
    for index in range(narrow):
        block = beside((own_ref, other_ref)[index // pair], index % pair)
        part = dot(g_blocks[n_order[index]], block, NN)
        total = part if total is None else total + part
    back_ref[...] = total
    field = tw_ref[...].astype(F32)
    scale = lax.rsqrt(mean_of(field * field, width) + EPS)
    gain_term = jnp.sum(total * (field * scale), axis=0, keepdims=True)
    for p in range(wide):
        gain_wide[w_order[p]] = gain_term[:, p * r_w : (p + 1) * r_w]
    gain_term = side([gain_wide[w][:, :d_w] for w in range(wide)])
    for n in range(narrow):
        gain_blocks[n] = zeros_beside(gain_term[:, n * d_n : (n + 1) * d_n], count, False)
    first = lax.broadcasted_iota(jnp.int32, (8, 1), 0) == 0
    lane = lax.broadcasted_iota(jnp.int32, (8, r_w), 1)
    chosen = jnp.where(first & (lane == d_w), 1.0, 0.0)
    a_wide = a_ref[...]
    for index in range(narrow):
        ref = (own_terms, other_terms)[index // pair]
        column = dot(jnp.broadcast_to(gain_blocks[n_order[index]], (8, count)), chosen, TN)
        term = dot(g_blocks[n_order[index]], a_wide, TN)
        for p in range(wide):
            ref[index % pair, p] = (term[:, p * r_w : (p + 1) * r_w] + column).astype(BF)


def outputs_kernel(
    sizes, batches, slots, w_order, n_order, lengths, hr_ref, mix_ref, gh_ref, tw_ref, back_ref, own_ref, other_ref,
    mixed_ref, grad_ref, n_blocks, d_blocks, gain_blocks, gain_wide,
):
    wide, d_w, r_w, d_n, kv_n, pair, d_pad = sizes
    narrow = 2 * pair
    width = wide * d_w
    rows = hr_ref.shape[0] // batches

    def natural(field):
        for index in range(narrow):
            n_blocks[n_order[index]] = field[:, index * d_pad : (index + 1) * d_pad]
        return side([n_blocks[n][:, d_pad - d_n :] for n in range(narrow)])

    inside = jnp.concatenate([places(lengths, b, slots, (rows, 1), 0)[2] for b in range(batches)], axis=0)
    mixed = natural(jnp.where(inside, hr_ref[...] + mix_ref[...], 0.0))
    for b in range(batches):
        mixed_ref[b] = mixed[b * rows : (b + 1) * rows].T.astype(BF)
    gain = gain_rows(sizes, own_ref, other_ref, n_order, gain_blocks)
    for w in range(wide):
        gain_wide[w] = zeros_beside(gain[:, w * d_w : (w + 1) * d_w], r_w, False)
    gain = side([gain_wide[w_order[p]] for p in range(wide)])
    field = tw_ref[...].astype(F32)
    scale = lax.rsqrt(mean_of(field * field, width) + EPS)
    normed = field * scale
    normed_grad = back_ref[...] * gain
    grad = scale * (normed_grad - normed * mean_of(normed_grad * normed, width))
    for p in range(wide):
        d_blocks[w_order[p]] = grad[:, p * r_w : (p + 1) * r_w]
    grad = side([d_blocks[w][:, :d_w] for w in range(wide)])
    grad = natural(gh_ref[...]) + grad
    for b in range(batches):
        grad_ref[b] = grad[b * rows : (b + 1) * rows].T.astype(BF)


VMEM = pl.BlockSpec(memory_space=pltpu.VMEM)
SMEM = pl.BlockSpec(memory_space=pltpu.SMEM)


def shaped(shape, dtype):
    return jax.ShapeDtypeStruct(shape, dtype)


def scratch(*shape, dtype=F32):
    return pltpu.VMEM(shape, dtype)


def call(name, kernel, operands, out_shapes, scratches, multiply_adds, megabytes, orders=(), transcendentals=0, aliases=None):
    return pl.pallas_call(
        kernel,
        in_specs=[SMEM] * len(orders) + [VMEM] * len(operands),
        out_specs=[VMEM] * len(out_shapes),
        out_shape=out_shapes,
        scratch_shapes=scratches,
        input_output_aliases=aliases or {},
        compiler_params=pltpu.CompilerParams(vmem_limit_bytes=megabytes * 1024 * 1024),
        cost_estimate=pl.CostEstimate(
            flops=2 * multiply_adds,
            bytes_accessed=sum(a.size * a.dtype.itemsize for a in list(operands) + list(out_shapes)),
            transcendentals=transcendentals,
        ),
        name=name,
    )(*orders, *operands)


FEED_MEGABYTES = 20


def feed_kernel(chained, rows_ref, grads_ref, own_ref, other_ref, *refs):
    before = refs[:2] if chained else ()
    mix_ref, back_ref, own_out, *other_out = refs[len(before) : -3]
    hidden, gate_part, up_part = refs[-3:]
    pair, wide = own_out.shape[:2]
    units, lanes = own_ref.shape[-2:]
    narrow = 2 * pair
    total = wide * units

    def weight(kind, lo=0, count=total):
        blocks = [
            (own_ref, other_ref)[index // pair][index % pair, :, kind].reshape(total, lanes)
            for index in range(narrow)
        ]
        return side([block[lo : lo + count] for block in blocks])

    rows_in = rows_ref[...]
    grad_in = grads_ref[...]
    step = 256
    for lo in range(0, total, step):
        gate_value = dot(rows_in, weight(0, lo, step), NT)
        up_value = dot(rows_in, weight(1, lo, step), NT)
        hidden_grad = dot(grad_in, weight(2, lo, step), NT)
        sigmoid_gate = 1.0 / (1.0 + jnp.exp(-gate_value))
        silu = gate_value * sigmoid_gate
        hidden[:, lo : lo + step] = (silu * up_value).astype(BF)
        gate_part[:, lo : lo + step] = (
            hidden_grad * up_value * (sigmoid_gate * (1.0 + gate_value * (1.0 - sigmoid_gate)))
        ).astype(BF)
        up_part[:, lo : lo + step] = (hidden_grad * silu).astype(BF)
    for kind, (left, right) in enumerate(((gate_part, rows_in), (up_part, rows_in), (hidden, grad_in))):
        term = dot(left[...], right, TN).astype(BF)
        for index in range(narrow):
            ref = own_out if index < pair else other_out[kind % len(other_out)]
            block = term[:, index * lanes : (index + 1) * lanes].reshape(wide, units, lanes)
            if index >= pair and len(other_out) > 1:
                ref[index % pair] = block
            elif len(ref.shape) == 5:
                ref[index % pair, :, kind] = block
            else:
                ref[index % pair, :, kind * units : (kind + 1) * units] = block
    mix = dot(hidden[...], weight(2), NN)
    mix_ref[...] = before[0][...] + mix if chained else mix
    back = dot(gate_part[...], weight(0), NN) + dot(up_part[...], weight(1), NN)
    back_ref[...] = before[1][...] + back if chained else back


def feed_call(rows_in, grad_in, own, other, before=(), flat=False):
    pair, wide, _, units, lanes = own.shape
    rows, width = rows_in.shape
    total = wide * units
    own_shape = (3 * units, lanes) if flat else (3, units, lanes)
    other_shapes = [own_shape] if flat else [(units, lanes)] * 3
    return call(
        "feed_forward",
        functools.partial(feed_kernel, bool(before)),
        (rows_in, grad_in, own, other, *before),
        [shaped((rows, width), F32)] * 2
        + [shaped((pair, wide, *shape), BF) for shape in [own_shape, *other_shapes]],
        [scratch(rows, total, dtype=BF)] * 3,
        9 * rows * width * total,
        FEED_MEGABYTES * total // 1024 + 2,
        transcendentals=rows * total,
        aliases={4: 0, 5: 1} if before else None,
    )


AXES = ("wide", "narrow")


class Grid:
    def __init__(self):
        self.wide = lax.axis_size("wide")
        self.narrow = lax.axis_size("narrow")
        self.outer = 4
        self.inner = self.wide // 4
        self.pair = self.narrow // 2
        self.size = {"outer": 4, "inner": self.inner, "pair": self.pair, "core": 2}
        self.stride = {"outer": self.inner * self.narrow, "inner": self.narrow, "pair": 2, "core": 1}
        linear = lax.axis_index("wide") * self.narrow + lax.axis_index("narrow")
        self.at = {name: (linear // self.stride[name]) % self.size[name] for name in self.size}

    def shift(self, value, name, count=1):
        size, stride = self.size[name], self.stride[name]
        pairs = []
        for source in range(self.wide * self.narrow):
            digit = (source // stride) % size
            pairs.append((source, source + ((digit + count) % size - digit) * stride))
        return lax.ppermute(value, AXES, pairs)

    def behind(self, name, steps):
        return (self.at[name] + (self.size[name] - steps)) % self.size[name]


def after(value, others):
    if not others:
        return value
    return lax.optimization_barrier((value, *others))[0]


class Flow:
    def __init__(self, make, grid, *args):
        self.grid = grid
        self.gates = ()
        self.last = ()
        self.result = None
        self.more = ()
        self.run = make(self, *args)

    def step(self, *others):
        self.gates = others
        try:
            self.last = next(self.run)
        except StopIteration as stop:
            self.result = stop.value
            return self.result
        return None

    def finish(self):
        while self.result is None:
            self.step()
        return self.result

    def shift(self, value, name, count=1):
        return self.grid.shift(after(value, self.gates), name, count)

    def settle(self, value):
        return after(value, self.gates)


class Clock:
    def __init__(self):
        self.held = ()

    def now(self, value):
        return after(value, self.held)

    def phase(self, *starts, done=(), wait=(), leave=()):
        gates = self.held + tuple(done)
        for flow, steps in starts:
            for _ in range(steps):
                flow.step(*gates)
        flows = [flow for flow, _ in starts if flow not in leave] + list(wait)
        held = sum([tuple(flow.last) for flow in flows], tuple(done))
        if not starts:
            held = self.held + held
        self.held = held if held else self.held


def both_rings(flow, first, first_name, second, second_name):
    one, two = [first], [second]
    for at in range(max(flow.grid.size[first_name], flow.grid.size[second_name]) - 1):
        if at < flow.grid.size[first_name] - 1:
            one.append(flow.shift(one[-1], first_name))
        if at < flow.grid.size[second_name] - 1:
            two.append(flow.shift(two[-1], second_name))
        yield (one[-1], two[-1])
        if at < flow.grid.size[first_name] - 1:
            one[-1] = flow.settle(one[-1])
        if at < flow.grid.size[second_name] - 1:
            two[-1] = flow.settle(two[-1])
    return one, two


def gather_outer(flow, shard):
    moved = [flow.shift(shard, "outer", count) for count in range(1, flow.grid.outer)]
    yield tuple(moved)
    return [shard] + [flow.settle(block) for block in moved]


def gather_ring(flow, shard):
    blocks = [shard]
    for _ in range(flow.grid.outer - 1):
        blocks.append(flow.shift(blocks[-1], "outer"))
        yield (blocks[-1],)
        blocks[-1] = flow.settle(blocks[-1])
    return blocks


def gather_plane(flow, blocks, cut):
    stacked = lax.optimization_barrier(jnp.stack(blocks))
    first, second = stacked[..., :cut, :], stacked[..., cut:, :]
    one, two = yield from both_rings(flow, first, "inner", second, "pair")
    one, two = yield from both_rings(flow, jnp.concatenate(one), "pair", jnp.stack(two), "inner")
    own = jnp.concatenate([jnp.stack(one), jnp.concatenate(two, axis=1)], axis=-2)
    other = flow.shift(own, "core")
    yield (other,)
    return own, other


def both_sums(flow, first, first_name, second, second_name):
    sizes = flow.grid.size
    one, two = first(1), second(1)
    for step in range(1, max(sizes[first_name], sizes[second_name])):
        moved = []
        if step < sizes[first_name]:
            one = flow.shift(one, first_name)
            moved.append(one)
        if step < sizes[second_name]:
            two = flow.shift(two, second_name)
            moved.append(two)
        yield tuple(moved)
        if step < sizes[first_name]:
            one = flow.settle(one) + first((step + 1) % sizes[first_name])
        if step < sizes[second_name]:
            two = flow.settle(two) + second((step + 1) % sizes[second_name])
    return one, two


def scatter_plane(flow, own, other, cut):
    outer = flow.grid.outer
    if isinstance(other, tuple):
        moved = tuple(flow.shift(part, "core") for part in other)
        yield moved
        moved = jnp.stack([flow.settle(part) for part in moved], axis=2)
    else:
        moved = flow.shift(other, "core")
        yield (moved,)
        moved = flow.settle(moved)
    more = None
    if flow.more:
        more = flow.shift(flow.more[1], "core")
        yield (more,)
        more = flow.settle(more)

    def wide_part(r):
        return slice(r * outer, (r + 1) * outer)

    def first(r):
        return moved[r, ..., :cut, :] + own[r, ..., :cut, :]

    def second(r):
        block = moved[:, wide_part(r), ..., cut:, :] + own[:, wide_part(r), ..., cut:, :]
        if more is None:
            return block
        return jnp.concatenate([block, more[:, wide_part(r)] + flow.more[0][:, wide_part(r)]], axis=-2)

    one, two = yield from both_sums(flow, first, "pair", second, "inner")
    one, two = yield from both_sums(
        flow, lambda r: one[wide_part(r)], "inner", lambda r: two[r], "pair"
    )
    return jnp.concatenate([one, two], axis=-2)


def scatter_outer(flow, sums):
    outer = flow.grid.outer
    moved = [flow.shift(sums[r], "outer", outer - r) for r in range(1, outer)]
    yield tuple(moved)
    return sum([flow.settle(block).astype(F32) for block in moved], sums[0].astype(F32))


def scatter_ring(flow, sums):
    outer = flow.grid.outer
    total = sums[1]
    for step in range(1, outer):
        total = flow.shift(total, "outer")
        yield (total,)
        total = flow.settle(total).astype(F32) + sums[(step + 1) % outer].astype(F32)
        if step < outer - 1:
            total = total.astype(BF)
    return total


def rounded_up(count, step):
    return -(-count // step) * step
GRANTS = {
    "prepare_narrow": 16,
    "prepare_wide": 12,
    "project": 24,
    "attend": 12,
    "residual": 20,
    "middle": 24,
    "attend_back": 20,
    "weights": 28,
    "outputs": 28,
}


def body(
    tokens,
    lengths,
    cotangent,
    query_weight,
    key_matrix,
    value_matrix,
    output_weight,
    gate_weight,
    up_weight,
    down_weight,
    attention_gain,
    feedforward_gain,
):
    grid = Grid()
    batches, bucket_rows, width = tokens.shape
    rows = batches * bucket_rows
    wide, narrow, pair, inner, outer = grid.wide, grid.narrow, grid.pair, grid.inner, grid.outer
    d_w, d_n = query_weight.shape
    kv_n = key_matrix.shape[1]
    f_w = down_weight.shape[0]
    d_pad = rounded_up(d_n, 128)
    r_w = rounded_up(d_w + 1, 64)
    taken = d_n + 2 * kv_n
    t_rows = rounded_up(taken, 16)
    sizes = (wide, d_w, r_w, d_n, kv_n, pair, d_pad)

    packed = jnp.concatenate([query_weight.T, key_matrix.T, value_matrix.T], axis=0)
    gain_column = jnp.concatenate([attention_gain, jnp.zeros((2 * kv_n,), BF)])[:, None]
    packed = jnp.concatenate([packed, gain_column, jnp.zeros((taken, r_w - d_w - 1), BF)], axis=1)
    a_shard = jnp.pad(packed, ((0, t_rows - taken), (0, 0)))
    a_cut = rounded_up(t_rows // 2, 16)
    o_shard = jnp.concatenate([output_weight, feedforward_gain[None], jnp.zeros((r_w - d_w - 1, d_n), BF)])
    f_shard = jnp.stack([gate_weight.T, up_weight.T, down_weight])
    sub = 256 // wide
    tiles_in = f_w // sub
    bounds = [0, 4 * tiles_in // 10 * sub, f_w]
    shards = [f_shard[:, lo:hi] for lo, hi in zip(bounds, bounds[1:])]
    shards[0] = jnp.concatenate([shards[0], o_shard[None]])
    shards = [jnp.pad(shard, ((0, 0), (0, 0), (d_pad - d_n, 0))) for shard in shards]
    cuts = [shard.shape[1] // 2 for shard in shards]

    place = jnp.arange(wide, dtype=jnp.int32)
    w_order = (grid.at["outer"] - place % outer) % outer * inner
    w_order = (w_order + (grid.at["inner"] - place // outer) % inner).astype(jnp.int32)
    place = jnp.arange(narrow, dtype=jnp.int32)
    n_order = (grid.at["pair"] - place % pair) % pair * 2
    n_order = (n_order + (grid.at["core"] - place // pair) % 2).astype(jnp.int32)
    slots = lengths.shape[2]
    orders = (w_order, n_order, lengths.reshape(-1))
    freqs = THETA ** (-jnp.arange(HEAD_WIDTH // 2, dtype=F32) * 2.0 / HEAD_WIDTH)
    freqs = jnp.concatenate([freqs] * 4)[None]

    flow_za = Flow(gather_outer, grid, a_shard)
    flow_z1 = Flow(gather_ring, grid, shards[0])
    flow_z2 = Flow(gather_ring, grid, shards[1])
    plane = max(inner, pair) - 1
    clock = Clock()
    clock.phase((flow_za, 1), (flow_z1, 1), leave=(flow_za, flow_z1))
    token_rows = tokens.reshape(rows, width)
    cotangent_rows = cotangent.reshape(rows, width)
    token_narrow, branch_grad = call(
        "prepare_narrow",
        functools.partial(prepare_narrow_kernel, sizes, batches, slots),
        (token_rows, cotangent_rows),
        [shaped((rows, narrow * d_pad), BF)] * 2,
        [scratch(narrow, rows, d_pad, dtype=BF)] * 2,
        0,
        GRANTS["prepare_narrow"],
        orders=orders,
    )
    clock.phase(done=(token_narrow,), wait=(flow_za, flow_z1))
    flow_a = Flow(gather_plane, grid, flow_za.finish(), a_cut)
    clock.phase((flow_a, plane), (flow_z1, 1), leave=(flow_a, flow_z1))
    token_wide, cosine, sine = call(
        "prepare_wide",
        functools.partial(prepare_wide_kernel, sizes, batches, slots),
        (clock.now(token_rows), freqs),
        [shaped((rows, wide * r_w), BF), shaped((rows, 128), F32), shaped((rows, 128), F32)],
        [scratch(wide, rows, r_w, dtype=BF)],
        0,
        GRANTS["prepare_wide"],
        orders=orders,
    )
    clock.phase(done=(token_wide,), wait=(flow_a, flow_z1))
    clock.phase((flow_a, plane), (flow_z1, 1))
    flow_1 = Flow(gather_plane, grid, flow_z1.finish(), cuts[0])
    clock.phase((flow_a, 1), (flow_1, plane), (flow_z2, 1), leave=(flow_1, flow_z2))
    a_own, a_other = flow_a.finish()
    a_in, query, key, value = call(
        "project",
        functools.partial(project_kernel, sizes),
        (clock.now(token_wide), cosine, sine, a_own, a_other),
        [
            shaped((rows, wide * r_w), BF),
            shaped((rows, QUERY_HEADS * HEAD_WIDTH), BF),
            shaped((rows, KEY_VALUE_HEADS * HEAD_WIDTH), BF),
            shaped((rows, KEY_VALUE_HEADS * HEAD_WIDTH), BF),
        ],
        [scratch(narrow, rows, t_rows), scratch(narrow, 1, t_rows), scratch(wide, 1, r_w)],
        rows * wide * r_w * narrow * t_rows,
        GRANTS["project"],
        orders=orders,
    )

    clock.phase(done=(query,), wait=(flow_1, flow_z2))
    clock.phase((flow_1, plane), (flow_z2, 1), leave=(flow_1, flow_z2))

    def by_bucket(field):
        return field.reshape(batches, bucket_rows, field.shape[-1])

    group = QUERY_HEADS // KEY_VALUE_HEADS
    steps = bucket_rows // 128
    p_shape = (KEY_VALUE_HEADS, group * 128, 128 * steps * (steps + 1) // 2)
    query, key, value = by_bucket(query), by_bucket(key), by_bucket(value)
    pair_work = QUERY_HEADS * bucket_rows * bucket_rows * HEAD_WIDTH
    attended, probs = [], []
    for b in range(batches):
        parts = call(
            "attend",
            functools.partial(attend_kernel, slots, b),
            (clock.now(query), key, value),
            [shaped(query.shape[1:], BF), shaped(p_shape, BF)],
            [],
            6 * pair_work,
            GRANTS["attend"],
            orders=orders,
            transcendentals=QUERY_HEADS * bucket_rows * bucket_rows,
        )
        attended.append(parts[0])
        probs.append(parts[1])
        if b < batches - 1:
            clock.phase(done=(parts[0],), wait=(flow_z2,))
            clock.phase((flow_z2, 1), leave=(flow_z2,))
    clock.phase(done=tuple(attended), wait=(flow_1, flow_z2))
    flow_2 = Flow(gather_plane, grid, flow_z2.finish(), cuts[1])
    clock.phase((flow_1, 1), (flow_2, plane), leave=(flow_2,))
    first_own, first_other = flow_1.finish()
    o_operands = (first_own[:, :, 3], first_other[:, :, 3])
    d_lanes = narrow * d_pad
    attended_wide, residual, feed_in = call(
        "residual",
        functools.partial(residual_kernel, sizes, batches),
        (clock.now(token_narrow), *o_operands, *attended),
        [
            shaped((rows, wide * r_w), BF),
            shaped((rows, d_lanes), F32),
            shaped((rows, d_lanes), BF),
        ],
        [scratch(wide, rows, r_w, dtype=BF)],
        rows * wide * r_w * d_lanes,
        GRANTS["residual"],
        orders=orders,
    )

    clock.phase(done=(feed_in,), wait=(flow_2,))
    clock.phase((flow_2, plane), leave=(flow_2,))
    *sums_so_far, own_terms, gate_terms, up_terms, down_terms = feed_call(
        clock.now(feed_in), branch_grad, first_own, first_other
    )
    back_1 = Flow(scatter_plane, grid, own_terms, (gate_terms, up_terms, down_terms), cuts[0])
    clock.phase(done=(own_terms,))
    clock.phase((back_1, 1), wait=(flow_2,))
    clock.phase((flow_2, 1), (back_1, plane), leave=(back_1,))
    *sums_so_far, own_terms, other_terms = feed_call(
        clock.now(feed_in), branch_grad, *flow_2.finish(), tuple(sums_so_far), True
    )
    back_2 = Flow(
        scatter_plane,
        grid,
        own_terms,
        other_terms,
        rounded_up((own_terms.shape[2] + r_w) // 2, 16),
    )
    clock.phase(done=(own_terms,), wait=(back_1,))
    clock.phase((back_1, plane), (back_2, 1), leave=(back_1, back_2))
    mix, back = sums_so_far
    grad, attended_grad, own_o, other_o = call(
        "middle",
        functools.partial(middle_kernel, sizes),
        (clock.now(residual), back, branch_grad, attended_wide) + o_operands,
        [
            shaped((rows, d_lanes), F32),
            shaped((rows, width), BF),
            shaped((pair, wide, r_w, d_pad), BF),
            shaped((pair, wide, r_w, d_pad), BF),
        ],
        [scratch(wide, rows, r_w)],
        2 * rows * wide * r_w * d_lanes,
        GRANTS["middle"],
        orders=orders,
    )
    clock.phase(done=(attended_grad,), wait=(back_1, back_2))
    back_2.more = (own_o, other_o)
    clock.phase((back_2, 1))
    back_z1 = Flow(scatter_ring, grid, back_1.finish())
    clock.phase((back_2, plane), (back_z1, 1), leave=(back_2, back_z1))
    by_parts = (by_bucket(attended_grad), by_bucket(cosine), by_bucket(sine))
    shapes = [x.shape[1:] for x in (query, key, value)]
    grads = []
    for b in range(batches):
        grads.append(
            call(
                "attend_back",
                functools.partial(attend_back_kernel, b),
                (clock.now(query), key, value, attended[b], by_parts[0], probs[b], *by_parts[1:]),
                [shaped(shape, BF) for shape in shapes],
                [scratch(*shape) for shape in shapes],
                12 * pair_work,
                GRANTS["attend_back"],
                orders=orders,
            )
        )
        if b < batches - 1:
            clock.phase(done=tuple(grads[b][:1]), wait=(back_z1,))
            clock.phase((back_z1, 1), leave=(back_z1,))
    clock.phase(done=tuple(x[0] for x in grads), wait=(back_2, back_z1))
    clock.phase((back_2, plane), (back_z1, 1), leave=(back_2, back_z1))
    operands = tuple(x for parts in zip(*grads) for x in parts)
    wide_back, own_terms, other_terms = call(
        "weights",
        functools.partial(weights_kernel, sizes, batches),
        (clock.now(token_wide), a_in, a_own, a_other) + operands,
        [shaped((rows, wide * r_w), F32)] + [shaped(a_own.shape, BF)] * 2,
        [scratch(narrow, rows, t_rows, dtype=BF), scratch(narrow, 1, t_rows), scratch(wide, 1, r_w)],
        2 * rows * wide * r_w * narrow * t_rows,
        GRANTS["weights"],
        orders=orders,
    )
    back_a = Flow(scatter_plane, grid, own_terms, other_terms, a_cut)
    clock.phase(done=(own_terms,), wait=(back_2, back_z1))
    clock.phase((back_a, 1))
    back_z2 = Flow(scatter_ring, grid, back_2.finish())
    clock.phase((back_a, plane), (back_z2, 1), leave=(back_a, back_z2))
    mixed, tokens_grad = call(
        "outputs",
        functools.partial(outputs_kernel, sizes, batches, slots),
        (clock.now(residual), mix, grad, token_wide, wide_back, a_own, a_other),
        [shaped((batches, width, bucket_rows), BF)] * 2,
        [
            scratch(narrow, rows, d_pad),
            scratch(wide, rows, r_w),
            scratch(narrow, 1, t_rows),
            scratch(wide, 1, r_w),
        ],
        0,
        GRANTS["outputs"],
        orders=orders,
    )
    clock.phase(done=(mixed,), wait=(back_a, back_z2))
    clock.phase((back_a, plane), (back_z2, 1))
    back_za = Flow(scatter_outer, grid, back_a.finish())
    clock.phase((back_z2, 1), (back_za, 1), leave=(back_z2, back_za))
    a_sum = back_za.finish()
    rest = back_z2.finish()
    o_sum = rest[rest.shape[0] - r_w :]
    rest = rest[: rest.shape[0] - r_w].reshape(3, -1, d_pad)
    feed_sum = jnp.concatenate([back_z1.finish(), rest], axis=1)[:, :, d_pad - d_n :]
    return (
        jnp.swapaxes(mixed, 1, 2),
        jnp.swapaxes(tokens_grad, 1, 2),
        a_sum[:d_n, :d_w].T,
        a_sum[d_n : d_n + kv_n, :d_w].T,
        a_sum[d_n + kv_n : taken, :d_w].T,
        o_sum[:d_w, d_pad - d_n :],
        feed_sum[0].T,
        feed_sum[1].T,
        feed_sum[2],
        a_sum[:d_n, d_w],
        o_sum[d_w, d_pad - d_n :],
    )


def solution(mesh):
    in_specs = (
        P(None, ("wide", "narrow"), None),
        P(None, ("wide", "narrow"), None),
        P(None, ("wide", "narrow"), None),
        P("wide", "narrow"),
        P("wide", "narrow"),
        P("wide", "narrow"),
        P("wide", "narrow"),
        P("narrow", "wide"),
        P("narrow", "wide"),
        P("wide", "narrow"),
        P("narrow"),
        P("narrow"),
    )
    out_specs = (
        P(None, ("wide", "narrow"), None),
        P(None, ("wide", "narrow"), None),
        P("wide", "narrow"),
        P("wide", "narrow"),
        P("wide", "narrow"),
        P("wide", "narrow"),
        P("narrow", "wide"),
        P("narrow", "wide"),
        P("wide", "narrow"),
        P("narrow"),
        P("narrow"),
    )
    return jax.shard_map(body, mesh=mesh, in_specs=in_specs, out_specs=out_specs, check_vma=False)
```

```python
import functools

import jax
import jax.numpy as jnp
from jax import lax
from jax.experimental import pallas as pl
from jax.experimental.pallas import tpu as pltpu
from jax.sharding import PartitionSpec as P

QUERY_HEADS = 15
KEY_VALUE_HEADS = 5
HEAD_WIDTH = 64


EPS = 1e-05
THETA = 10000.0


def segments_of(lengths_row, count_of_rows):
    ends = jnp.cumsum(lengths_row, dtype=jnp.int32)
    starts = ends - lengths_row
    places = jnp.arange(count_of_rows, dtype=jnp.int32)
    segment = jnp.sum((places[:, None] >= ends[None, :]).astype(jnp.int32), axis=1, dtype=jnp.int32)
    slot_ids = jnp.arange(lengths_row.shape[0], dtype=jnp.int32)
    opening = jnp.sum(
        jnp.where(segment[:, None] == slot_ids[None, :], starts[None, :], 0),
        axis=1,
        dtype=jnp.int32,
    )
    opening = jnp.where(segment == lengths_row.shape[0], ends[-1], opening)
    return (segment, places - opening)


F32 = jnp.float32
BF = jnp.bfloat16
NT = (((1,), (1,)), ((), ()))
TN = (((0,), (0,)), ((), ()))
NN = (((1,), (0,)), ((), ()))


def dot(left, right, dims):
    return lax.dot_general(left, right, dims, preferred_element_type=F32)


def side(parts):
    return parts[0] if len(parts) == 1 else jnp.concatenate(parts, axis=1)


def mean_of(field, width):
    return jnp.sum(field, axis=1, keepdims=True) * (1.0 / width)


def row_of(block, row):
    at = lax.broadcasted_iota(jnp.int32, (block.shape[0], 1), 0)
    return jnp.sum(jnp.where(at == row, block.astype(F32), 0.0), axis=0, keepdims=True)


def zeros_beside(field, lanes, before):
    pad = jnp.zeros((field.shape[0], lanes - field.shape[1]), field.dtype)
    return side([pad, field] if before else [field, pad])


def turn(field, cosine, sine):
    lane = lax.broadcasted_iota(jnp.int32, (1, 128), 1)
    low = (lane % 64) < 32
    tiles = []
    for start in range(0, field.shape[1], 128):
        piece = field[:, start : start + 128]
        count = piece.shape[1]
        if count < 128:
            piece = zeros_beside(piece, 128, False)
        other = jnp.where(low, pltpu.roll(piece, 96, 1), pltpu.roll(piece, 32, 1))
        tiles.append((piece * cosine + other * sine)[:, :count])
    return side(tiles)


def places(lengths, bucket, slots, shape, axis):
    at = lax.broadcasted_iota(jnp.int32, shape, axis)
    end = jnp.int32(0)
    segment = jnp.zeros(shape, jnp.int32)
    opening = jnp.zeros(shape, jnp.int32)
    for slot in range(slots):
        length = lengths[bucket * slots + slot]
        end = end + length
        over = at >= end
        segment += jnp.where(over, 1, 0)
        opening += jnp.where(over, length, 0)
    return segment, at - opening, segment < slots


def prepare_narrow_kernel(sizes, batches, slots, w_order, n_order, lengths, tok_ref, cot_ref, tn_ref, gf_ref, n_blocks, c_blocks):
    wide, d_w, r_w, d_n, kv_n, pair, d_pad = sizes
    narrow = 2 * pair
    rows = tok_ref.shape[0] // batches
    for b in range(batches):
        part = slice(b * rows, (b + 1) * rows)
        _, _, inside = places(lengths, b, slots, (rows, 1), 0)
        field = tok_ref[part].astype(F32)
        upstream = jnp.where(inside, cot_ref[part].astype(F32), 0.0)
        for n in range(narrow):
            n_blocks[n, part] = zeros_beside(field[:, n * d_n : (n + 1) * d_n], d_pad, True).astype(BF)
            c_blocks[n, part] = zeros_beside(upstream[:, n * d_n : (n + 1) * d_n], d_pad, True).astype(BF)
    tn_ref[...] = side([n_blocks[n_order[index]] for index in range(narrow)])
    gf_ref[...] = side([c_blocks[n_order[index]] for index in range(narrow)])


def prepare_wide_kernel(sizes, batches, slots, w_order, n_order, lengths, tok_ref, freq_ref, tw_ref, cos_ref, sin_ref, w_blocks):
    wide, d_w, r_w, d_n, kv_n, pair, d_pad = sizes
    rows = tok_ref.shape[0] // batches
    field = tok_ref[...].astype(F32)
    for w in range(wide):
        w_blocks[w] = zeros_beside(field[:, w * d_w : (w + 1) * d_w], r_w, False).astype(BF)
    tw_ref[...] = side([w_blocks[w_order[p]] for p in range(wide)])
    sign = jnp.where(lax.broadcasted_iota(jnp.int32, (1, 128), 1) % 64 < 32, -1.0, 1.0)
    for b in range(batches):
        part = slice(b * rows, (b + 1) * rows)
        _, position, _ = places(lengths, b, slots, (rows, 1), 0)
        angle = position.astype(F32) * freq_ref[...]
        cos_ref[part] = jnp.cos(angle)
        sin_ref[part] = jnp.sin(angle) * sign


def beside(ref, at):
    return side([ref[at, p] for p in range(ref.shape[1])])


def gain_rows(sizes, own_ref, other_ref, n_order, gain_blocks):
    wide, d_w, r_w, d_n, kv_n, pair, d_pad = sizes
    lane = lax.broadcasted_iota(jnp.int32, (16, r_w), 1)
    chosen = jnp.where(lane == d_w, 1.0, 0.0).astype(BF)
    for index in range(2 * pair):
        block = (own_ref, other_ref)[index // pair][index % pair, 0]
        gain_blocks[n_order[index]] = dot(chosen, block, NT)[:1]
    return side([gain_blocks[n][:, :d_n] for n in range(2 * pair)])


def project_kernel(
    sizes, w_order, n_order, lengths, tw_ref, cos_ref, sin_ref, own_ref, other_ref,
    a_ref, q_ref, k_ref, v_ref, projected, gain_blocks, gain_wide,
):
    wide, d_w, r_w, d_n, kv_n, pair, d_pad = sizes
    narrow = 2 * pair
    width = wide * d_w
    gain = gain_rows(sizes, own_ref, other_ref, n_order, gain_blocks)
    for w in range(wide):
        gain_wide[w] = zeros_beside(gain[:, w * d_w : (w + 1) * d_w], r_w, False)
    field = tw_ref[...].astype(F32)
    scale = lax.rsqrt(mean_of(field * field, width) + EPS)
    a_wide = (field * scale * side([gain_wide[w_order[p]] for p in range(wide)])).astype(BF)
    a_ref[...] = a_wide
    for index in range(narrow):
        block = beside((own_ref, other_ref)[index // pair], index % pair)
        projected[n_order[index]] = dot(a_wide, block, NT)
    cosine, sine = cos_ref[...], sin_ref[...]

    def taken(start, count):
        return side([projected[n][:, start : start + count] for n in range(narrow)])

    q_ref[...] = (turn(taken(0, d_n), cosine, sine) * HEAD_WIDTH**-0.5).astype(BF)
    k_ref[...] = turn(taken(d_n, kv_n), cosine, sine).astype(BF)
    v_ref[...] = taken(d_n + kv_n, kv_n).astype(BF)


def attend_kernel(slots, bucket, w_order, n_order, lengths, q_ref, k_ref, v_ref, ob_ref, p_ref):
    rows = q_ref.shape[1]
    seg_row, _, _ = places(lengths, bucket, slots, (1, rows), 1)
    seg_col, _, _ = places(lengths, bucket, slots, (rows, 1), 0)
    step = 128
    group = QUERY_HEADS // KEY_VALUE_HEADS
    head = HEAD_WIDTH
    offset = 0
    for i in range(rows // step):
        upto = (i + 1) * step
        query_at = i * step + lax.broadcasted_iota(jnp.int32, (step, upto), 0)
        key_at = lax.broadcasted_iota(jnp.int32, (step, upto), 1)
        same = seg_col[i * step : upto] == seg_row[:, :upto]
        bias = jnp.where(same & (key_at <= query_at), 0.0, -1000000000.0)
        for g in range(KEY_VALUE_HEADS):
            queries = jnp.concatenate(
                [
                    q_ref[bucket, i * step : upto, (g * group + j) * head : (g * group + j + 1) * head]
                    for j in range(group)
                ],
                axis=0,
            )
            keys = k_ref[bucket, :upto, g * head : (g + 1) * head]
            values = v_ref[bucket, :upto, g * head : (g + 1) * head]
            logits = dot(queries, keys, NT).reshape(group, step, upto) + bias[None]
            peak = jnp.max(logits, axis=-1, keepdims=True)
            shifted = jnp.exp(logits - peak)
            total = jnp.sum(shifted, axis=-1, keepdims=True)
            probs = (shifted * (1.0 / total)).astype(BF).reshape(group * step, upto)
            p_ref[g, :, offset : offset + upto] = probs
            out = dot(probs, values, NN).astype(BF)
            ob_ref[i * step : upto, g * group * head : (g + 1) * group * head] = side(
                [out[j * step : (j + 1) * step] for j in range(group)]
            )
        offset += upto


def residual_kernel(
    sizes, batches, w_order, n_order, lengths, tn_ref, own_ref, other_ref, *refs
):
    ob_wide_ref, hr_ref, bf_ref, e_blocks = refs[batches:]
    wide, d_w, r_w, d_n, kv_n, pair, d_pad = sizes
    narrow = 2 * pair
    spare = d_w // 16 * 16
    width = wide * d_w
    attended = jnp.concatenate([ref[...].astype(F32) for ref in refs[:batches]], axis=0)
    for w in range(wide):
        e_blocks[w] = zeros_beside(attended[:, w * d_w : (w + 1) * d_w], r_w, False).astype(BF)
    ob_wide = side([e_blocks[w_order[p]] for p in range(wide)])
    ob_wide_ref[...] = ob_wide
    blocks = []
    gains = []
    for index in range(narrow):
        block = (own_ref, other_ref)[index // pair][index % pair].reshape(wide * r_w, d_pad)
        gains.append(row_of(block[spare : spare + 16], d_w - spare))
        rows_in = tn_ref[:, index * d_pad : (index + 1) * d_pad].astype(F32)
        blocks.append(rows_in + dot(ob_wide, block, NN))
    residual = side(blocks)
    hr_ref[...] = residual
    scale = lax.rsqrt(mean_of(residual * residual, width) + EPS)
    bf_ref[...] = (residual * scale * side(gains)).astype(BF)


def middle_kernel(
    sizes, w_order, n_order, lengths, hr_ref, back_ref, gf_ref, ob_ref, own_ref, other_ref,
    gh_ref, go_ref, own_terms, other_terms, e_blocks,
):
    wide, d_w, r_w, d_n, kv_n, pair, d_pad = sizes
    narrow = 2 * pair
    spare = d_w // 16 * 16
    width = wide * d_w
    residual = hr_ref[...]
    blocks = [
        (own_ref, other_ref)[index // pair][index % pair].reshape(wide * r_w, d_pad)
        for index in range(narrow)
    ]
    gain = side([row_of(block[spare : spare + 16], d_w - spare) for block in blocks])
    back = back_ref[...]
    scale = lax.rsqrt(mean_of(residual * residual, width) + EPS)
    normed = residual * scale
    gain_term = jnp.sum(back * normed, axis=0, keepdims=True)
    here = lax.broadcasted_iota(jnp.int32, (r_w, 1), 0) == d_w
    normed_grad = back * gain
    grad = gf_ref[...].astype(F32) + scale * (
        normed_grad - normed * mean_of(normed_grad * normed, width)
    )
    gh_ref[...] = grad
    low = grad.astype(BF)
    total = None
    ob_wide = ob_ref[...]
    for index in range(narrow):
        piece = low[:, index * d_pad : (index + 1) * d_pad]
        part = dot(piece, blocks[index], NT)
        total = part if total is None else total + part
        term = dot(ob_wide, piece, TN).reshape(wide, r_w, d_pad)
        row = gain_term[:, index * d_pad : (index + 1) * d_pad]
        ref = (own_terms, other_terms)[index // pair]
        ref[index % pair] = (term + jnp.where(here, row, 0.0)[None]).astype(BF)
    for p in range(wide):
        e_blocks[w_order[p]] = total[:, p * r_w : (p + 1) * r_w]
    go_ref[...] = side([e_blocks[w][:, :d_w] for w in range(wide)]).astype(BF)


def attend_back_kernel(
    bucket, w_order, n_order, lengths, q_ref, k_ref, v_ref, ob_ref, go_ref, p_ref, cos_ref, sin_ref, gq_ref, gk_ref, gv_ref, gq_sum, gk_sum, gv_sum
):
    rows = q_ref.shape[1]
    step = 128
    group = QUERY_HEADS // KEY_VALUE_HEADS
    head = HEAD_WIDTH
    for g in range(KEY_VALUE_HEADS):
        offset = 0
        lanes = slice(g * head, (g + 1) * head)
        gk_total, gv_total = [], []
        for i in range(rows // step):
            upto = (i + 1) * step

            def stacked(ref, *at):
                return jnp.concatenate(
                    [
                        ref[(*at, slice(i * step, upto), slice((g * group + j) * head, (g * group + j + 1) * head))]
                        for j in range(group)
                    ],
                    axis=0,
                )

            queries, out_grads, outs = stacked(q_ref, bucket), stacked(go_ref, bucket), stacked(ob_ref)
            keys = k_ref[bucket, :upto, lanes]
            values = v_ref[bucket, :upto, lanes]
            probs = p_ref[g, :, offset : offset + upto]
            delta = jnp.sum(out_grads.astype(F32) * outs.astype(F32), axis=1, keepdims=True)
            prob_grad = dot(out_grads, values, NT)
            logit_grad = (probs.astype(F32) * (prob_grad - delta)).astype(BF)
            query_part = dot(logit_grad, keys, NN) * head**-0.5
            gq_sum[i * step : upto, g * group * head : (g + 1) * group * head] = side(
                [query_part[j * step : (j + 1) * step] for j in range(group)]
            )
            key_part = dot(logit_grad, queries, TN)
            value_part = dot(probs, out_grads, TN)
            for j in range(i + 1):
                if j == i:
                    gk_total.append(key_part[j * step : (j + 1) * step])
                    gv_total.append(value_part[j * step : (j + 1) * step])
                else:
                    gk_total[j] += key_part[j * step : (j + 1) * step]
                    gv_total[j] += value_part[j * step : (j + 1) * step]
            offset += upto
        gk_sum[:, lanes] = jnp.concatenate(gk_total, axis=0)
        gv_sum[:, lanes] = jnp.concatenate(gv_total, axis=0)
    cosine, sine = cos_ref[bucket], sin_ref[bucket]
    gq_ref[...] = turn(gq_sum[...], cosine, -sine).astype(BF)
    gk_ref[...] = turn(gk_sum[...], cosine, -sine).astype(BF)
    gv_ref[...] = gv_sum[...].astype(BF)


def weights_kernel(
    sizes, batches, w_order, n_order, lengths, tw_ref, a_ref, own_ref, other_ref, *refs
):
    wide, d_w, r_w, d_n, kv_n, pair, d_pad = sizes
    narrow = 2 * pair
    width = wide * d_w
    back_ref, own_terms, *other_terms, g_blocks, gain_blocks, gain_wide = refs[3 * batches :]
    count = own_ref.shape[2]
    for b in range(batches):
        gq, gk, gv = [refs[kind * batches + b][...].astype(F32) for kind in range(3)]
        bucket = slice(b * gq.shape[0], (b + 1) * gq.shape[0])
        for n in range(narrow):
            piece = side(
                [
                    gq[:, n * d_n : (n + 1) * d_n],
                    gk[:, n * kv_n : (n + 1) * kv_n],
                    gv[:, n * kv_n : (n + 1) * kv_n],
                ]
            )
            if piece.shape[1] < count:
                piece = zeros_beside(piece, count, False)
            g_blocks[n, bucket] = piece.astype(BF)
    total = None
    for index in range(narrow):
        block = beside((own_ref, other_ref)[index // pair], index % pair)
        part = dot(g_blocks[n_order[index]], block, NN)
        total = part if total is None else total + part
    back_ref[...] = total
    field = tw_ref[...].astype(F32)
    scale = lax.rsqrt(mean_of(field * field, width) + EPS)
    gain_term = jnp.sum(total * (field * scale), axis=0, keepdims=True)
    for p in range(wide):
        gain_wide[w_order[p]] = gain_term[:, p * r_w : (p + 1) * r_w]
    gain_term = side([gain_wide[w][:, :d_w] for w in range(wide)])
    for n in range(narrow):
        gain_blocks[n] = zeros_beside(gain_term[:, n * d_n : (n + 1) * d_n], count, False)
    first = lax.broadcasted_iota(jnp.int32, (8, 1), 0) == 0
    lane = lax.broadcasted_iota(jnp.int32, (8, r_w), 1)
    chosen = jnp.where(first & (lane == d_w), 1.0, 0.0)
    a_wide = a_ref[...]
    for index in range(narrow):
        column = dot(jnp.broadcast_to(gain_blocks[n_order[index]], (8, count)), chosen, TN)
        term = dot(g_blocks[n_order[index]], a_wide, TN)
        for p in range(wide):
            block = (term[:, p * r_w : (p + 1) * r_w] + column).astype(BF)
            if index < pair:
                own_terms[index, p] = block
                continue
            start = 0
            for ref in other_terms:
                ref[index % pair, p] = block[start : start + ref.shape[2]]
                start += ref.shape[2]


def outputs_kernel(
    sizes, batches, slots, w_order, n_order, lengths, hr_ref, mix_ref, gh_ref, tw_ref, back_ref, own_ref, other_ref,
    mixed_ref, grad_ref, n_blocks, d_blocks, gain_blocks, gain_wide,
):
    wide, d_w, r_w, d_n, kv_n, pair, d_pad = sizes
    narrow = 2 * pair
    width = wide * d_w
    rows = hr_ref.shape[0] // batches

    def natural(field):
        for index in range(narrow):
            n_blocks[n_order[index]] = field[:, index * d_pad : (index + 1) * d_pad]
        return side([n_blocks[n][:, d_pad - d_n :] for n in range(narrow)])

    inside = jnp.concatenate([places(lengths, b, slots, (rows, 1), 0)[2] for b in range(batches)], axis=0)
    mixed = natural(jnp.where(inside, hr_ref[...] + mix_ref[...], 0.0))
    for b in range(batches):
        mixed_ref[b] = mixed[b * rows : (b + 1) * rows].T.astype(BF)
    gain = gain_rows(sizes, own_ref, other_ref, n_order, gain_blocks)
    for w in range(wide):
        gain_wide[w] = zeros_beside(gain[:, w * d_w : (w + 1) * d_w], r_w, False)
    gain = side([gain_wide[w_order[p]] for p in range(wide)])
    field = tw_ref[...].astype(F32)
    scale = lax.rsqrt(mean_of(field * field, width) + EPS)
    normed = field * scale
    normed_grad = back_ref[...] * gain
    grad = scale * (normed_grad - normed * mean_of(normed_grad * normed, width))
    for p in range(wide):
        d_blocks[w_order[p]] = grad[:, p * r_w : (p + 1) * r_w]
    grad = side([d_blocks[w][:, :d_w] for w in range(wide)])
    grad = natural(gh_ref[...]) + grad
    for b in range(batches):
        grad_ref[b] = grad[b * rows : (b + 1) * rows].T.astype(BF)


VMEM = pl.BlockSpec(memory_space=pltpu.VMEM)
SMEM = pl.BlockSpec(memory_space=pltpu.SMEM)


def shaped(shape, dtype):
    return jax.ShapeDtypeStruct(shape, dtype)


def scratch(*shape, dtype=F32):
    return pltpu.VMEM(shape, dtype)


def call(name, kernel, operands, out_shapes, scratches, multiply_adds, megabytes, orders=(), transcendentals=0, aliases=None, anywhere=0):
    out_specs = [VMEM] * (len(out_shapes) - anywhere) + [pl.BlockSpec(memory_space=pl.ANY)] * anywhere
    return pl.pallas_call(
        kernel,
        in_specs=[SMEM] * len(orders) + [VMEM] * len(operands),
        out_specs=out_specs,
        out_shape=out_shapes,
        scratch_shapes=scratches,
        input_output_aliases=aliases or {},
        compiler_params=pltpu.CompilerParams(vmem_limit_bytes=megabytes * 1024 * 1024),
        cost_estimate=pl.CostEstimate(
            flops=2 * multiply_adds,
            bytes_accessed=sum(a.size * a.dtype.itemsize for a in list(operands) + list(out_shapes)),
            transcendentals=transcendentals,
        ),
        name=name,
    )(*orders, *operands)


FEED_MEGABYTES = (18, 22)


def feed_kernel(chained, rows_ref, grads_ref, own_ref, other_ref, *refs):
    before = refs[:2] if chained else ()
    mix_ref, back_ref, own_out, *other_out = refs[len(before) : -3]
    hidden, gate_part, up_part = refs[-3:]
    pair, wide = own_out.shape[:2]
    units, lanes = own_ref.shape[-2:]
    narrow = 2 * pair
    total = wide * units

    def weight(kind, lo=0, count=total):
        blocks = [
            (own_ref, other_ref)[index // pair][index % pair, :, kind].reshape(total, lanes)
            for index in range(narrow)
        ]
        return side([block[lo : lo + count] for block in blocks])

    rows_in = rows_ref[...]
    grad_in = grads_ref[...]
    step = 256
    for lo in range(0, total, step):
        gate_value = dot(rows_in, weight(0, lo, step), NT)
        up_value = dot(rows_in, weight(1, lo, step), NT)
        hidden_grad = dot(grad_in, weight(2, lo, step), NT)
        sigmoid_gate = 1.0 / (1.0 + jnp.exp(-gate_value))
        silu = gate_value * sigmoid_gate
        hidden[:, lo : lo + step] = (silu * up_value).astype(BF)
        gate_part[:, lo : lo + step] = (
            hidden_grad * up_value * (sigmoid_gate * (1.0 + gate_value * (1.0 - sigmoid_gate)))
        ).astype(BF)
        up_part[:, lo : lo + step] = (hidden_grad * silu).astype(BF)
    part = max(wide // 4, 1)
    for kind, (left, right) in enumerate(((gate_part, rows_in), (up_part, rows_in), (hidden, grad_in))):
        for first in range(0, wide, part):
            term = dot(left[:, first * units : (first + part) * units], right, TN).astype(BF)
            for index in range(narrow):
                ref = own_out if index < pair else other_out[kind % len(other_out)]
                block = term[:, index * lanes : (index + 1) * lanes].reshape(part, units, lanes)
                to = slice(first, first + part)
                if len(ref.shape) == 5:
                    ref[index % pair, to, kind] = block
                elif ref.shape[2] == units:
                    ref[index % pair, to] = block
                else:
                    ref[index % pair, to, kind * units : (kind + 1) * units] = block
    mix = dot(hidden[...], weight(2), NN)
    mix_ref[...] = before[0][...] + mix if chained else mix
    back = dot(gate_part[...], weight(0), NN) + dot(up_part[...], weight(1), NN)
    back_ref[...] = before[1][...] + back if chained else back


def feed_call(rows_in, grad_in, own, other, before=(), flat=False):
    pair, wide, _, units, lanes = own.shape
    rows, width = rows_in.shape
    total = wide * units
    own_shape = (3 * units, lanes) if flat else (3, units, lanes)
    other_shapes = [own_shape] if flat else [(units, lanes)] * 3
    return call(
        "feed_forward",
        functools.partial(feed_kernel, bool(before)),
        (rows_in, grad_in, own, other, *before),
        [shaped((rows, width), F32)] * 2
        + [shaped((pair, wide, *shape), BF) for shape in [own_shape, *other_shapes]],
        [scratch(rows, total, dtype=BF)] * 3,
        9 * rows * width * total,
        FEED_MEGABYTES[flat],
        transcendentals=rows * total,
        aliases={4: 0, 5: 1} if before else None,
    )


AXES = ("wide", "narrow")


class Grid:
    def __init__(self):
        self.wide = lax.axis_size("wide")
        self.narrow = lax.axis_size("narrow")
        self.outer = 4
        self.inner = self.wide // 4
        self.pair = self.narrow // 2
        self.size = {"outer": 4, "inner": self.inner, "pair": self.pair, "core": 2}
        self.stride = {"outer": self.inner * self.narrow, "inner": self.narrow, "pair": 2, "core": 1}
        linear = lax.axis_index("wide") * self.narrow + lax.axis_index("narrow")
        self.at = {name: (linear // self.stride[name]) % self.size[name] for name in self.size}

    def shift(self, value, name, count=1):
        size, stride = self.size[name], self.stride[name]
        pairs = []
        for source in range(self.wide * self.narrow):
            digit = (source // stride) % size
            pairs.append((source, source + ((digit + count) % size - digit) * stride))
        return lax.ppermute(value, AXES, pairs)

    def behind(self, name, steps):
        return (self.at[name] + (self.size[name] - steps)) % self.size[name]


def after(value, others):
    if not others:
        return value
    return lax.optimization_barrier((value, *others))[0]


class Flow:
    def __init__(self, make, grid, *args):
        self.grid = grid
        self.gates = ()
        self.last = ()
        self.result = None
        self.more = ()
        self.run = make(self, *args)

    def step(self, *others):
        self.gates = others
        try:
            self.last = next(self.run)
        except StopIteration as stop:
            self.result = stop.value
            return self.result
        return None

    def finish(self):
        while self.result is None:
            self.step()
        return self.result

    def shift(self, value, name, count=1):
        return self.grid.shift(after(value, self.gates), name, count)

    def settle(self, value):
        return after(value, self.gates)


class Clock:
    def __init__(self):
        self.held = ()

    def now(self, value):
        return after(value, self.held)

    def phase(self, *starts, done=(), wait=(), leave=()):
        gates = self.held + tuple(done)
        for flow, steps in starts:
            for _ in range(steps):
                flow.step(*gates)
        flows = [flow for flow, _ in starts if flow not in leave] + list(wait)
        held = sum([tuple(flow.last) for flow in flows], tuple(done))
        if not starts:
            held = self.held + held
        self.held = held if held else self.held


def both_rings(flow, first, first_name, second, second_name):
    one, two = [first], [second]
    for at in range(max(flow.grid.size[first_name], flow.grid.size[second_name]) - 1):
        if at < flow.grid.size[first_name] - 1:
            one.append(flow.shift(one[-1], first_name))
        if at < flow.grid.size[second_name] - 1:
            two.append(flow.shift(two[-1], second_name))
        yield (one[-1], two[-1])
        if at < flow.grid.size[first_name] - 1:
            one[-1] = flow.settle(one[-1])
        if at < flow.grid.size[second_name] - 1:
            two[-1] = flow.settle(two[-1])
    return one, two


def gather_outer(flow, shard):
    moved = [flow.shift(shard, "outer", count) for count in range(1, flow.grid.outer)]
    yield tuple(moved)
    return [shard] + [flow.settle(block) for block in moved]


def gather_ring(flow, shard):
    blocks = [shard]
    for _ in range(flow.grid.outer - 1):
        blocks.append(flow.shift(blocks[-1], "outer"))
        yield (blocks[-1],)
        blocks[-1] = flow.settle(blocks[-1])
    return blocks


def gather_plane(flow, blocks, cut):
    stacked = lax.optimization_barrier(jnp.stack(blocks))
    first, second = stacked[..., :cut, :], stacked[..., cut:, :]
    one, two = yield from both_rings(flow, first, "inner", second, "pair")
    one, two = yield from both_rings(flow, jnp.concatenate(one), "pair", jnp.stack(two), "inner")
    own = jnp.concatenate([jnp.stack(one), jnp.concatenate(two, axis=1)], axis=-2)
    other = flow.shift(own, "core")
    yield (other,)
    return own, other


def both_sums(flow, first, first_name, second, second_name):
    sizes = flow.grid.size
    one, two = first(1), second(1)
    for step in range(1, max(sizes[first_name], sizes[second_name])):
        moved = []
        if step < sizes[first_name]:
            one = flow.shift(one, first_name)
            moved.append(one)
        if step < sizes[second_name]:
            two = flow.shift(two, second_name)
            moved.append(two)
        yield tuple(moved)
        if step < sizes[first_name]:
            one = flow.settle(one) + first((step + 1) % sizes[first_name])
        if step < sizes[second_name]:
            two = flow.settle(two) + second((step + 1) % sizes[second_name])
    return one, two


def scatter_plane(flow, own, other, cut):
    outer = flow.grid.outer
    if isinstance(other, tuple):
        moved = tuple(flow.shift(part, "core") for part in other)
        yield moved
        moved = [flow.settle(part) for part in moved]
        moved = jnp.stack(moved, axis=2) if own.ndim == 5 else jnp.concatenate(moved, axis=2)
    else:
        moved = flow.shift(other, "core")
        yield (moved,)
        moved = flow.settle(moved)
    more = None
    if flow.more:
        more = flow.shift(flow.more[1], "core")
        yield (more,)
        more = flow.settle(more)

    def wide_part(r):
        return slice(r * outer, (r + 1) * outer)

    def first(r):
        return moved[r, ..., :cut, :] + own[r, ..., :cut, :]

    def second(r):
        block = moved[:, wide_part(r), ..., cut:, :] + own[:, wide_part(r), ..., cut:, :]
        if more is None:
            return block
        return jnp.concatenate([block, more[:, wide_part(r)] + flow.more[0][:, wide_part(r)]], axis=-2)

    one, two = yield from both_sums(flow, first, "pair", second, "inner")
    one, two = yield from both_sums(
        flow, lambda r: one[wide_part(r)], "inner", lambda r: two[r], "pair"
    )
    return jnp.concatenate([one, two], axis=-2)


def scatter_outer(flow, sums):
    outer = flow.grid.outer
    moved = [flow.shift(sums[r], "outer", outer - r) for r in range(1, outer)]
    yield tuple(moved)
    return sum([flow.settle(block).astype(F32) for block in moved], sums[0].astype(F32))


def scatter_split(flow, sums):
    outer = flow.grid.outer
    moved = [flow.shift(sums[r], "outer", outer - r) for r in range(2, outer)]
    yield tuple(moved)
    moved = [flow.settle(block) for block in moved]
    moved.append(flow.shift(sums[1], "outer", outer - 1))
    yield tuple(moved[-1:])
    return sum([flow.settle(block).astype(F32) for block in moved], sums[0].astype(F32))


def scatter_ring(flow, sums):
    outer = flow.grid.outer
    total = sums[1]
    for step in range(1, outer):
        total = flow.shift(total, "outer")
        yield (total,)
        total = flow.settle(total).astype(F32) + sums[(step + 1) % outer].astype(F32)
        if step < outer - 1:
            total = total.astype(BF)
    return total


def rounded_up(count, step):
    return -(-count // step) * step
GRANTS = {
    "prepare_narrow": 16,
    "prepare_wide": 12,
    "project": 24,
    "attend": 12,
    "residual": 20,
    "middle": 24,
    "attend_back": 20,
    "weights": 28,
    "outputs": 28,
}


def body(
    tokens,
    lengths,
    cotangent,
    query_weight,
    key_matrix,
    value_matrix,
    output_weight,
    gate_weight,
    up_weight,
    down_weight,
    attention_gain,
    feedforward_gain,
):
    grid = Grid()
    batches, bucket_rows, width = tokens.shape
    rows = batches * bucket_rows
    wide, narrow, pair, inner, outer = grid.wide, grid.narrow, grid.pair, grid.inner, grid.outer
    d_w, d_n = query_weight.shape
    kv_n = key_matrix.shape[1]
    f_w = down_weight.shape[0]
    d_pad = rounded_up(d_n, 128)
    r_w = rounded_up(d_w + 1, 64)
    taken = d_n + 2 * kv_n
    t_rows = rounded_up(taken, 16)
    sizes = (wide, d_w, r_w, d_n, kv_n, pair, d_pad)

    packed = jnp.concatenate([query_weight.T, key_matrix.T, value_matrix.T], axis=0)
    gain_column = jnp.concatenate([attention_gain, jnp.zeros((2 * kv_n,), BF)])[:, None]
    packed = jnp.concatenate([packed, gain_column, jnp.zeros((taken, r_w - d_w - 1), BF)], axis=1)
    a_shard = jnp.pad(packed, ((0, t_rows - taken), (0, 0)))
    a_cut = rounded_up(t_rows // 2, 16)
    o_shard = jnp.concatenate([output_weight, feedforward_gain[None], jnp.zeros((r_w - d_w - 1, d_n), BF)])
    f_shard = jnp.stack([gate_weight.T, up_weight.T, down_weight])
    sub = 256 // wide
    tiles_in = f_w // sub
    bounds = [0, 4 * tiles_in // 10 * sub, f_w]
    shards = [f_shard[:, lo:hi] for lo, hi in zip(bounds, bounds[1:])]
    shards[0] = jnp.concatenate([shards[0], o_shard[None]])
    shards = [jnp.pad(shard, ((0, 0), (0, 0), (d_pad - d_n, 0))) for shard in shards]
    cuts = [shard.shape[1] // 2 for shard in shards]

    place = jnp.arange(wide, dtype=jnp.int32)
    w_order = (grid.at["outer"] - place % outer) % outer * inner
    w_order = (w_order + (grid.at["inner"] - place // outer) % inner).astype(jnp.int32)
    place = jnp.arange(narrow, dtype=jnp.int32)
    n_order = (grid.at["pair"] - place % pair) % pair * 2
    n_order = (n_order + (grid.at["core"] - place // pair) % 2).astype(jnp.int32)
    slots = lengths.shape[2]
    orders = (w_order, n_order, lengths.reshape(-1))
    freqs = THETA ** (-jnp.arange(HEAD_WIDTH // 2, dtype=F32) * 2.0 / HEAD_WIDTH)
    freqs = jnp.concatenate([freqs] * 4)[None]

    flow_za = Flow(gather_outer, grid, a_shard)
    flow_z1 = Flow(gather_ring, grid, shards[0])
    flow_z2 = Flow(gather_ring, grid, shards[1])
    plane = max(inner, pair) - 1
    clock = Clock()
    clock.phase((flow_za, 1), (flow_z1, 1), leave=(flow_za, flow_z1))
    token_rows = tokens.reshape(rows, width)
    cotangent_rows = cotangent.reshape(rows, width)
    token_narrow, branch_grad = call(
        "prepare_narrow",
        functools.partial(prepare_narrow_kernel, sizes, batches, slots),
        (token_rows, cotangent_rows),
        [shaped((rows, narrow * d_pad), BF)] * 2,
        [scratch(narrow, rows, d_pad, dtype=BF)] * 2,
        0,
        GRANTS["prepare_narrow"],
        orders=orders,
    )
    clock.phase(done=(token_narrow,), wait=(flow_za, flow_z1))
    flow_a = Flow(gather_plane, grid, flow_za.finish(), a_cut)
    clock.phase((flow_a, plane), (flow_z1, 1), leave=(flow_a, flow_z1))
    token_wide, cosine, sine = call(
        "prepare_wide",
        functools.partial(prepare_wide_kernel, sizes, batches, slots),
        (clock.now(token_rows), freqs),
        [shaped((rows, wide * r_w), BF), shaped((rows, 128), F32), shaped((rows, 128), F32)],
        [scratch(wide, rows, r_w, dtype=BF)],
        0,
        GRANTS["prepare_wide"],
        orders=orders,
    )
    clock.phase(done=(token_wide,), wait=(flow_a, flow_z1))
    clock.phase((flow_a, plane), (flow_z1, 1))
    flow_1 = Flow(gather_plane, grid, flow_z1.finish(), cuts[0])
    clock.phase((flow_a, 1), (flow_1, plane), (flow_z2, 1), leave=(flow_1, flow_z2))
    a_own, a_other = flow_a.finish()
    a_in, query, key, value = call(
        "project",
        functools.partial(project_kernel, sizes),
        (clock.now(token_wide), cosine, sine, a_own, a_other),
        [
            shaped((rows, wide * r_w), BF),
            shaped((rows, QUERY_HEADS * HEAD_WIDTH), BF),
            shaped((rows, KEY_VALUE_HEADS * HEAD_WIDTH), BF),
            shaped((rows, KEY_VALUE_HEADS * HEAD_WIDTH), BF),
        ],
        [scratch(narrow, rows, t_rows), scratch(narrow, 1, t_rows), scratch(wide, 1, r_w)],
        rows * wide * r_w * narrow * t_rows,
        GRANTS["project"],
        orders=orders,
    )

    clock.phase(done=(query,), wait=(flow_1, flow_z2))
    clock.phase((flow_1, plane), (flow_z2, 1), leave=(flow_1, flow_z2))

    def by_bucket(field):
        return field.reshape(batches, bucket_rows, field.shape[-1])

    group = QUERY_HEADS // KEY_VALUE_HEADS
    steps = bucket_rows // 128
    p_shape = (KEY_VALUE_HEADS, group * 128, 128 * steps * (steps + 1) // 2)
    query, key, value = by_bucket(query), by_bucket(key), by_bucket(value)
    pair_work = QUERY_HEADS * bucket_rows * bucket_rows * HEAD_WIDTH
    attended, probs = [], []
    for b in range(batches):
        parts = call(
            "attend",
            functools.partial(attend_kernel, slots, b),
            (clock.now(query), key, value),
            [shaped(query.shape[1:], BF), shaped(p_shape, BF)],
            [],
            6 * pair_work,
            GRANTS["attend"],
            orders=orders,
            transcendentals=QUERY_HEADS * bucket_rows * bucket_rows,
        )
        attended.append(parts[0])
        probs.append(parts[1])
        if b < batches - 1:
            clock.phase(done=(parts[0],), wait=(flow_z2,))
            clock.phase((flow_z2, 1), leave=(flow_z2,))
    clock.phase(done=tuple(attended), wait=(flow_1, flow_z2))
    flow_2 = Flow(gather_plane, grid, flow_z2.finish(), cuts[1])
    clock.phase((flow_1, 1), (flow_2, plane), leave=(flow_2,))
    first_own, first_other = flow_1.finish()
    o_operands = (first_own[:, :, 3], first_other[:, :, 3])
    d_lanes = narrow * d_pad
    attended_wide, residual, feed_in = call(
        "residual",
        functools.partial(residual_kernel, sizes, batches),
        (clock.now(token_narrow), *o_operands, *attended),
        [
            shaped((rows, wide * r_w), BF),
            shaped((rows, d_lanes), F32),
            shaped((rows, d_lanes), BF),
        ],
        [scratch(wide, rows, r_w, dtype=BF)],
        rows * wide * r_w * d_lanes,
        GRANTS["residual"],
        orders=orders,
    )

    clock.phase(done=(feed_in,), wait=(flow_2,))
    clock.phase((flow_2, plane), leave=(flow_2,))
    *sums_so_far, own_terms, gate_terms, up_terms, down_terms = feed_call(
        clock.now(feed_in), branch_grad, first_own, first_other
    )
    back_1 = Flow(scatter_plane, grid, own_terms, (gate_terms, up_terms, down_terms), cuts[0])
    clock.phase(done=(own_terms,))
    clock.phase((back_1, 1), wait=(flow_2,))
    clock.phase((flow_2, 1), (back_1, plane), leave=(back_1,))
    *sums_so_far, own_terms, other_terms = feed_call(
        clock.now(feed_in), branch_grad, *flow_2.finish(), tuple(sums_so_far), True
    )
    back_2 = Flow(
        scatter_plane,
        grid,
        own_terms,
        other_terms,
        rounded_up((own_terms.shape[2] + r_w) // 2, 16),
    )
    clock.phase(done=(own_terms,), wait=(back_1,))
    clock.phase((back_1, plane), (back_2, 1), leave=(back_1, back_2))
    mix, back = sums_so_far
    grad, attended_grad, own_o, other_o = call(
        "middle",
        functools.partial(middle_kernel, sizes),
        (clock.now(residual), back, branch_grad, attended_wide) + o_operands,
        [
            shaped((rows, d_lanes), F32),
            shaped((rows, width), BF),
            shaped((pair, wide, r_w, d_pad), BF),
            shaped((pair, wide, r_w, d_pad), BF),
        ],
        [scratch(wide, rows, r_w)],
        2 * rows * wide * r_w * d_lanes,
        GRANTS["middle"],
        orders=orders,
    )
    clock.phase(done=(attended_grad,), wait=(back_1, back_2))
    back_2.more = (own_o, other_o)
    clock.phase((back_2, 1))
    back_z1 = Flow(scatter_split, grid, back_1.finish())
    clock.phase((back_2, plane), (back_z1, 1), leave=(back_2, back_z1))
    by_parts = (by_bucket(attended_grad), by_bucket(cosine), by_bucket(sine))
    shapes = [x.shape[1:] for x in (query, key, value)]
    grads = []
    for b in range(batches):
        grads.append(
            call(
                "attend_back",
                functools.partial(attend_back_kernel, b),
                (clock.now(query), key, value, attended[b], by_parts[0], probs[b], *by_parts[1:]),
                [shaped(shape, BF) for shape in shapes],
                [scratch(*shape) for shape in shapes],
                12 * pair_work,
                GRANTS["attend_back"],
                orders=orders,
            )
        )
        if b < batches - 1:
            clock.phase(done=tuple(grads[b][:1]), wait=(back_z1,))
            clock.phase((back_z1, 1), leave=(back_z1,))
    clock.phase(done=tuple(x[0] for x in grads), wait=(back_2, back_z1))
    clock.phase((back_2, plane), leave=(back_2,))
    operands = tuple(x for parts in zip(*grads) for x in parts)
    cuts_a = [0, rounded_up(t_rows // 3, 16), rounded_up(2 * t_rows // 3, 16), t_rows]
    wide_back, own_terms, *other_terms = call(
        "weights",
        functools.partial(weights_kernel, sizes, batches),
        (clock.now(token_wide), a_in, a_own, a_other) + operands,
        [shaped((rows, wide * r_w), F32), shaped(a_own.shape, BF)]
        + [shaped((pair, wide, hi - lo, r_w), BF) for lo, hi in zip(cuts_a, cuts_a[1:])],
        [scratch(narrow, rows, t_rows, dtype=BF), scratch(narrow, 1, t_rows), scratch(wide, 1, r_w)],
        2 * rows * wide * r_w * narrow * t_rows,
        GRANTS["weights"],
        orders=orders,
    )
    back_a = Flow(scatter_plane, grid, own_terms, tuple(other_terms), a_cut)
    clock.phase(done=(own_terms,))
    clock.phase((back_a, 1), wait=(back_2,))
    back_z2 = Flow(scatter_ring, grid, back_2.finish())
    clock.phase((back_a, plane), (back_z2, 1), leave=(back_a, back_z2))
    mixed, tokens_grad = call(
        "outputs",
        functools.partial(outputs_kernel, sizes, batches, slots),
        (clock.now(residual), mix, grad, token_wide, wide_back, a_own, a_other),
        [shaped((batches, width, bucket_rows), BF)] * 2,
        [
            scratch(narrow, rows, d_pad),
            scratch(wide, rows, r_w),
            scratch(narrow, 1, t_rows),
            scratch(wide, 1, r_w),
        ],
        0,
        GRANTS["outputs"],
        orders=orders,
    )
    clock.phase(done=(mixed,), wait=(back_z2,))
    clock.phase((back_z2, 1), wait=(back_a,), leave=(back_z2,))
    clock.phase((back_a, plane), wait=(back_z2,))
    back_za = Flow(scatter_outer, grid, back_a.finish())
    clock.phase((back_z2, 1), (back_za, 1), leave=(back_z2, back_za))
    a_sum = back_za.finish()
    rest = back_z2.finish()
    o_sum = rest[rest.shape[0] - r_w :]
    rest = rest[: rest.shape[0] - r_w].reshape(3, -1, d_pad)
    feed_sum = jnp.concatenate([back_z1.finish(), rest], axis=1)[:, :, d_pad - d_n :]
    return (
        jnp.swapaxes(mixed, 1, 2),
        jnp.swapaxes(tokens_grad, 1, 2),
        a_sum[:d_n, :d_w].T,
        a_sum[d_n : d_n + kv_n, :d_w].T,
        a_sum[d_n + kv_n : taken, :d_w].T,
        o_sum[:d_w, d_pad - d_n :],
        feed_sum[0].T,
        feed_sum[1].T,
        feed_sum[2],
        a_sum[:d_n, d_w],
        o_sum[d_w, d_pad - d_n :],
    )


def solution(mesh):
    in_specs = (
        P(None, ("wide", "narrow"), None),
        P(None, ("wide", "narrow"), None),
        P(None, ("wide", "narrow"), None),
        P("wide", "narrow"),
        P("wide", "narrow"),
        P("wide", "narrow"),
        P("wide", "narrow"),
        P("narrow", "wide"),
        P("narrow", "wide"),
        P("wide", "narrow"),
        P("narrow"),
        P("narrow"),
    )
    out_specs = (
        P(None, ("wide", "narrow"), None),
        P(None, ("wide", "narrow"), None),
        P("wide", "narrow"),
        P("wide", "narrow"),
        P("wide", "narrow"),
        P("wide", "narrow"),
        P("narrow", "wide"),
        P("narrow", "wide"),
        P("wide", "narrow"),
        P("narrow"),
        P("narrow"),
    )
    return jax.shard_map(body, mesh=mesh, in_specs=in_specs, out_specs=out_specs, check_vma=False)
```

```python
import functools

import jax
import jax.numpy as jnp
from jax import lax
from jax.experimental import pallas as pl
from jax.experimental.pallas import tpu as pltpu
from jax.sharding import PartitionSpec as P

QUERY_HEADS = 15
KEY_VALUE_HEADS = 5
HEAD_WIDTH = 64


EPS = 1e-05
THETA = 10000.0


def segments_of(lengths_row, count_of_rows):
    ends = jnp.cumsum(lengths_row, dtype=jnp.int32)
    starts = ends - lengths_row
    places = jnp.arange(count_of_rows, dtype=jnp.int32)
    segment = jnp.sum((places[:, None] >= ends[None, :]).astype(jnp.int32), axis=1, dtype=jnp.int32)
    slot_ids = jnp.arange(lengths_row.shape[0], dtype=jnp.int32)
    opening = jnp.sum(
        jnp.where(segment[:, None] == slot_ids[None, :], starts[None, :], 0),
        axis=1,
        dtype=jnp.int32,
    )
    opening = jnp.where(segment == lengths_row.shape[0], ends[-1], opening)
    return (segment, places - opening)


F32 = jnp.float32
BF = jnp.bfloat16
NT = (((1,), (1,)), ((), ()))
TN = (((0,), (0,)), ((), ()))
NN = (((1,), (0,)), ((), ()))


def dot(left, right, dims):
    return lax.dot_general(left, right, dims, preferred_element_type=F32)


def side(parts):
    return parts[0] if len(parts) == 1 else jnp.concatenate(parts, axis=1)


def mean_of(field, width):
    return jnp.sum(field, axis=1, keepdims=True) * (1.0 / width)


def row_of(block, row):
    at = lax.broadcasted_iota(jnp.int32, (block.shape[0], 1), 0)
    return jnp.sum(jnp.where(at == row, block.astype(F32), 0.0), axis=0, keepdims=True)


def zeros_beside(field, lanes, before):
    pad = jnp.zeros((field.shape[0], lanes - field.shape[1]), field.dtype)
    return side([pad, field] if before else [field, pad])


def turn(field, cosine, sine):
    lane = lax.broadcasted_iota(jnp.int32, (1, 128), 1)
    low = (lane % 64) < 32
    tiles = []
    for start in range(0, field.shape[1], 128):
        piece = field[:, start : start + 128]
        count = piece.shape[1]
        if count < 128:
            piece = zeros_beside(piece, 128, False)
        other = jnp.where(low, pltpu.roll(piece, 96, 1), pltpu.roll(piece, 32, 1))
        tiles.append((piece * cosine + other * sine)[:, :count])
    return side(tiles)


def places(lengths, bucket, slots, shape, axis):
    at = lax.broadcasted_iota(jnp.int32, shape, axis)
    end = jnp.int32(0)
    segment = jnp.zeros(shape, jnp.int32)
    opening = jnp.zeros(shape, jnp.int32)
    for slot in range(slots):
        length = lengths[bucket * slots + slot]
        end = end + length
        over = at >= end
        segment += jnp.where(over, 1, 0)
        opening += jnp.where(over, length, 0)
    return segment, at - opening, segment < slots


def prepare_narrow_kernel(sizes, batches, slots, w_order, n_order, lengths, tok_ref, cot_ref, tn_ref, gf_ref, n_blocks, c_blocks):
    wide, d_w, r_w, d_n, kv_n, pair, d_pad = sizes
    narrow = 2 * pair
    rows = tok_ref.shape[0] // batches
    for b in range(batches):
        part = slice(b * rows, (b + 1) * rows)
        _, _, inside = places(lengths, b, slots, (rows, 1), 0)
        field = tok_ref[part].astype(F32)
        upstream = jnp.where(inside, cot_ref[part].astype(F32), 0.0)
        for n in range(narrow):
            n_blocks[n, part] = zeros_beside(field[:, n * d_n : (n + 1) * d_n], d_pad, True).astype(BF)
            c_blocks[n, part] = zeros_beside(upstream[:, n * d_n : (n + 1) * d_n], d_pad, True).astype(BF)
    tn_ref[...] = side([n_blocks[n_order[index]] for index in range(narrow)])
    gf_ref[...] = side([c_blocks[n_order[index]] for index in range(narrow)])


def prepare_wide_kernel(sizes, batches, slots, w_order, n_order, lengths, tok_ref, freq_ref, tw_ref, cos_ref, sin_ref, w_blocks):
    wide, d_w, r_w, d_n, kv_n, pair, d_pad = sizes
    rows = tok_ref.shape[0] // batches
    field = tok_ref[...].astype(F32)
    for w in range(wide):
        w_blocks[w] = zeros_beside(field[:, w * d_w : (w + 1) * d_w], r_w, False).astype(BF)
    tw_ref[...] = side([w_blocks[w_order[p]] for p in range(wide)])
    sign = jnp.where(lax.broadcasted_iota(jnp.int32, (1, 128), 1) % 64 < 32, -1.0, 1.0)
    for b in range(batches):
        part = slice(b * rows, (b + 1) * rows)
        _, position, _ = places(lengths, b, slots, (rows, 1), 0)
        angle = position.astype(F32) * freq_ref[...]
        cos_ref[part] = jnp.cos(angle)
        sin_ref[part] = jnp.sin(angle) * sign


def beside(ref, at):
    return side([ref[at, p] for p in range(ref.shape[1])])


def gain_rows(sizes, own_ref, other_ref, n_order, gain_blocks):
    wide, d_w, r_w, d_n, kv_n, pair, d_pad = sizes
    lane = lax.broadcasted_iota(jnp.int32, (16, r_w), 1)
    chosen = jnp.where(lane == d_w, 1.0, 0.0).astype(BF)
    for index in range(2 * pair):
        block = (own_ref, other_ref)[index // pair][index % pair, 0]
        gain_blocks[n_order[index]] = dot(chosen, block, NT)[:1]
    return side([gain_blocks[n][:, :d_n] for n in range(2 * pair)])


def project_kernel(
    sizes, w_order, n_order, lengths, tw_ref, cos_ref, sin_ref, own_ref, other_ref,
    a_ref, q_ref, k_ref, v_ref, projected, gain_blocks, gain_wide,
):
    wide, d_w, r_w, d_n, kv_n, pair, d_pad = sizes
    narrow = 2 * pair
    width = wide * d_w
    gain = gain_rows(sizes, own_ref, other_ref, n_order, gain_blocks)
    for w in range(wide):
        gain_wide[w] = zeros_beside(gain[:, w * d_w : (w + 1) * d_w], r_w, False)
    field = tw_ref[...].astype(F32)
    scale = lax.rsqrt(mean_of(field * field, width) + EPS)
    a_wide = (field * scale * side([gain_wide[w_order[p]] for p in range(wide)])).astype(BF)
    a_ref[...] = a_wide
    for index in range(narrow):
        block = beside((own_ref, other_ref)[index // pair], index % pair)
        projected[n_order[index]] = dot(a_wide, block, NT)
    cosine, sine = cos_ref[...], sin_ref[...]

    def taken(start, count):
        return side([projected[n][:, start : start + count] for n in range(narrow)])

    q_ref[...] = (turn(taken(0, d_n), cosine, sine) * HEAD_WIDTH**-0.5).astype(BF)
    k_ref[...] = turn(taken(d_n, kv_n), cosine, sine).astype(BF)
    v_ref[...] = taken(d_n + kv_n, kv_n).astype(BF)


def attend_kernel(slots, bucket, w_order, n_order, lengths, q_ref, k_ref, v_ref, ob_ref, p_ref):
    rows = q_ref.shape[1]
    seg_row, _, _ = places(lengths, bucket, slots, (1, rows), 1)
    seg_col, _, _ = places(lengths, bucket, slots, (rows, 1), 0)
    step = 128
    group = QUERY_HEADS // KEY_VALUE_HEADS
    head = HEAD_WIDTH
    offset = 0
    for i in range(rows // step):
        upto = (i + 1) * step
        query_at = i * step + lax.broadcasted_iota(jnp.int32, (step, upto), 0)
        key_at = lax.broadcasted_iota(jnp.int32, (step, upto), 1)
        same = seg_col[i * step : upto] == seg_row[:, :upto]
        bias = jnp.where(same & (key_at <= query_at), 0.0, -1000000000.0)
        for g in range(KEY_VALUE_HEADS):
            queries = jnp.concatenate(
                [
                    q_ref[bucket, i * step : upto, (g * group + j) * head : (g * group + j + 1) * head]
                    for j in range(group)
                ],
                axis=0,
            )
            keys = k_ref[bucket, :upto, g * head : (g + 1) * head]
            values = v_ref[bucket, :upto, g * head : (g + 1) * head]
            logits = dot(queries, keys, NT).reshape(group, step, upto) + bias[None]
            peak = jnp.max(logits, axis=-1, keepdims=True)
            shifted = jnp.exp(logits - peak)
            total = jnp.sum(shifted, axis=-1, keepdims=True)
            probs = (shifted * (1.0 / total)).astype(BF).reshape(group * step, upto)
            p_ref[g, :, offset : offset + upto] = probs
            out = dot(probs, values, NN).astype(BF)
            ob_ref[i * step : upto, g * group * head : (g + 1) * group * head] = side(
                [out[j * step : (j + 1) * step] for j in range(group)]
            )
        offset += upto


def residual_kernel(
    sizes, batches, w_order, n_order, lengths, tn_ref, own_ref, other_ref, *refs
):
    ob_wide_ref, hr_ref, bf_ref, e_blocks = refs[batches:]
    wide, d_w, r_w, d_n, kv_n, pair, d_pad = sizes
    narrow = 2 * pair
    spare = d_w // 16 * 16
    width = wide * d_w
    attended = jnp.concatenate([ref[...].astype(F32) for ref in refs[:batches]], axis=0)
    for w in range(wide):
        e_blocks[w] = zeros_beside(attended[:, w * d_w : (w + 1) * d_w], r_w, False).astype(BF)
    ob_wide = side([e_blocks[w_order[p]] for p in range(wide)])
    ob_wide_ref[...] = ob_wide
    blocks = []
    gains = []
    for index in range(narrow):
        block = (own_ref, other_ref)[index // pair][index % pair].reshape(wide * r_w, d_pad)
        gains.append(row_of(block[spare : spare + 16], d_w - spare))
        rows_in = tn_ref[:, index * d_pad : (index + 1) * d_pad].astype(F32)
        blocks.append(rows_in + dot(ob_wide, block, NN))
    residual = side(blocks)
    hr_ref[...] = residual
    scale = lax.rsqrt(mean_of(residual * residual, width) + EPS)
    bf_ref[...] = (residual * scale * side(gains)).astype(BF)


def middle_kernel(
    sizes, w_order, n_order, lengths, hr_ref, back_ref, gf_ref, ob_ref, own_ref, other_ref,
    gh_ref, go_ref, own_terms, other_terms, e_blocks,
):
    wide, d_w, r_w, d_n, kv_n, pair, d_pad = sizes
    narrow = 2 * pair
    spare = d_w // 16 * 16
    width = wide * d_w
    residual = hr_ref[...]
    blocks = [
        (own_ref, other_ref)[index // pair][index % pair].reshape(wide * r_w, d_pad)
        for index in range(narrow)
    ]
    gain = side([row_of(block[spare : spare + 16], d_w - spare) for block in blocks])
    back = back_ref[...]
    scale = lax.rsqrt(mean_of(residual * residual, width) + EPS)
    normed = residual * scale
    gain_term = jnp.sum(back * normed, axis=0, keepdims=True)
    here = lax.broadcasted_iota(jnp.int32, (r_w, 1), 0) == d_w
    normed_grad = back * gain
    grad = gf_ref[...].astype(F32) + scale * (
        normed_grad - normed * mean_of(normed_grad * normed, width)
    )
    gh_ref[...] = grad
    low = grad.astype(BF)
    total = None
    ob_wide = ob_ref[...]
    for index in range(narrow):
        piece = low[:, index * d_pad : (index + 1) * d_pad]
        part = dot(piece, blocks[index], NT)
        total = part if total is None else total + part
        term = dot(ob_wide, piece, TN).reshape(wide, r_w, d_pad)
        row = gain_term[:, index * d_pad : (index + 1) * d_pad]
        ref = (own_terms, other_terms)[index // pair]
        ref[index % pair] = (term + jnp.where(here, row, 0.0)[None]).astype(BF)
    for p in range(wide):
        e_blocks[w_order[p]] = total[:, p * r_w : (p + 1) * r_w]
    go_ref[...] = side([e_blocks[w][:, :d_w] for w in range(wide)]).astype(BF)


def attend_back_kernel(
    bucket, w_order, n_order, lengths, q_ref, k_ref, v_ref, ob_ref, go_ref, p_ref, cos_ref, sin_ref, gq_ref, gk_ref, gv_ref, gq_sum, gk_sum, gv_sum
):
    rows = q_ref.shape[1]
    step = 128
    group = QUERY_HEADS // KEY_VALUE_HEADS
    head = HEAD_WIDTH
    for g in range(KEY_VALUE_HEADS):
        offset = 0
        lanes = slice(g * head, (g + 1) * head)
        gk_total, gv_total = [], []
        for i in range(rows // step):
            upto = (i + 1) * step

            def stacked(ref, *at):
                return jnp.concatenate(
                    [
                        ref[(*at, slice(i * step, upto), slice((g * group + j) * head, (g * group + j + 1) * head))]
                        for j in range(group)
                    ],
                    axis=0,
                )

            queries, out_grads, outs = stacked(q_ref, bucket), stacked(go_ref, bucket), stacked(ob_ref)
            keys = k_ref[bucket, :upto, lanes]
            values = v_ref[bucket, :upto, lanes]
            probs = p_ref[g, :, offset : offset + upto]
            delta = jnp.sum(out_grads.astype(F32) * outs.astype(F32), axis=1, keepdims=True)
            prob_grad = dot(out_grads, values, NT)
            logit_grad = (probs.astype(F32) * (prob_grad - delta)).astype(BF)
            query_part = dot(logit_grad, keys, NN) * head**-0.5
            gq_sum[i * step : upto, g * group * head : (g + 1) * group * head] = side(
                [query_part[j * step : (j + 1) * step] for j in range(group)]
            )
            key_part = dot(logit_grad, queries, TN)
            value_part = dot(probs, out_grads, TN)
            for j in range(i + 1):
                if j == i:
                    gk_total.append(key_part[j * step : (j + 1) * step])
                    gv_total.append(value_part[j * step : (j + 1) * step])
                else:
                    gk_total[j] += key_part[j * step : (j + 1) * step]
                    gv_total[j] += value_part[j * step : (j + 1) * step]
            offset += upto
        gk_sum[:, lanes] = jnp.concatenate(gk_total, axis=0)
        gv_sum[:, lanes] = jnp.concatenate(gv_total, axis=0)
    cosine, sine = cos_ref[bucket], sin_ref[bucket]
    gq_ref[...] = turn(gq_sum[...], cosine, -sine).astype(BF)
    gk_ref[...] = turn(gk_sum[...], cosine, -sine).astype(BF)
    gv_ref[...] = gv_sum[...].astype(BF)


def weights_kernel(
    sizes, batches, w_order, n_order, lengths, tw_ref, a_ref, own_ref, other_ref, *refs
):
    wide, d_w, r_w, d_n, kv_n, pair, d_pad = sizes
    narrow = 2 * pair
    width = wide * d_w
    back_ref, own_terms, *other_terms, g_blocks, gain_blocks, gain_wide = refs[3 * batches :]
    count = own_ref.shape[2]
    for b in range(batches):
        gq, gk, gv = [refs[kind * batches + b][...].astype(F32) for kind in range(3)]
        bucket = slice(b * gq.shape[0], (b + 1) * gq.shape[0])
        for n in range(narrow):
            piece = side(
                [
                    gq[:, n * d_n : (n + 1) * d_n],
                    gk[:, n * kv_n : (n + 1) * kv_n],
                    gv[:, n * kv_n : (n + 1) * kv_n],
                ]
            )
            if piece.shape[1] < count:
                piece = zeros_beside(piece, count, False)
            g_blocks[n, bucket] = piece.astype(BF)
    total = None
    for index in range(narrow):
        block = beside((own_ref, other_ref)[index // pair], index % pair)
        part = dot(g_blocks[n_order[index]], block, NN)
        total = part if total is None else total + part
    back_ref[...] = total
    field = tw_ref[...].astype(F32)
    scale = lax.rsqrt(mean_of(field * field, width) + EPS)
    gain_term = jnp.sum(total * (field * scale), axis=0, keepdims=True)
    for p in range(wide):
        gain_wide[w_order[p]] = gain_term[:, p * r_w : (p + 1) * r_w]
    gain_term = side([gain_wide[w][:, :d_w] for w in range(wide)])
    for n in range(narrow):
        gain_blocks[n] = zeros_beside(gain_term[:, n * d_n : (n + 1) * d_n], count, False)
    first = lax.broadcasted_iota(jnp.int32, (8, 1), 0) == 0
    lane = lax.broadcasted_iota(jnp.int32, (8, r_w), 1)
    chosen = jnp.where(first & (lane == d_w), 1.0, 0.0)
    a_wide = a_ref[...]
    for index in range(narrow):
        column = dot(jnp.broadcast_to(gain_blocks[n_order[index]], (8, count)), chosen, TN)
        term = dot(g_blocks[n_order[index]], a_wide, TN)
        for p in range(wide):
            block = (term[:, p * r_w : (p + 1) * r_w] + column).astype(BF)
            if index < pair:
                own_terms[index, p] = block
                continue
            start = 0
            for ref in other_terms:
                ref[index % pair, p] = block[start : start + ref.shape[2]]
                start += ref.shape[2]


def outputs_kernel(
    sizes, batches, slots, w_order, n_order, lengths, hr_ref, mix_ref, gh_ref, tw_ref, back_ref, own_ref, other_ref,
    mixed_ref, grad_ref, n_blocks, d_blocks, gain_blocks, gain_wide,
):
    wide, d_w, r_w, d_n, kv_n, pair, d_pad = sizes
    narrow = 2 * pair
    width = wide * d_w
    rows = hr_ref.shape[0] // batches

    def natural(field):
        for index in range(narrow):
            n_blocks[n_order[index]] = field[:, index * d_pad : (index + 1) * d_pad]
        return side([n_blocks[n][:, d_pad - d_n :] for n in range(narrow)])

    inside = jnp.concatenate([places(lengths, b, slots, (rows, 1), 0)[2] for b in range(batches)], axis=0)
    mixed = natural(jnp.where(inside, hr_ref[...] + mix_ref[...], 0.0))
    for b in range(batches):
        mixed_ref[b] = mixed[b * rows : (b + 1) * rows].T.astype(BF)
    gain = gain_rows(sizes, own_ref, other_ref, n_order, gain_blocks)
    for w in range(wide):
        gain_wide[w] = zeros_beside(gain[:, w * d_w : (w + 1) * d_w], r_w, False)
    gain = side([gain_wide[w_order[p]] for p in range(wide)])
    field = tw_ref[...].astype(F32)
    scale = lax.rsqrt(mean_of(field * field, width) + EPS)
    normed = field * scale
    normed_grad = back_ref[...] * gain
    grad = scale * (normed_grad - normed * mean_of(normed_grad * normed, width))
    for p in range(wide):
        d_blocks[w_order[p]] = grad[:, p * r_w : (p + 1) * r_w]
    grad = side([d_blocks[w][:, :d_w] for w in range(wide)])
    grad = natural(gh_ref[...]) + grad
    for b in range(batches):
        grad_ref[b] = grad[b * rows : (b + 1) * rows].T.astype(BF)


def results_kernel(sizes, *refs):
    wide, d_w, r_w, d_n, kv_n, pair, d_pad = sizes
    *a_refs, moved_ref, kept_ref, first_ref = refs[: len(refs) - 9]
    query, key, value, output, gate, up, down, first_gain, second_gain = refs[len(refs) - 9 :]
    total = a_refs[0][...].astype(F32)
    for ref in a_refs[1:]:
        total = total + ref[...].astype(F32)
    turned = total[:d_n].T
    query[...] = turned[:d_w]
    first_gain[...] = turned[d_w : d_w + 1]
    key[...] = total[d_n : d_n + kv_n, :d_w]
    value[...] = total[d_n + kv_n : d_n + 2 * kv_n, :d_w]
    rest = moved_ref[...].astype(F32) + kept_ref[...].astype(F32)
    units = (rest.shape[0] - r_w) // 3
    first_units = first_ref.shape[1]
    for kind, ref in enumerate((gate, up, down)):
        ref[:first_units] = first_ref[kind, :, d_pad - d_n :]
        ref[first_units:] = rest[kind * units : (kind + 1) * units, d_pad - d_n :]
    block = rest[3 * units :]
    output[...] = block[:d_w, d_pad - d_n :]
    second_gain[...] = block[d_w : d_w + 1, d_pad - d_n :]


VMEM = pl.BlockSpec(memory_space=pltpu.VMEM)
SMEM = pl.BlockSpec(memory_space=pltpu.SMEM)


def shaped(shape, dtype):
    return jax.ShapeDtypeStruct(shape, dtype)


def scratch(*shape, dtype=F32):
    return pltpu.VMEM(shape, dtype)


def call(name, kernel, operands, out_shapes, scratches, multiply_adds, megabytes, orders=(), transcendentals=0, aliases=None, anywhere=0):
    out_specs = [VMEM] * (len(out_shapes) - anywhere) + [pl.BlockSpec(memory_space=pl.ANY)] * anywhere
    return pl.pallas_call(
        kernel,
        in_specs=[SMEM] * len(orders) + [VMEM] * len(operands),
        out_specs=out_specs,
        out_shape=out_shapes,
        scratch_shapes=scratches,
        input_output_aliases=aliases or {},
        compiler_params=pltpu.CompilerParams(vmem_limit_bytes=megabytes * 1024 * 1024),
        cost_estimate=pl.CostEstimate(
            flops=2 * multiply_adds,
            bytes_accessed=sum(a.size * a.dtype.itemsize for a in list(operands) + list(out_shapes)),
            transcendentals=transcendentals,
        ),
        name=name,
    )(*orders, *operands)


FEED_MEGABYTES = (18, 22)


def feed_kernel(chained, rows_ref, grads_ref, own_ref, other_ref, *refs):
    before = refs[:2] if chained else ()
    mix_ref, back_ref, own_out, *other_out = refs[len(before) : -3 - 2 * chained]
    hidden, gate_part, up_part = refs[-3:] if not chained else refs[-5:-2]
    if chained:
        far_out, other_out = other_out[0], [refs[-2]]
    pair, wide = own_out.shape[:2]
    units, lanes = own_ref.shape[-2:]
    narrow = 2 * pair
    total = wide * units

    def weight(kind, lo=0, count=total):
        blocks = [
            (own_ref, other_ref)[index // pair][index % pair, :, kind].reshape(total, lanes)
            for index in range(narrow)
        ]
        return side([block[lo : lo + count] for block in blocks])

    rows_in = rows_ref[...]
    grad_in = grads_ref[...]
    step = 256
    for lo in range(0, total, step):
        gate_value = dot(rows_in, weight(0, lo, step), NT)
        up_value = dot(rows_in, weight(1, lo, step), NT)
        hidden_grad = dot(grad_in, weight(2, lo, step), NT)
        sigmoid_gate = 1.0 / (1.0 + jnp.exp(-gate_value))
        silu = gate_value * sigmoid_gate
        hidden[:, lo : lo + step] = (silu * up_value).astype(BF)
        gate_part[:, lo : lo + step] = (
            hidden_grad * up_value * (sigmoid_gate * (1.0 + gate_value * (1.0 - sigmoid_gate)))
        ).astype(BF)
        up_part[:, lo : lo + step] = (hidden_grad * silu).astype(BF)
    part = max(wide // 4, 1)
    for kind, (left, right) in enumerate(((gate_part, rows_in), (up_part, rows_in), (hidden, grad_in))):
        for first in range(0, wide, part):
            term = dot(left[:, first * units : (first + part) * units], right, TN).astype(BF)
            for index in range(narrow):
                ref = own_out if index < pair else other_out[kind % len(other_out)]
                block = term[:, index * lanes : (index + 1) * lanes].reshape(part, units, lanes)
                to = slice(first, first + part)
                if len(ref.shape) == 5:
                    ref[index % pair, to, kind] = block
                elif ref.shape[2] == units:
                    ref[index % pair, to] = block
                else:
                    ref[index % pair, to, kind * units : (kind + 1) * units] = block
    if chained:
        leaving = pltpu.make_async_copy(other_out[0], far_out, refs[-1])
        leaving.start()
    mix = dot(hidden[...], weight(2), NN)
    mix_ref[...] = before[0][...] + mix if chained else mix
    back = dot(gate_part[...], weight(0), NN) + dot(up_part[...], weight(1), NN)
    back_ref[...] = before[1][...] + back if chained else back
    if chained:
        leaving.wait()


def feed_call(rows_in, grad_in, own, other, before=(), flat=False):
    pair, wide, _, units, lanes = own.shape
    rows, width = rows_in.shape
    total = wide * units
    own_shape = (3 * units, lanes) if flat else (3, units, lanes)
    other_shapes = [own_shape] if flat else [(units, lanes)] * 3
    return call(
        "feed_forward",
        functools.partial(feed_kernel, bool(before)),
        (rows_in, grad_in, own, other, *before),
        [shaped((rows, width), F32)] * 2
        + [shaped((pair, wide, *shape), BF) for shape in [own_shape, *other_shapes]],
        [scratch(rows, total, dtype=BF)] * 3
        + ([scratch(pair, wide, *own_shape, dtype=BF), pltpu.SemaphoreType.DMA] if before else []),
        9 * rows * width * total,
        FEED_MEGABYTES[flat],
        transcendentals=rows * total,
        aliases={4: 0, 5: 1} if before else None,
        anywhere=1 if before else 0,
    )


AXES = ("wide", "narrow")


class Grid:
    def __init__(self):
        self.wide = lax.axis_size("wide")
        self.narrow = lax.axis_size("narrow")
        self.outer = 4
        self.inner = self.wide // 4
        self.pair = self.narrow // 2
        self.size = {"outer": 4, "inner": self.inner, "pair": self.pair, "core": 2}
        self.stride = {"outer": self.inner * self.narrow, "inner": self.narrow, "pair": 2, "core": 1}
        linear = lax.axis_index("wide") * self.narrow + lax.axis_index("narrow")
        self.at = {name: (linear // self.stride[name]) % self.size[name] for name in self.size}

    def shift(self, value, name, count=1):
        size, stride = self.size[name], self.stride[name]
        pairs = []
        for source in range(self.wide * self.narrow):
            digit = (source // stride) % size
            pairs.append((source, source + ((digit + count) % size - digit) * stride))
        return lax.ppermute(value, AXES, pairs)

    def behind(self, name, steps):
        return (self.at[name] + (self.size[name] - steps)) % self.size[name]


def after(value, others):
    if not others:
        return value
    return lax.optimization_barrier((value, *others))[0]


class Flow:
    def __init__(self, make, grid, *args):
        self.grid = grid
        self.gates = ()
        self.last = ()
        self.result = None
        self.more = ()
        self.run = make(self, *args)

    def step(self, *others):
        self.gates = others
        try:
            self.last = next(self.run)
        except StopIteration as stop:
            self.result = stop.value
            return self.result
        return None

    def finish(self):
        while self.result is None:
            self.step()
        return self.result

    def shift(self, value, name, count=1):
        return self.grid.shift(after(value, self.gates), name, count)

    def settle(self, value):
        return after(value, self.gates)


class Clock:
    def __init__(self):
        self.held = ()

    def now(self, value):
        return after(value, self.held)

    def phase(self, *starts, done=(), wait=(), leave=()):
        gates = self.held + tuple(done)
        for flow, steps in starts:
            for _ in range(steps):
                flow.step(*gates)
        flows = [flow for flow, _ in starts if flow not in leave] + list(wait)
        held = sum([tuple(flow.last) for flow in flows], tuple(done))
        if not starts:
            held = self.held + held
        self.held = held if held else self.held


def both_rings(flow, first, first_name, second, second_name):
    one, two = [first], [second]
    for at in range(max(flow.grid.size[first_name], flow.grid.size[second_name]) - 1):
        if at < flow.grid.size[first_name] - 1:
            one.append(flow.shift(one[-1], first_name))
        if at < flow.grid.size[second_name] - 1:
            two.append(flow.shift(two[-1], second_name))
        yield (one[-1], two[-1])
        if at < flow.grid.size[first_name] - 1:
            one[-1] = flow.settle(one[-1])
        if at < flow.grid.size[second_name] - 1:
            two[-1] = flow.settle(two[-1])
    return one, two


def gather_outer(flow, shard):
    moved = [flow.shift(shard, "outer", count) for count in range(1, flow.grid.outer)]
    yield tuple(moved)
    return [shard] + [flow.settle(block) for block in moved]


def gather_ring(flow, shard):
    blocks = [shard]
    for _ in range(flow.grid.outer - 1):
        blocks.append(flow.shift(blocks[-1], "outer"))
        yield (blocks[-1],)
        blocks[-1] = flow.settle(blocks[-1])
    return blocks


def gather_plane(flow, blocks, cut):
    stacked = lax.optimization_barrier(jnp.stack(blocks))
    first, second = stacked[..., :cut, :], stacked[..., cut:, :]
    one, two = yield from both_rings(flow, first, "inner", second, "pair")
    one, two = yield from both_rings(flow, jnp.concatenate(one), "pair", jnp.stack(two), "inner")
    own = jnp.concatenate([jnp.stack(one), jnp.concatenate(two, axis=1)], axis=-2)
    other = flow.shift(own, "core")
    yield (other,)
    return own, other


def both_sums(flow, first, first_name, second, second_name):
    sizes = flow.grid.size
    one, two = first(1), second(1)
    for step in range(1, max(sizes[first_name], sizes[second_name])):
        moved = []
        if step < sizes[first_name]:
            one = flow.shift(one, first_name)
            moved.append(one)
        if step < sizes[second_name]:
            two = flow.shift(two, second_name)
            moved.append(two)
        yield tuple(moved)
        if step < sizes[first_name]:
            one = flow.settle(one)
            one = one + first(step + 1) if step < sizes[first_name] - 1 else one
        if step < sizes[second_name]:
            two = flow.settle(two)
            two = two + second(step + 1) if step < sizes[second_name] - 1 else two
    return one, two


def scatter_plane(flow, own, other, cut):
    outer = flow.grid.outer
    if isinstance(other, tuple):
        moved = tuple(flow.shift(part, "core") for part in other)
        yield moved
        moved = [flow.settle(part) for part in moved]
        moved = jnp.stack(moved, axis=2) if own.ndim == 5 else jnp.concatenate(moved, axis=2)
    else:
        moved = flow.shift(other, "core")
        yield (moved,)
        moved = flow.settle(moved)
    more = None
    if flow.more:
        more = flow.shift(flow.more[1], "core")
        yield (more,)
        more = flow.settle(more)

    def wide_part(r):
        return slice(r * outer, (r + 1) * outer)

    def first(r, part=slice(None)):
        return moved[r, part, ..., :cut, :] + own[r, part, ..., :cut, :]

    def second(r, at=slice(None)):
        part = wide_part(r)
        block = moved[at, part, ..., cut:, :] + own[at, part, ..., cut:, :]
        if more is None:
            return block
        return jnp.concatenate([block, more[at, part] + flow.more[0][at, part]], axis=-2)

    one, two = yield from both_sums(flow, first, "pair", second, "inner")

    def first_next(r):
        return one[wide_part(r)] + first(0, wide_part(r))

    def second_next(r):
        return two[r] + second(0, r)

    last = yield from both_sums(flow, first_next, "inner", second_next, "pair")
    return jnp.concatenate([last[0] + first_next(0), last[1] + second_next(0)], axis=-2)


def scatter_outer(flow, sums):
    outer = flow.grid.outer
    moved = [flow.shift(sums[r], "outer", outer - r) for r in range(1, outer)]
    yield tuple(moved)
    return [flow.settle(block) for block in moved] + [sums[0]]


def scatter_split(flow, sums):
    outer = flow.grid.outer
    moved = [flow.shift(sums[r], "outer", outer - r) for r in range(2, outer)]
    yield tuple(moved)
    moved = [flow.settle(block) for block in moved]
    moved.append(flow.shift(sums[1], "outer", outer - 1))
    yield tuple(moved[-1:])
    return sum([flow.settle(block).astype(F32) for block in moved], sums[0].astype(F32))


def scatter_ring(flow, sums):
    outer = flow.grid.outer
    total = sums[1]
    for step in range(1, outer):
        total = flow.shift(total, "outer")
        yield (total,)
        total = flow.settle(total)
        if step < outer - 1:
            total = (total.astype(F32) + sums[step + 1].astype(F32)).astype(BF)
    return [total, sums[0]]


def rounded_up(count, step):
    return -(-count // step) * step
GRANTS = {
    "prepare_narrow": 16,
    "prepare_wide": 12,
    "project": 24,
    "attend": 12,
    "residual": 20,
    "middle": 24,
    "attend_back": 20,
    "weights": 28,
    "outputs": 28,
    "results": 10,
}


def body(
    tokens,
    lengths,
    cotangent,
    query_weight,
    key_matrix,
    value_matrix,
    output_weight,
    gate_weight,
    up_weight,
    down_weight,
    attention_gain,
    feedforward_gain,
):
    grid = Grid()
    batches, bucket_rows, width = tokens.shape
    rows = batches * bucket_rows
    wide, narrow, pair, inner, outer = grid.wide, grid.narrow, grid.pair, grid.inner, grid.outer
    d_w, d_n = query_weight.shape
    kv_n = key_matrix.shape[1]
    f_w = down_weight.shape[0]
    d_pad = rounded_up(d_n, 128)
    r_w = rounded_up(d_w + 1, 64)
    taken = d_n + 2 * kv_n
    t_rows = rounded_up(taken, 16)
    sizes = (wide, d_w, r_w, d_n, kv_n, pair, d_pad)

    packed = jnp.concatenate([query_weight.T, key_matrix.T, value_matrix.T], axis=0)
    gain_column = jnp.concatenate([attention_gain, jnp.zeros((2 * kv_n,), BF)])[:, None]
    packed = jnp.concatenate([packed, gain_column, jnp.zeros((taken, r_w - d_w - 1), BF)], axis=1)
    a_shard = jnp.pad(packed, ((0, t_rows - taken), (0, 0)))
    a_cut = rounded_up(t_rows // 2, 16)
    o_shard = jnp.concatenate([output_weight, feedforward_gain[None], jnp.zeros((r_w - d_w - 1, d_n), BF)])
    f_shard = jnp.stack([gate_weight.T, up_weight.T, down_weight])
    sub = 256 // wide
    tiles_in = f_w // sub
    bounds = [0, 4 * tiles_in // 10 * sub, f_w]
    shards = [f_shard[:, lo:hi] for lo, hi in zip(bounds, bounds[1:])]
    shards[0] = jnp.concatenate([shards[0], o_shard[None]])
    shards = [jnp.pad(shard, ((0, 0), (0, 0), (d_pad - d_n, 0))) for shard in shards]
    cuts = [shard.shape[1] // 2 for shard in shards]

    place = jnp.arange(wide, dtype=jnp.int32)
    w_order = (grid.at["outer"] - place % outer) % outer * inner
    w_order = (w_order + (grid.at["inner"] - place // outer) % inner).astype(jnp.int32)
    place = jnp.arange(narrow, dtype=jnp.int32)
    n_order = (grid.at["pair"] - place % pair) % pair * 2
    n_order = (n_order + (grid.at["core"] - place // pair) % 2).astype(jnp.int32)
    slots = lengths.shape[2]
    orders = (w_order, n_order, lengths.reshape(-1))
    freqs = THETA ** (-jnp.arange(HEAD_WIDTH // 2, dtype=F32) * 2.0 / HEAD_WIDTH)
    freqs = jnp.concatenate([freqs] * 4)[None]

    flow_za = Flow(gather_outer, grid, a_shard)
    flow_z1 = Flow(gather_ring, grid, shards[0])
    flow_z2 = Flow(gather_ring, grid, shards[1])
    plane = max(inner, pair) - 1
    clock = Clock()
    clock.phase((flow_za, 1), (flow_z1, 1), leave=(flow_za, flow_z1))
    token_rows = tokens.reshape(rows, width)
    cotangent_rows = cotangent.reshape(rows, width)
    token_narrow, branch_grad = call(
        "prepare_narrow",
        functools.partial(prepare_narrow_kernel, sizes, batches, slots),
        (token_rows, cotangent_rows),
        [shaped((rows, narrow * d_pad), BF)] * 2,
        [scratch(narrow, rows, d_pad, dtype=BF)] * 2,
        0,
        GRANTS["prepare_narrow"],
        orders=orders,
    )
    clock.phase(done=(token_narrow,), wait=(flow_za, flow_z1))
    flow_a = Flow(gather_plane, grid, flow_za.finish(), a_cut)
    clock.phase((flow_a, plane), (flow_z1, 1), leave=(flow_a, flow_z1))
    token_wide, cosine, sine = call(
        "prepare_wide",
        functools.partial(prepare_wide_kernel, sizes, batches, slots),
        (clock.now(token_rows), freqs),
        [shaped((rows, wide * r_w), BF), shaped((rows, 128), F32), shaped((rows, 128), F32)],
        [scratch(wide, rows, r_w, dtype=BF)],
        0,
        GRANTS["prepare_wide"],
        orders=orders,
    )
    clock.phase(done=(token_wide,), wait=(flow_a, flow_z1))
    clock.phase((flow_a, plane), (flow_z1, 1))
    flow_1 = Flow(gather_plane, grid, flow_z1.finish(), cuts[0])
    clock.phase((flow_a, 1), (flow_1, plane), (flow_z2, 1), leave=(flow_1, flow_z2))
    a_own, a_other = flow_a.finish()
    a_in, query, key, value = call(
        "project",
        functools.partial(project_kernel, sizes),
        (clock.now(token_wide), cosine, sine, a_own, a_other),
        [
            shaped((rows, wide * r_w), BF),
            shaped((rows, QUERY_HEADS * HEAD_WIDTH), BF),
            shaped((rows, KEY_VALUE_HEADS * HEAD_WIDTH), BF),
            shaped((rows, KEY_VALUE_HEADS * HEAD_WIDTH), BF),
        ],
        [scratch(narrow, rows, t_rows), scratch(narrow, 1, t_rows), scratch(wide, 1, r_w)],
        rows * wide * r_w * narrow * t_rows,
        GRANTS["project"],
        orders=orders,
    )

    clock.phase(done=(query,), wait=(flow_1, flow_z2))
    clock.phase((flow_1, plane), (flow_z2, 1), leave=(flow_1, flow_z2))

    def by_bucket(field):
        return field.reshape(batches, bucket_rows, field.shape[-1])

    group = QUERY_HEADS // KEY_VALUE_HEADS
    steps = bucket_rows // 128
    p_shape = (KEY_VALUE_HEADS, group * 128, 128 * steps * (steps + 1) // 2)
    query, key, value = by_bucket(query), by_bucket(key), by_bucket(value)
    pair_work = QUERY_HEADS * bucket_rows * bucket_rows * HEAD_WIDTH
    attended, probs = [], []
    for b in range(batches):
        parts = call(
            "attend",
            functools.partial(attend_kernel, slots, b),
            (clock.now(query), key, value),
            [shaped(query.shape[1:], BF), shaped(p_shape, BF)],
            [],
            6 * pair_work,
            GRANTS["attend"],
            orders=orders,
            transcendentals=QUERY_HEADS * bucket_rows * bucket_rows,
        )
        attended.append(parts[0])
        probs.append(parts[1])
        if b < batches - 1:
            clock.phase(done=(parts[0],), wait=(flow_z2,))
            clock.phase((flow_z2, 1), leave=(flow_z2,))
    clock.phase(done=tuple(attended), wait=(flow_1, flow_z2))
    flow_2 = Flow(gather_plane, grid, flow_z2.finish(), cuts[1])
    clock.phase((flow_1, 1), (flow_2, plane), leave=(flow_2,))
    first_own, first_other = flow_1.finish()
    o_operands = (first_own[:, :, 3], first_other[:, :, 3])
    d_lanes = narrow * d_pad
    attended_wide, residual, feed_in = call(
        "residual",
        functools.partial(residual_kernel, sizes, batches),
        (clock.now(token_narrow), *o_operands, *attended),
        [
            shaped((rows, wide * r_w), BF),
            shaped((rows, d_lanes), F32),
            shaped((rows, d_lanes), BF),
        ],
        [scratch(wide, rows, r_w, dtype=BF)],
        rows * wide * r_w * d_lanes,
        GRANTS["residual"],
        orders=orders,
    )

    clock.phase(done=(feed_in,), wait=(flow_2,))
    clock.phase((flow_2, plane), leave=(flow_2,))
    *sums_so_far, own_terms, gate_terms, up_terms, down_terms = feed_call(
        clock.now(feed_in), branch_grad, first_own, first_other
    )
    back_1 = Flow(scatter_plane, grid, own_terms, (gate_terms, up_terms, down_terms), cuts[0])
    clock.phase(done=(own_terms,))
    clock.phase((back_1, 1), wait=(flow_2,))
    clock.phase((flow_2, 1), (back_1, plane), leave=(back_1,))
    *sums_so_far, own_terms, other_terms = feed_call(
        clock.now(feed_in), branch_grad, *flow_2.finish(), tuple(sums_so_far), True
    )
    back_2 = Flow(
        scatter_plane,
        grid,
        own_terms,
        other_terms,
        rounded_up((own_terms.shape[2] + r_w) // 2, 16),
    )
    clock.phase(done=(own_terms,), wait=(back_1,))
    clock.phase((back_1, plane), (back_2, 1), leave=(back_1, back_2))
    mix, back = sums_so_far
    grad, attended_grad, own_o, other_o = call(
        "middle",
        functools.partial(middle_kernel, sizes),
        (clock.now(residual), back, branch_grad, attended_wide) + o_operands,
        [
            shaped((rows, d_lanes), F32),
            shaped((rows, width), BF),
            shaped((pair, wide, r_w, d_pad), BF),
            shaped((pair, wide, r_w, d_pad), BF),
        ],
        [scratch(wide, rows, r_w)],
        2 * rows * wide * r_w * d_lanes,
        GRANTS["middle"],
        orders=orders,
    )
    clock.phase(done=(attended_grad,), wait=(back_1, back_2))
    back_2.more = (own_o, other_o)
    clock.phase((back_2, 1))
    back_z1 = Flow(scatter_split, grid, back_1.finish())
    clock.phase((back_2, plane), (back_z1, 1), leave=(back_2, back_z1))
    by_parts = (by_bucket(attended_grad), by_bucket(cosine), by_bucket(sine))
    shapes = [x.shape[1:] for x in (query, key, value)]
    grads = []
    for b in range(batches):
        grads.append(
            call(
                "attend_back",
                functools.partial(attend_back_kernel, b),
                (clock.now(query), key, value, attended[b], by_parts[0], probs[b], *by_parts[1:]),
                [shaped(shape, BF) for shape in shapes],
                [scratch(*shape) for shape in shapes],
                12 * pair_work,
                GRANTS["attend_back"],
                orders=orders,
            )
        )
        if b < batches - 1:
            clock.phase(done=tuple(grads[b][:1]), wait=(back_z1,))
            clock.phase((back_z1, 1), leave=(back_z1,))
    clock.phase(done=tuple(x[0] for x in grads), wait=(back_2, back_z1))
    clock.phase((back_2, plane), leave=(back_2,))
    operands = tuple(x for parts in zip(*grads) for x in parts)
    cuts_a = [0, rounded_up(t_rows // 3, 16), rounded_up(2 * t_rows // 3, 16), t_rows]
    wide_back, own_terms, *other_terms = call(
        "weights",
        functools.partial(weights_kernel, sizes, batches),
        (clock.now(token_wide), a_in, a_own, a_other) + operands,
        [shaped((rows, wide * r_w), F32), shaped(a_own.shape, BF)]
        + [shaped((pair, wide, hi - lo, r_w), BF) for lo, hi in zip(cuts_a, cuts_a[1:])],
        [scratch(narrow, rows, t_rows, dtype=BF), scratch(narrow, 1, t_rows), scratch(wide, 1, r_w)],
        2 * rows * wide * r_w * narrow * t_rows,
        GRANTS["weights"],
        orders=orders,
    )
    back_a = Flow(scatter_plane, grid, own_terms, tuple(other_terms), a_cut)
    clock.phase(done=(own_terms,))
    clock.phase((back_a, 1), wait=(back_2,))
    back_z2 = Flow(scatter_ring, grid, back_2.finish())
    clock.phase((back_a, plane), (back_z2, 1), leave=(back_a, back_z2))
    mixed, tokens_grad = call(
        "outputs",
        functools.partial(outputs_kernel, sizes, batches, slots),
        (clock.now(residual), mix, grad, token_wide, wide_back, a_own, a_other),
        [shaped((batches, width, bucket_rows), BF)] * 2,
        [
            scratch(narrow, rows, d_pad),
            scratch(wide, rows, r_w),
            scratch(narrow, 1, t_rows),
            scratch(wide, 1, r_w),
        ],
        0,
        GRANTS["outputs"],
        orders=orders,
    )
    clock.phase(done=(mixed,), wait=(back_z2,))
    clock.phase((back_z2, 1), wait=(back_a,), leave=(back_z2,))
    clock.phase((back_a, plane), wait=(back_z2,))
    back_za = Flow(scatter_outer, grid, back_a.finish())
    clock.phase((back_z2, 1), (back_za, 1), leave=(back_z2, back_za))
    outputs = call(
        "results",
        functools.partial(results_kernel, sizes),
        (*back_za.finish(), *back_z2.finish(), back_z1.finish()),
        [
            shaped(shape, F32)
            for shape in [(d_w, d_n), (kv_n, d_w), (kv_n, d_w), (d_w, d_n), *[(f_w, d_n)] * 3, (1, d_n), (1, d_n)]
        ],
        [],
        0,
        GRANTS["results"],
    )
    query_grad, key_grad, value_grad, output_grad, gate_grad, up_grad, down_grad, *gain_grads = outputs
    return (
        jnp.swapaxes(mixed, 1, 2),
        jnp.swapaxes(tokens_grad, 1, 2),
        query_grad,
        key_grad.T,
        value_grad.T,
        output_grad,
        gate_grad.T,
        up_grad.T,
        down_grad,
        gain_grads[0][0],
        gain_grads[1][0],
    )


def solution(mesh):
    in_specs = (
        P(None, ("wide", "narrow"), None),
        P(None, ("wide", "narrow"), None),
        P(None, ("wide", "narrow"), None),
        P("wide", "narrow"),
        P("wide", "narrow"),
        P("wide", "narrow"),
        P("wide", "narrow"),
        P("narrow", "wide"),
        P("narrow", "wide"),
        P("wide", "narrow"),
        P("narrow"),
        P("narrow"),
    )
    out_specs = (
        P(None, ("wide", "narrow"), None),
        P(None, ("wide", "narrow"), None),
        P("wide", "narrow"),
        P("wide", "narrow"),
        P("wide", "narrow"),
        P("wide", "narrow"),
        P("narrow", "wide"),
        P("narrow", "wide"),
        P("wide", "narrow"),
        P("narrow"),
        P("narrow"),
    )
    return jax.shard_map(body, mesh=mesh, in_specs=in_specs, out_specs=out_specs, check_vma=False)
```

```python
import functools

import jax
import jax.numpy as jnp
from jax import lax
from jax.experimental import pallas as pl
from jax.experimental.pallas import tpu as pltpu
from jax.sharding import PartitionSpec as P

QUERY_HEADS = 15
KEY_VALUE_HEADS = 5
HEAD_WIDTH = 64


EPS = 1e-05
THETA = 10000.0


def segments_of(lengths_row, count_of_rows):
    ends = jnp.cumsum(lengths_row, dtype=jnp.int32)
    starts = ends - lengths_row
    places = jnp.arange(count_of_rows, dtype=jnp.int32)
    segment = jnp.sum((places[:, None] >= ends[None, :]).astype(jnp.int32), axis=1, dtype=jnp.int32)
    slot_ids = jnp.arange(lengths_row.shape[0], dtype=jnp.int32)
    opening = jnp.sum(
        jnp.where(segment[:, None] == slot_ids[None, :], starts[None, :], 0),
        axis=1,
        dtype=jnp.int32,
    )
    opening = jnp.where(segment == lengths_row.shape[0], ends[-1], opening)
    return (segment, places - opening)


F32 = jnp.float32
BF = jnp.bfloat16
NT = (((1,), (1,)), ((), ()))
TN = (((0,), (0,)), ((), ()))
NN = (((1,), (0,)), ((), ()))


def dot(left, right, dims):
    return lax.dot_general(left, right, dims, preferred_element_type=F32)


def side(parts):
    return parts[0] if len(parts) == 1 else jnp.concatenate(parts, axis=1)


def mean_of(field, width):
    return jnp.sum(field, axis=1, keepdims=True) * (1.0 / width)


def row_of(block, row):
    at = lax.broadcasted_iota(jnp.int32, (block.shape[0], 1), 0)
    return jnp.sum(jnp.where(at == row, block.astype(F32), 0.0), axis=0, keepdims=True)


def zeros_beside(field, lanes, before):
    pad = jnp.zeros((field.shape[0], lanes - field.shape[1]), field.dtype)
    return side([pad, field] if before else [field, pad])


def turn(field, cosine, sine):
    lane = lax.broadcasted_iota(jnp.int32, (1, 128), 1)
    low = (lane % 64) < 32
    tiles = []
    for start in range(0, field.shape[1], 128):
        piece = field[:, start : start + 128]
        count = piece.shape[1]
        if count < 128:
            piece = zeros_beside(piece, 128, False)
        other = jnp.where(low, pltpu.roll(piece, 96, 1), pltpu.roll(piece, 32, 1))
        tiles.append((piece * cosine + other * sine)[:, :count])
    return side(tiles)


def places(lengths, bucket, slots, shape, axis):
    at = lax.broadcasted_iota(jnp.int32, shape, axis)
    end = jnp.int32(0)
    segment = jnp.zeros(shape, jnp.int32)
    opening = jnp.zeros(shape, jnp.int32)
    for slot in range(slots):
        length = lengths[bucket * slots + slot]
        end = end + length
        over = at >= end
        segment += jnp.where(over, 1, 0)
        opening += jnp.where(over, length, 0)
    return segment, at - opening, segment < slots


def prepare_narrow_kernel(sizes, batches, slots, w_order, n_order, lengths, tok_ref, cot_ref, tn_ref, gf_ref, n_blocks, c_blocks):
    wide, d_w, r_w, d_n, kv_n, pair, d_pad = sizes
    narrow = 2 * pair
    rows = tok_ref.shape[0] // batches
    for b in range(batches):
        part = slice(b * rows, (b + 1) * rows)
        _, _, inside = places(lengths, b, slots, (rows, 1), 0)
        field = tok_ref[part].astype(F32)
        upstream = jnp.where(inside, cot_ref[part].astype(F32), 0.0)
        for n in range(narrow):
            n_blocks[n, part] = zeros_beside(field[:, n * d_n : (n + 1) * d_n], d_pad, True).astype(BF)
            c_blocks[n, part] = zeros_beside(upstream[:, n * d_n : (n + 1) * d_n], d_pad, True).astype(BF)
    tn_ref[...] = side([n_blocks[n_order[index]] for index in range(narrow)])
    gf_ref[...] = side([c_blocks[n_order[index]] for index in range(narrow)])


def prepare_wide_kernel(sizes, batches, slots, w_order, n_order, lengths, tok_ref, freq_ref, tw_ref, cos_ref, sin_ref, w_blocks):
    wide, d_w, r_w, d_n, kv_n, pair, d_pad = sizes
    rows = tok_ref.shape[0] // batches
    field = tok_ref[...].astype(F32)
    for w in range(wide):
        w_blocks[w] = zeros_beside(field[:, w * d_w : (w + 1) * d_w], r_w, False).astype(BF)
    tw_ref[...] = side([w_blocks[w_order[p]] for p in range(wide)])
    sign = jnp.where(lax.broadcasted_iota(jnp.int32, (1, 128), 1) % 64 < 32, -1.0, 1.0)
    for b in range(batches):
        part = slice(b * rows, (b + 1) * rows)
        _, position, _ = places(lengths, b, slots, (rows, 1), 0)
        angle = position.astype(F32) * freq_ref[...]
        cos_ref[part] = jnp.cos(angle)
        sin_ref[part] = jnp.sin(angle) * sign


def beside(ref, at):
    return side([ref[at, p] for p in range(ref.shape[1])])


def gain_rows(sizes, own_ref, other_ref, n_order, gain_blocks):
    wide, d_w, r_w, d_n, kv_n, pair, d_pad = sizes
    lane = lax.broadcasted_iota(jnp.int32, (16, r_w), 1)
    chosen = jnp.where(lane == d_w, 1.0, 0.0).astype(BF)
    for index in range(2 * pair):
        block = (own_ref, other_ref)[index // pair][index % pair, 0]
        gain_blocks[n_order[index]] = dot(chosen, block, NT)[:1]
    return side([gain_blocks[n][:, :d_n] for n in range(2 * pair)])


def project_kernel(
    sizes, w_order, n_order, lengths, tw_ref, cos_ref, sin_ref, own_ref, other_ref,
    a_ref, q_ref, k_ref, v_ref, projected, gain_blocks, gain_wide,
):
    wide, d_w, r_w, d_n, kv_n, pair, d_pad = sizes
    narrow = 2 * pair
    width = wide * d_w
    gain = gain_rows(sizes, own_ref, other_ref, n_order, gain_blocks)
    for w in range(wide):
        gain_wide[w] = zeros_beside(gain[:, w * d_w : (w + 1) * d_w], r_w, False)
    field = tw_ref[...].astype(F32)
    scale = lax.rsqrt(mean_of(field * field, width) + EPS)
    a_wide = (field * scale * side([gain_wide[w_order[p]] for p in range(wide)])).astype(BF)
    a_ref[...] = a_wide
    for index in range(narrow):
        block = beside((own_ref, other_ref)[index // pair], index % pair)
        projected[n_order[index]] = dot(a_wide, block, NT)
    cosine, sine = cos_ref[...], sin_ref[...]

    def taken(start, count):
        return side([projected[n][:, start : start + count] for n in range(narrow)])

    q_ref[...] = (turn(taken(0, d_n), cosine, sine) * HEAD_WIDTH**-0.5).astype(BF)
    k_ref[...] = turn(taken(d_n, kv_n), cosine, sine).astype(BF)
    v_ref[...] = taken(d_n + kv_n, kv_n).astype(BF)


def attend_kernel(slots, bucket, w_order, n_order, lengths, q_ref, k_ref, v_ref, ob_ref, p_ref):
    rows = q_ref.shape[1]
    seg_row, _, _ = places(lengths, bucket, slots, (1, rows), 1)
    seg_col, _, _ = places(lengths, bucket, slots, (rows, 1), 0)
    step = 128
    group = QUERY_HEADS // KEY_VALUE_HEADS
    head = HEAD_WIDTH
    offset = 0
    for i in range(rows // step):
        upto = (i + 1) * step
        query_at = i * step + lax.broadcasted_iota(jnp.int32, (step, upto), 0)
        key_at = lax.broadcasted_iota(jnp.int32, (step, upto), 1)
        same = seg_col[i * step : upto] == seg_row[:, :upto]
        bias = jnp.where(same & (key_at <= query_at), 0.0, -1000000000.0)
        for g in range(KEY_VALUE_HEADS):
            queries = jnp.concatenate(
                [
                    q_ref[bucket, i * step : upto, (g * group + j) * head : (g * group + j + 1) * head]
                    for j in range(group)
                ],
                axis=0,
            )
            keys = k_ref[bucket, :upto, g * head : (g + 1) * head]
            values = v_ref[bucket, :upto, g * head : (g + 1) * head]
            logits = dot(queries, keys, NT).reshape(group, step, upto) + bias[None]
            peak = jnp.max(logits, axis=-1, keepdims=True)
            shifted = jnp.exp(logits - peak)
            total = jnp.sum(shifted, axis=-1, keepdims=True)
            probs = (shifted * (1.0 / total)).astype(BF).reshape(group * step, upto)
            p_ref[g, :, offset : offset + upto] = probs
            out = dot(probs, values, NN).astype(BF)
            ob_ref[i * step : upto, g * group * head : (g + 1) * group * head] = side(
                [out[j * step : (j + 1) * step] for j in range(group)]
            )
        offset += upto


def residual_kernel(
    sizes, batches, w_order, n_order, lengths, tn_ref, own_ref, other_ref, *refs
):
    ob_wide_ref, hr_ref, bf_ref, e_blocks = refs[batches:]
    wide, d_w, r_w, d_n, kv_n, pair, d_pad = sizes
    narrow = 2 * pair
    spare = d_w // 16 * 16
    width = wide * d_w
    attended = jnp.concatenate([ref[...].astype(F32) for ref in refs[:batches]], axis=0)
    for w in range(wide):
        e_blocks[w] = zeros_beside(attended[:, w * d_w : (w + 1) * d_w], r_w, False).astype(BF)
    ob_wide = side([e_blocks[w_order[p]] for p in range(wide)])
    ob_wide_ref[...] = ob_wide
    blocks = []
    gains = []
    for index in range(narrow):
        block = (own_ref, other_ref)[index // pair][index % pair].reshape(wide * r_w, d_pad)
        gains.append(row_of(block[spare : spare + 16], d_w - spare))
        rows_in = tn_ref[:, index * d_pad : (index + 1) * d_pad].astype(F32)
        blocks.append(rows_in + dot(ob_wide, block, NN))
    residual = side(blocks)
    hr_ref[...] = residual
    scale = lax.rsqrt(mean_of(residual * residual, width) + EPS)
    bf_ref[...] = (residual * scale * side(gains)).astype(BF)


def middle_kernel(
    sizes, w_order, n_order, lengths, hr_ref, back_ref, gf_ref, ob_ref, own_ref, other_ref,
    gh_ref, go_ref, own_terms, other_terms, e_blocks,
):
    wide, d_w, r_w, d_n, kv_n, pair, d_pad = sizes
    narrow = 2 * pair
    spare = d_w // 16 * 16
    width = wide * d_w
    residual = hr_ref[...]
    blocks = [
        (own_ref, other_ref)[index // pair][index % pair].reshape(wide * r_w, d_pad)
        for index in range(narrow)
    ]
    gain = side([row_of(block[spare : spare + 16], d_w - spare) for block in blocks])
    back = back_ref[...]
    scale = lax.rsqrt(mean_of(residual * residual, width) + EPS)
    normed = residual * scale
    gain_term = jnp.sum(back * normed, axis=0, keepdims=True)
    here = lax.broadcasted_iota(jnp.int32, (r_w, 1), 0) == d_w
    normed_grad = back * gain
    grad = gf_ref[...].astype(F32) + scale * (
        normed_grad - normed * mean_of(normed_grad * normed, width)
    )
    gh_ref[...] = grad
    low = grad.astype(BF)
    total = None
    ob_wide = ob_ref[...]
    for index in range(narrow):
        piece = low[:, index * d_pad : (index + 1) * d_pad]
        part = dot(piece, blocks[index], NT)
        total = part if total is None else total + part
        term = dot(ob_wide, piece, TN).reshape(wide, r_w, d_pad)
        row = gain_term[:, index * d_pad : (index + 1) * d_pad]
        ref = (own_terms, other_terms)[index // pair]
        ref[index % pair] = (term + jnp.where(here, row, 0.0)[None]).astype(BF)
    for p in range(wide):
        e_blocks[w_order[p]] = total[:, p * r_w : (p + 1) * r_w]
    go_ref[...] = side([e_blocks[w][:, :d_w] for w in range(wide)]).astype(BF)


def attend_back_kernel(
    bucket, w_order, n_order, lengths, q_ref, k_ref, v_ref, ob_ref, go_ref, p_ref, cos_ref, sin_ref, gq_ref, gk_ref, gv_ref, gq_sum, gk_sum, gv_sum
):
    rows = q_ref.shape[1]
    step = 128
    group = QUERY_HEADS // KEY_VALUE_HEADS
    head = HEAD_WIDTH
    for g in range(KEY_VALUE_HEADS):
        offset = 0
        lanes = slice(g * head, (g + 1) * head)
        gk_total, gv_total = [], []
        for i in range(rows // step):
            upto = (i + 1) * step

            def stacked(ref, *at):
                return jnp.concatenate(
                    [
                        ref[(*at, slice(i * step, upto), slice((g * group + j) * head, (g * group + j + 1) * head))]
                        for j in range(group)
                    ],
                    axis=0,
                )

            queries, out_grads, outs = stacked(q_ref, bucket), stacked(go_ref, bucket), stacked(ob_ref)
            keys = k_ref[bucket, :upto, lanes]
            values = v_ref[bucket, :upto, lanes]
            probs = p_ref[g, :, offset : offset + upto]
            delta = jnp.sum(out_grads.astype(F32) * outs.astype(F32), axis=1, keepdims=True)
            prob_grad = dot(out_grads, values, NT)
            logit_grad = (probs.astype(F32) * (prob_grad - delta)).astype(BF)
            query_part = dot(logit_grad, keys, NN) * head**-0.5
            gq_sum[i * step : upto, g * group * head : (g + 1) * group * head] = side(
                [query_part[j * step : (j + 1) * step] for j in range(group)]
            )
            key_part = dot(logit_grad, queries, TN)
            value_part = dot(probs, out_grads, TN)
            for j in range(i + 1):
                if j == i:
                    gk_total.append(key_part[j * step : (j + 1) * step])
                    gv_total.append(value_part[j * step : (j + 1) * step])
                else:
                    gk_total[j] += key_part[j * step : (j + 1) * step]
                    gv_total[j] += value_part[j * step : (j + 1) * step]
            offset += upto
        gk_sum[:, lanes] = jnp.concatenate(gk_total, axis=0)
        gv_sum[:, lanes] = jnp.concatenate(gv_total, axis=0)
    cosine, sine = cos_ref[bucket], sin_ref[bucket]
    gq_ref[...] = turn(gq_sum[...], cosine, -sine).astype(BF)
    gk_ref[...] = turn(gk_sum[...], cosine, -sine).astype(BF)
    gv_ref[...] = gv_sum[...].astype(BF)


def weights_kernel(
    sizes, batches, w_order, n_order, lengths, tw_ref, a_ref, own_ref, other_ref, *refs
):
    wide, d_w, r_w, d_n, kv_n, pair, d_pad = sizes
    narrow = 2 * pair
    width = wide * d_w
    back_ref, own_terms, *other_terms, g_blocks, gain_blocks, gain_wide = refs[3 * batches :]
    count = own_ref.shape[2]
    for b in range(batches):
        gq, gk, gv = [refs[kind * batches + b][...].astype(F32) for kind in range(3)]
        bucket = slice(b * gq.shape[0], (b + 1) * gq.shape[0])
        for n in range(narrow):
            piece = side(
                [
                    gq[:, n * d_n : (n + 1) * d_n],
                    gk[:, n * kv_n : (n + 1) * kv_n],
                    gv[:, n * kv_n : (n + 1) * kv_n],
                ]
            )
            if piece.shape[1] < count:
                piece = zeros_beside(piece, count, False)
            g_blocks[n, bucket] = piece.astype(BF)
    total = None
    for index in range(narrow):
        block = beside((own_ref, other_ref)[index // pair], index % pair)
        part = dot(g_blocks[n_order[index]], block, NN)
        total = part if total is None else total + part
    back_ref[...] = total
    field = tw_ref[...].astype(F32)
    scale = lax.rsqrt(mean_of(field * field, width) + EPS)
    gain_term = jnp.sum(total * (field * scale), axis=0, keepdims=True)
    for p in range(wide):
        gain_wide[w_order[p]] = gain_term[:, p * r_w : (p + 1) * r_w]
    gain_term = side([gain_wide[w][:, :d_w] for w in range(wide)])
    for n in range(narrow):
        gain_blocks[n] = zeros_beside(gain_term[:, n * d_n : (n + 1) * d_n], count, False)
    first = lax.broadcasted_iota(jnp.int32, (8, 1), 0) == 0
    lane = lax.broadcasted_iota(jnp.int32, (8, r_w), 1)
    chosen = jnp.where(first & (lane == d_w), 1.0, 0.0)
    a_wide = a_ref[...]
    for index in range(narrow):
        column = dot(jnp.broadcast_to(gain_blocks[n_order[index]], (8, count)), chosen, TN)
        term = dot(g_blocks[n_order[index]], a_wide, TN)
        for p in range(wide):
            block = (term[:, p * r_w : (p + 1) * r_w] + column).astype(BF)
            if index < pair:
                own_terms[index, p] = block
                continue
            start = 0
            for ref in other_terms:
                ref[index % pair, p] = block[start : start + ref.shape[2]]
                start += ref.shape[2]


def outputs_kernel(
    sizes, batches, slots, w_order, n_order, lengths, hr_ref, mix_ref, gh_ref, tw_ref, back_ref, own_ref, other_ref,
    mixed_ref, grad_ref, n_blocks, d_blocks, gain_blocks, gain_wide,
):
    wide, d_w, r_w, d_n, kv_n, pair, d_pad = sizes
    narrow = 2 * pair
    width = wide * d_w
    rows = hr_ref.shape[0] // batches

    def natural(field):
        for index in range(narrow):
            n_blocks[n_order[index]] = field[:, index * d_pad : (index + 1) * d_pad]
        return side([n_blocks[n][:, d_pad - d_n :] for n in range(narrow)])

    inside = jnp.concatenate([places(lengths, b, slots, (rows, 1), 0)[2] for b in range(batches)], axis=0)
    mixed = natural(jnp.where(inside, hr_ref[...] + mix_ref[...], 0.0))
    for b in range(batches):
        mixed_ref[b] = mixed[b * rows : (b + 1) * rows].T.astype(BF)
    gain = gain_rows(sizes, own_ref, other_ref, n_order, gain_blocks)
    for w in range(wide):
        gain_wide[w] = zeros_beside(gain[:, w * d_w : (w + 1) * d_w], r_w, False)
    gain = side([gain_wide[w_order[p]] for p in range(wide)])
    field = tw_ref[...].astype(F32)
    scale = lax.rsqrt(mean_of(field * field, width) + EPS)
    normed = field * scale
    normed_grad = back_ref[...] * gain
    grad = scale * (normed_grad - normed * mean_of(normed_grad * normed, width))
    for p in range(wide):
        d_blocks[w_order[p]] = grad[:, p * r_w : (p + 1) * r_w]
    grad = side([d_blocks[w][:, :d_w] for w in range(wide)])
    grad = natural(gh_ref[...]) + grad
    for b in range(batches):
        grad_ref[b] = grad[b * rows : (b + 1) * rows].T.astype(BF)


def results_kernel(sizes, *refs):
    wide, d_w, r_w, d_n, kv_n, pair, d_pad = sizes
    *a_refs, moved_ref, kept_ref, first_ref = refs[: len(refs) - 9]
    query, key, value, output, gate, up, down, first_gain, second_gain = refs[len(refs) - 9 :]
    total = a_refs[0][...].astype(F32)
    for ref in a_refs[1:]:
        total = total + ref[...].astype(F32)
    turned = total[:d_n].T
    query[...] = turned[:d_w]
    first_gain[...] = turned[d_w : d_w + 1]
    key[...] = total[d_n : d_n + kv_n, :d_w]
    value[...] = total[d_n + kv_n : d_n + 2 * kv_n, :d_w]
    rest = moved_ref[...].astype(F32) + kept_ref[...].astype(F32)
    units = (rest.shape[0] - r_w) // 3
    first_units = first_ref.shape[1]
    for kind, ref in enumerate((gate, up, down)):
        ref[:first_units] = first_ref[kind, :, d_pad - d_n :]
        ref[first_units:] = rest[kind * units : (kind + 1) * units, d_pad - d_n :]
    block = rest[3 * units :]
    output[...] = block[:d_w, d_pad - d_n :]
    second_gain[...] = block[d_w : d_w + 1, d_pad - d_n :]


VMEM = pl.BlockSpec(memory_space=pltpu.VMEM)
SMEM = pl.BlockSpec(memory_space=pltpu.SMEM)


def shaped(shape, dtype):
    return jax.ShapeDtypeStruct(shape, dtype)


def scratch(*shape, dtype=F32):
    return pltpu.VMEM(shape, dtype)


def call(name, kernel, operands, out_shapes, scratches, multiply_adds, megabytes, orders=(), transcendentals=0, aliases=None, anywhere=0):
    out_specs = [VMEM] * (len(out_shapes) - anywhere) + [pl.BlockSpec(memory_space=pl.ANY)] * anywhere
    return pl.pallas_call(
        kernel,
        in_specs=[SMEM] * len(orders) + [VMEM] * len(operands),
        out_specs=out_specs,
        out_shape=out_shapes,
        scratch_shapes=scratches,
        input_output_aliases=aliases or {},
        compiler_params=pltpu.CompilerParams(vmem_limit_bytes=megabytes * 1024 * 1024),
        cost_estimate=pl.CostEstimate(
            flops=2 * multiply_adds,
            bytes_accessed=sum(a.size * a.dtype.itemsize for a in list(operands) + list(out_shapes)),
            transcendentals=transcendentals,
        ),
        name=name,
    )(*orders, *operands)


FEED_MEGABYTES = (18, 22)


def feed_kernel(chained, rows_ref, grads_ref, own_ref, other_ref, *refs):
    before = refs[:2] if chained else ()
    mix_ref, back_ref, own_out, *other_out = refs[len(before) : -3 - 2 * chained]
    hidden, gate_part, up_part = refs[-3:] if not chained else refs[-5:-2]
    if chained:
        far_out, other_out = other_out[0], [refs[-2]]
    pair, wide = own_out.shape[:2]
    units, lanes = own_ref.shape[-2:]
    narrow = 2 * pair
    total = wide * units

    def weight(kind, lo=0, count=total):
        blocks = [
            (own_ref, other_ref)[index // pair][index % pair, :, kind].reshape(total, lanes)
            for index in range(narrow)
        ]
        return side([block[lo : lo + count] for block in blocks])

    rows_in = rows_ref[...]
    grad_in = grads_ref[...]
    step = 256
    for lo in range(0, total, step):
        gate_value = dot(rows_in, weight(0, lo, step), NT)
        up_value = dot(rows_in, weight(1, lo, step), NT)
        hidden_grad = dot(grad_in, weight(2, lo, step), NT)
        sigmoid_gate = 1.0 / (1.0 + jnp.exp(-gate_value))
        silu = gate_value * sigmoid_gate
        hidden[:, lo : lo + step] = (silu * up_value).astype(BF)
        gate_part[:, lo : lo + step] = (
            hidden_grad * up_value * (sigmoid_gate * (1.0 + gate_value * (1.0 - sigmoid_gate)))
        ).astype(BF)
        up_part[:, lo : lo + step] = (hidden_grad * silu).astype(BF)
    part = max(wide // 4, 1)
    for kind, (left, right) in enumerate(((gate_part, rows_in), (up_part, rows_in), (hidden, grad_in))):
        for first in range(0, wide, part):
            term = dot(left[:, first * units : (first + part) * units], right, TN).astype(BF)
            for index in range(narrow):
                ref = own_out if index < pair else other_out[kind % len(other_out)]
                block = term[:, index * lanes : (index + 1) * lanes].reshape(part, units, lanes)
                to = slice(first, first + part)
                if len(ref.shape) == 5:
                    ref[index % pair, to, kind] = block
                elif ref.shape[2] == units:
                    ref[index % pair, to] = block
                else:
                    ref[index % pair, to, kind * units : (kind + 1) * units] = block
    if chained:
        leaving = pltpu.make_async_copy(other_out[0], far_out, refs[-1])
        leaving.start()
    mix = dot(hidden[...], weight(2), NN)
    mix_ref[...] = before[0][...] + mix if chained else mix
    back = dot(gate_part[...], weight(0), NN) + dot(up_part[...], weight(1), NN)
    back_ref[...] = before[1][...] + back if chained else back
    if chained:
        leaving.wait()


def feed_call(rows_in, grad_in, own, other, before=(), flat=False):
    pair, wide, _, units, lanes = own.shape
    rows, width = rows_in.shape
    total = wide * units
    own_shape = (3 * units, lanes) if flat else (3, units, lanes)
    other_shapes = [own_shape] if flat else [(units, lanes)] * 3
    return call(
        "feed_forward",
        functools.partial(feed_kernel, bool(before)),
        (rows_in, grad_in, own, other, *before),
        [shaped((rows, width), F32)] * 2
        + [shaped((pair, wide, *shape), BF) for shape in [own_shape, *other_shapes]],
        [scratch(rows, total, dtype=BF)] * 3
        + ([scratch(pair, wide, *own_shape, dtype=BF), pltpu.SemaphoreType.DMA] if before else []),
        9 * rows * width * total,
        FEED_MEGABYTES[flat],
        transcendentals=rows * total,
        aliases={4: 0, 5: 1} if before else None,
        anywhere=1 if before else 0,
    )


AXES = ("wide", "narrow")


class Grid:
    def __init__(self):
        self.wide = lax.axis_size("wide")
        self.narrow = lax.axis_size("narrow")
        self.outer = 4
        self.inner = self.wide // 4
        self.pair = self.narrow // 2
        self.size = {"outer": 4, "inner": self.inner, "pair": self.pair, "core": 2}
        self.stride = {"outer": self.inner * self.narrow, "inner": self.narrow, "pair": 2, "core": 1}
        linear = lax.axis_index("wide") * self.narrow + lax.axis_index("narrow")
        self.at = {name: (linear // self.stride[name]) % self.size[name] for name in self.size}

    def shift(self, value, name, count=1):
        size, stride = self.size[name], self.stride[name]
        pairs = []
        for source in range(self.wide * self.narrow):
            digit = (source // stride) % size
            pairs.append((source, source + ((digit + count) % size - digit) * stride))
        return lax.ppermute(value, AXES, pairs)

    def behind(self, name, steps):
        return (self.at[name] + (self.size[name] - steps)) % self.size[name]


def after(value, others):
    if not others:
        return value
    return lax.optimization_barrier((value, *others))[0]


class Flow:
    def __init__(self, make, grid, *args):
        self.grid = grid
        self.gates = ()
        self.last = ()
        self.result = None
        self.more = ()
        self.run = make(self, *args)

    def step(self, *others):
        self.gates = others
        try:
            self.last = next(self.run)
        except StopIteration as stop:
            self.result = stop.value
            return self.result
        return None

    def finish(self):
        while self.result is None:
            self.step()
        return self.result

    def shift(self, value, name, count=1):
        return self.grid.shift(after(value, self.gates), name, count)

    def settle(self, value):
        return after(value, self.gates)


class Clock:
    def __init__(self):
        self.held = ()

    def now(self, value):
        return after(value, self.held)

    def phase(self, *starts, done=(), wait=(), leave=()):
        gates = self.held + tuple(done)
        for flow, steps in starts:
            for _ in range(steps):
                flow.step(*gates)
        flows = [flow for flow, _ in starts if flow not in leave] + list(wait)
        held = sum([tuple(flow.last) for flow in flows], tuple(done))
        if not starts:
            held = self.held + held
        self.held = held if held else self.held


def both_rings(flow, first, first_name, second, second_name):
    one, two = [first], [second]
    for at in range(max(flow.grid.size[first_name], flow.grid.size[second_name]) - 1):
        if at < flow.grid.size[first_name] - 1:
            one.append(flow.shift(one[-1], first_name))
        if at < flow.grid.size[second_name] - 1:
            two.append(flow.shift(two[-1], second_name))
        yield (one[-1], two[-1])
        if at < flow.grid.size[first_name] - 1:
            one[-1] = flow.settle(one[-1])
        if at < flow.grid.size[second_name] - 1:
            two[-1] = flow.settle(two[-1])
    return one, two


def gather_outer(flow, shard):
    moved = [flow.shift(shard, "outer", count) for count in range(1, flow.grid.outer)]
    yield tuple(moved)
    return [shard] + [flow.settle(block) for block in moved]


def gather_ring(flow, shard):
    blocks = [shard]
    for _ in range(flow.grid.outer - 1):
        blocks.append(flow.shift(blocks[-1], "outer"))
        yield (blocks[-1],)
        blocks[-1] = flow.settle(blocks[-1])
    return blocks


def gather_plane(flow, blocks, cut):
    stacked = lax.optimization_barrier(jnp.stack(blocks))
    first, second = stacked[..., :cut, :], stacked[..., cut:, :]
    one, two = yield from both_rings(flow, first, "inner", second, "pair")
    one, two = yield from both_rings(flow, jnp.concatenate(one), "pair", jnp.stack(two), "inner")
    own = jnp.concatenate([jnp.stack(one), jnp.concatenate(two, axis=1)], axis=-2)
    other = flow.shift(own, "core")
    yield (other,)
    return own, other


def both_sums(flow, first, first_name, second, second_name, sent=None):
    sizes = flow.grid.size
    one, two = first(1) if sent is None else sent, second(1)
    for step in range(1, max(sizes[first_name], sizes[second_name])):
        moved = []
        if step < sizes[first_name]:
            one = one if step == 1 and sent is not None else flow.shift(one, first_name)
            moved.append(one)
        if step < sizes[second_name]:
            two = flow.shift(two, second_name)
            moved.append(two)
        yield tuple(moved)
        if step < sizes[first_name]:
            one = flow.settle(one)
            one = one + first(step + 1) if step < sizes[first_name] - 1 else one
        if step < sizes[second_name]:
            two = flow.settle(two)
            two = two + second(step + 1) if step < sizes[second_name] - 1 else two
    return one, two


def scatter_plane(flow, own, other, cut):
    outer = flow.grid.outer
    if isinstance(other, tuple):
        moved = tuple(flow.shift(part, "core") for part in other)
        yield moved
        moved = [flow.settle(part) for part in moved]
        moved = jnp.stack(moved, axis=2) if own.ndim == 5 else jnp.concatenate(moved, axis=2)
    else:
        moved = flow.shift(other, "core")
        yield (moved,)
        moved = flow.settle(moved)
    more = sent = None

    def wide_part(r):
        return slice(r * outer, (r + 1) * outer)

    def first(r, part=slice(None)):
        return moved[r, part, ..., :cut, :] + own[r, part, ..., :cut, :]

    def second(r, at=slice(None)):
        part = wide_part(r)
        block = moved[at, part, ..., cut:, :] + own[at, part, ..., cut:, :]
        if more is None:
            return block
        return jnp.concatenate([block, more[at, part] + flow.more[0][at, part]], axis=-2)

    if flow.more:
        sent = flow.shift(first(1), "pair")
        more = flow.shift(flow.more[1], "core")
        yield (more,)
        more = flow.settle(more)
    one, two = yield from both_sums(flow, first, "pair", second, "inner", sent)

    def first_next(r):
        return one[wide_part(r)] + first(0, wide_part(r))

    def second_next(r):
        return two[r] + second(0, r)

    last = yield from both_sums(flow, first_next, "inner", second_next, "pair")
    return jnp.concatenate([last[0] + first_next(0), last[1] + second_next(0)], axis=-2)


def scatter_outer(flow, sums):
    outer = flow.grid.outer
    moved = [flow.shift(sums[r], "outer", outer - r) for r in range(1, outer)]
    yield tuple(moved)
    return [flow.settle(block) for block in moved] + [sums[0]]


def scatter_split(flow, sums):
    outer = flow.grid.outer
    moved = [flow.shift(sums[r], "outer", outer - r) for r in range(2, outer)]
    yield tuple(moved)
    moved = [flow.settle(block) for block in moved]
    moved.append(flow.shift(sums[1], "outer", outer - 1))
    yield tuple(moved[-1:])
    return sum([flow.settle(block).astype(F32) for block in moved], sums[0].astype(F32))


def scatter_ring(flow, sums):
    outer = flow.grid.outer
    total = sums[1]
    for step in range(1, outer):
        total = flow.shift(total, "outer")
        yield (total,)
        total = flow.settle(total)
        if step < outer - 1:
            total = (total.astype(F32) + sums[step + 1].astype(F32)).astype(BF)
    return [total, sums[0]]


def rounded_up(count, step):
    return -(-count // step) * step
GRANTS = {
    "prepare_narrow": 16,
    "prepare_wide": 12,
    "project": 24,
    "attend": 12,
    "residual": 20,
    "middle": 24,
    "attend_back": 20,
    "weights": 28,
    "outputs": 28,
    "results": 10,
}


def body(
    tokens,
    lengths,
    cotangent,
    query_weight,
    key_matrix,
    value_matrix,
    output_weight,
    gate_weight,
    up_weight,
    down_weight,
    attention_gain,
    feedforward_gain,
):
    grid = Grid()
    batches, bucket_rows, width = tokens.shape
    rows = batches * bucket_rows
    wide, narrow, pair, inner, outer = grid.wide, grid.narrow, grid.pair, grid.inner, grid.outer
    d_w, d_n = query_weight.shape
    kv_n = key_matrix.shape[1]
    f_w = down_weight.shape[0]
    d_pad = rounded_up(d_n, 128)
    r_w = rounded_up(d_w + 1, 64)
    taken = d_n + 2 * kv_n
    t_rows = rounded_up(taken, 16)
    sizes = (wide, d_w, r_w, d_n, kv_n, pair, d_pad)

    packed = jnp.concatenate([query_weight.T, key_matrix.T, value_matrix.T], axis=0)
    gain_column = jnp.concatenate([attention_gain, jnp.zeros((2 * kv_n,), BF)])[:, None]
    packed = jnp.concatenate([packed, gain_column, jnp.zeros((taken, r_w - d_w - 1), BF)], axis=1)
    a_shard = jnp.pad(packed, ((0, t_rows - taken), (0, 0)))
    a_cut = rounded_up(t_rows // 2, 16)
    o_shard = jnp.concatenate([output_weight, feedforward_gain[None], jnp.zeros((r_w - d_w - 1, d_n), BF)])
    f_shard = jnp.stack([gate_weight.T, up_weight.T, down_weight])
    sub = 256 // wide
    tiles_in = f_w // sub
    bounds = [0, 4 * tiles_in // 10 * sub, f_w]
    shards = [f_shard[:, lo:hi] for lo, hi in zip(bounds, bounds[1:])]
    shards[0] = jnp.concatenate([shards[0], o_shard[None]])
    shards = [jnp.pad(shard, ((0, 0), (0, 0), (d_pad - d_n, 0))) for shard in shards]
    cuts = [shard.shape[1] // 2 for shard in shards]

    place = jnp.arange(wide, dtype=jnp.int32)
    w_order = (grid.at["outer"] - place % outer) % outer * inner
    w_order = (w_order + (grid.at["inner"] - place // outer) % inner).astype(jnp.int32)
    place = jnp.arange(narrow, dtype=jnp.int32)
    n_order = (grid.at["pair"] - place % pair) % pair * 2
    n_order = (n_order + (grid.at["core"] - place // pair) % 2).astype(jnp.int32)
    slots = lengths.shape[2]
    orders = (w_order, n_order, lengths.reshape(-1))
    freqs = THETA ** (-jnp.arange(HEAD_WIDTH // 2, dtype=F32) * 2.0 / HEAD_WIDTH)
    freqs = jnp.concatenate([freqs] * 4)[None]

    flow_za = Flow(gather_outer, grid, a_shard)
    flow_z1 = Flow(gather_ring, grid, shards[0])
    flow_z2 = Flow(gather_ring, grid, shards[1])
    plane = max(inner, pair) - 1
    clock = Clock()
    clock.phase((flow_za, 1), (flow_z1, 1), leave=(flow_za, flow_z1))
    token_rows = tokens.reshape(rows, width)
    cotangent_rows = cotangent.reshape(rows, width)
    token_narrow, branch_grad = call(
        "prepare_narrow",
        functools.partial(prepare_narrow_kernel, sizes, batches, slots),
        (token_rows, cotangent_rows),
        [shaped((rows, narrow * d_pad), BF)] * 2,
        [scratch(narrow, rows, d_pad, dtype=BF)] * 2,
        0,
        GRANTS["prepare_narrow"],
        orders=orders,
    )
    clock.phase(done=(token_narrow,), wait=(flow_za, flow_z1))
    flow_a = Flow(gather_plane, grid, flow_za.finish(), a_cut)
    clock.phase((flow_a, plane), (flow_z1, 1), leave=(flow_a, flow_z1))
    token_wide, cosine, sine = call(
        "prepare_wide",
        functools.partial(prepare_wide_kernel, sizes, batches, slots),
        (clock.now(token_rows), freqs),
        [shaped((rows, wide * r_w), BF), shaped((rows, 128), F32), shaped((rows, 128), F32)],
        [scratch(wide, rows, r_w, dtype=BF)],
        0,
        GRANTS["prepare_wide"],
        orders=orders,
    )
    clock.phase(done=(token_wide,), wait=(flow_a, flow_z1))
    clock.phase((flow_a, plane), (flow_z1, 1))
    flow_1 = Flow(gather_plane, grid, flow_z1.finish(), cuts[0])
    clock.phase((flow_a, 1), (flow_1, plane), (flow_z2, 1), leave=(flow_1, flow_z2))
    a_own, a_other = flow_a.finish()
    a_in, query, key, value = call(
        "project",
        functools.partial(project_kernel, sizes),
        (clock.now(token_wide), cosine, sine, a_own, a_other),
        [
            shaped((rows, wide * r_w), BF),
            shaped((rows, QUERY_HEADS * HEAD_WIDTH), BF),
            shaped((rows, KEY_VALUE_HEADS * HEAD_WIDTH), BF),
            shaped((rows, KEY_VALUE_HEADS * HEAD_WIDTH), BF),
        ],
        [scratch(narrow, rows, t_rows), scratch(narrow, 1, t_rows), scratch(wide, 1, r_w)],
        rows * wide * r_w * narrow * t_rows,
        GRANTS["project"],
        orders=orders,
    )

    clock.phase(done=(query,), wait=(flow_1, flow_z2))
    clock.phase((flow_1, plane), (flow_z2, 1), leave=(flow_1, flow_z2))

    def by_bucket(field):
        return field.reshape(batches, bucket_rows, field.shape[-1])

    group = QUERY_HEADS // KEY_VALUE_HEADS
    steps = bucket_rows // 128
    p_shape = (KEY_VALUE_HEADS, group * 128, 128 * steps * (steps + 1) // 2)
    query, key, value = by_bucket(query), by_bucket(key), by_bucket(value)
    pair_work = QUERY_HEADS * bucket_rows * bucket_rows * HEAD_WIDTH
    attended, probs = [], []
    for b in range(batches):
        parts = call(
            "attend",
            functools.partial(attend_kernel, slots, b),
            (clock.now(query), key, value),
            [shaped(query.shape[1:], BF), shaped(p_shape, BF)],
            [],
            6 * pair_work,
            GRANTS["attend"],
            orders=orders,
            transcendentals=QUERY_HEADS * bucket_rows * bucket_rows,
        )
        attended.append(parts[0])
        probs.append(parts[1])
        if b < batches - 1:
            clock.phase(done=(parts[0],), wait=(flow_z2,))
            clock.phase((flow_z2, 1), leave=(flow_z2,))
    clock.phase(done=tuple(attended), wait=(flow_1, flow_z2))
    flow_2 = Flow(gather_plane, grid, flow_z2.finish(), cuts[1])
    clock.phase((flow_1, 1), (flow_2, plane), leave=(flow_2,))
    first_own, first_other = flow_1.finish()
    o_operands = (first_own[:, :, 3], first_other[:, :, 3])
    d_lanes = narrow * d_pad
    attended_wide, residual, feed_in = call(
        "residual",
        functools.partial(residual_kernel, sizes, batches),
        (clock.now(token_narrow), *o_operands, *attended),
        [
            shaped((rows, wide * r_w), BF),
            shaped((rows, d_lanes), F32),
            shaped((rows, d_lanes), BF),
        ],
        [scratch(wide, rows, r_w, dtype=BF)],
        rows * wide * r_w * d_lanes,
        GRANTS["residual"],
        orders=orders,
    )

    clock.phase(done=(feed_in,), wait=(flow_2,))
    clock.phase((flow_2, plane), leave=(flow_2,))
    *sums_so_far, own_terms, gate_terms, up_terms, down_terms = feed_call(
        clock.now(feed_in), branch_grad, first_own, first_other
    )
    back_1 = Flow(scatter_plane, grid, own_terms, (gate_terms, up_terms, down_terms), cuts[0])
    clock.phase(done=(own_terms,))
    clock.phase((back_1, 1), wait=(flow_2,))
    clock.phase((flow_2, 1), (back_1, plane), leave=(back_1,))
    *sums_so_far, own_terms, other_terms = feed_call(
        clock.now(feed_in), branch_grad, *flow_2.finish(), tuple(sums_so_far), True
    )
    back_2 = Flow(
        scatter_plane,
        grid,
        own_terms,
        other_terms,
        rounded_up((own_terms.shape[2] + r_w) // 2, 16) + 16,
    )
    clock.phase(done=(own_terms,), wait=(back_1,))
    clock.phase((back_1, plane), (back_2, 1), leave=(back_1, back_2))
    mix, back = sums_so_far
    grad, attended_grad, own_o, other_o = call(
        "middle",
        functools.partial(middle_kernel, sizes),
        (clock.now(residual), back, branch_grad, attended_wide) + o_operands,
        [
            shaped((rows, d_lanes), F32),
            shaped((rows, width), BF),
            shaped((pair, wide, r_w, d_pad), BF),
            shaped((pair, wide, r_w, d_pad), BF),
        ],
        [scratch(wide, rows, r_w)],
        2 * rows * wide * r_w * d_lanes,
        GRANTS["middle"],
        orders=orders,
    )
    clock.phase(done=(attended_grad,), wait=(back_1, back_2))
    back_2.more = (own_o, other_o)
    clock.phase((back_2, 1))
    back_z1 = Flow(scatter_split, grid, back_1.finish())
    clock.phase((back_2, plane), (back_z1, 1), leave=(back_2, back_z1))
    by_parts = (by_bucket(attended_grad), by_bucket(cosine), by_bucket(sine))
    shapes = [x.shape[1:] for x in (query, key, value)]
    grads = []
    for b in range(batches):
        grads.append(
            call(
                "attend_back",
                functools.partial(attend_back_kernel, b),
                (clock.now(query), key, value, attended[b], by_parts[0], probs[b], *by_parts[1:]),
                [shaped(shape, BF) for shape in shapes],
                [scratch(*shape) for shape in shapes],
                12 * pair_work,
                GRANTS["attend_back"],
                orders=orders,
            )
        )
        if b < batches - 1:
            clock.phase(done=tuple(grads[b][:1]), wait=(back_z1,))
            clock.phase((back_z1, 1), leave=(back_z1,))
    clock.phase(done=tuple(x[0] for x in grads), wait=(back_2, back_z1))
    clock.phase((back_2, plane), leave=(back_2,))
    operands = tuple(x for parts in zip(*grads) for x in parts)
    cuts_a = [0, rounded_up(t_rows // 3, 16), rounded_up(2 * t_rows // 3, 16), t_rows]
    wide_back, own_terms, *other_terms = call(
        "weights",
        functools.partial(weights_kernel, sizes, batches),
        (clock.now(token_wide), a_in, a_own, a_other) + operands,
        [shaped((rows, wide * r_w), F32), shaped(a_own.shape, BF)]
        + [shaped((pair, wide, hi - lo, r_w), BF) for lo, hi in zip(cuts_a, cuts_a[1:])],
        [scratch(narrow, rows, t_rows, dtype=BF), scratch(narrow, 1, t_rows), scratch(wide, 1, r_w)],
        2 * rows * wide * r_w * narrow * t_rows,
        GRANTS["weights"],
        orders=orders,
    )
    back_a = Flow(scatter_plane, grid, own_terms, tuple(other_terms), a_cut)
    clock.phase(done=(own_terms,))
    clock.phase((back_a, 1), wait=(back_2,))
    back_z2 = Flow(scatter_ring, grid, back_2.finish())
    clock.phase((back_a, plane), (back_z2, 1), leave=(back_a, back_z2))
    mixed, tokens_grad = call(
        "outputs",
        functools.partial(outputs_kernel, sizes, batches, slots),
        (clock.now(residual), mix, grad, token_wide, wide_back, a_own, a_other),
        [shaped((batches, width, bucket_rows), BF)] * 2,
        [
            scratch(narrow, rows, d_pad),
            scratch(wide, rows, r_w),
            scratch(narrow, 1, t_rows),
            scratch(wide, 1, r_w),
        ],
        0,
        GRANTS["outputs"],
        orders=orders,
    )
    clock.phase(done=(mixed,), wait=(back_z2,))
    clock.phase((back_z2, 1), wait=(back_a,), leave=(back_z2,))
    clock.phase((back_a, plane), wait=(back_z2,))
    back_za = Flow(scatter_outer, grid, back_a.finish())
    clock.phase((back_z2, 1), (back_za, 1), leave=(back_z2, back_za))
    outputs = call(
        "results",
        functools.partial(results_kernel, sizes),
        (*back_za.finish(), *back_z2.finish(), back_z1.finish()),
        [
            shaped(shape, F32)
            for shape in [(d_w, d_n), (kv_n, d_w), (kv_n, d_w), (d_w, d_n), *[(f_w, d_n)] * 3, (1, d_n), (1, d_n)]
        ],
        [],
        0,
        GRANTS["results"],
    )
    query_grad, key_grad, value_grad, output_grad, gate_grad, up_grad, down_grad, *gain_grads = outputs
    return (
        jnp.swapaxes(mixed, 1, 2),
        jnp.swapaxes(tokens_grad, 1, 2),
        query_grad,
        key_grad.T,
        value_grad.T,
        output_grad,
        gate_grad.T,
        up_grad.T,
        down_grad,
        gain_grads[0][0],
        gain_grads[1][0],
    )


def solution(mesh):
    in_specs = (
        P(None, ("wide", "narrow"), None),
        P(None, ("wide", "narrow"), None),
        P(None, ("wide", "narrow"), None),
        P("wide", "narrow"),
        P("wide", "narrow"),
        P("wide", "narrow"),
        P("wide", "narrow"),
        P("narrow", "wide"),
        P("narrow", "wide"),
        P("wide", "narrow"),
        P("narrow"),
        P("narrow"),
    )
    out_specs = (
        P(None, ("wide", "narrow"), None),
        P(None, ("wide", "narrow"), None),
        P("wide", "narrow"),
        P("wide", "narrow"),
        P("wide", "narrow"),
        P("wide", "narrow"),
        P("narrow", "wide"),
        P("narrow", "wide"),
        P("wide", "narrow"),
        P("narrow"),
        P("narrow"),
    )
    return jax.shard_map(body, mesh=mesh, in_specs=in_specs, out_specs=out_specs, check_vma=False)
```
